128 devices in a mesh: gx: 4 (over y), gy: 4 (over z), gz: 8 (over x, core).
Axes of the slice: x: 4, y: 4, z: 4, core: 2. Of those that a mesh axis runs over, the one named last changes fastest.
Arguments:
- emission: bfloat16 [3, 256, 1024, 512], P(None, 'gz', 'gx', 'gy'), may hold values from 0 to 2
- absorption: bfloat16 [256, 1024, 512], P('gz', 'gx', 'gy'), may hold values from 0.19921875 to 5
- target_z: bfloat16 [3, 1024, 1024], replicated, may hold values from 0 to 2
- target_x: bfloat16 [3, 256, 1024], replicated, may hold values from 0 to 2
- owner_z: int32 [4, 4, 256, 1], replicated, may hold values from 0 to 31; in each aligned block of 256 rows (0 to 255, 256 to 511, ..., all dimensions but the last counted through in order) at most 16 rows name the same one
- owner_x: int32 [4, 8, 32, 1], replicated, may hold values from 0 to 15; in each aligned block of 32 rows (0 to 31, 32 to 63, ..., all dimensions but the last counted through in order) at most 4 rows name the same one
Outputs:
- grad_emission: bfloat16 [3, 256, 1024, 512], P(None, 'gz', 'gx', 'gy')
- grad_absorption: bfloat16 [256, 1024, 512], P('gz', 'gx', 'gy')
- owned_error: float32 [4, 4, 8], P('gx', 'gy', 'gz')
The draws below stay inside these ranges and needn't reach their ends.
Inputs may be any that keep to these rules, and one draw needn't show every extreme that they name: Within each block owner_z[a, b, :, 0] of 256 tiles no value appears more than 16 times. Within each block owner_x[b, c, :, 0] of 32 tiles no value appears more than 4 times.
All inputs are finite; a program needn't handle non-finite values.
Results may differ from the reference program's by a relative error of at most 0.001.
Values sent between devices are 32-bit elements; how exact they have to be, the bound alone decides.
A program may use at most 256 MiB of HBM per device.

```python
import math
import jax
import jax.numpy as jnp
import numpy as np
from jax import lax

BX = 256
BZ = 32
BY = 128
GX_COUNT = 4
GY_COUNT = 4
GZ_COUNT = 8
NX = 1024
NY = 512
NZ = 256
PY = 256
IMY = 1024
GROUP_Z = 32
GROUP_X = 16
SLOT_Z = 16
SLOT_X = 4


def shard_levels(stream_key, extent, shards, least, high):
    def one(dim, blocks):
        steps = jax.random.uniform(jax.random.fold_in(jax.random.fold_in(stream_key, 6), dim), (blocks,), jnp.float32, least / len(shards), high / len(shards))
        return jnp.repeat(jnp.exp(steps), extent[dim] // blocks).reshape((-1,) + (1,) * (len(extent) - dim - 1))

    gain = one(*shards[0])
    for cut in shards[1:]:
        gain = gain * one(*cut)
    return gain


def deal_out(rng, own, number, rows, number_of, top, reach, slope):
    order = jax.random.permutation(rng, number_of)
    crowded, ordinary = portions_of(number_of, rows * top, reach, slope, True), portions_of(number_of, rows * top, reach, slope, False)
    places = jnp.arange(number_of)

    def named(sizes, offset_by):
        used = int((sizes > 0).sum())
        fixed = max(1, used // 4)
        shifted = fixed + (places - fixed + offset_by * (used - fixed)) % max(1, number_of - fixed)
        return jnp.zeros((number_of,), jnp.int32).at[order[jnp.where(places < fixed, places, shifted)]].set(jnp.asarray(sizes, jnp.int32))

    sizes = jnp.where(number % 4 == 0, named(crowded, number // 4), named(ordinary, number - number // 4 - 1))
    mixed = jax.random.permutation(jax.random.fold_in(own, 3), number_of)
    donor, taker = mixed[0:number_of // 2 * 2:2], mixed[1:number_of // 2 * 2:2]
    room = jnp.minimum(sizes[donor] - 1, reach - sizes[taker]) // 2
    room = jnp.where((donor == order[0]) | (taker == order[0]) | (sizes[taker] == 0), 0, jnp.maximum(room, 0))
    shifted = jax.random.randint(jax.random.fold_in(own, 4), (number_of // 2,), 0, 1 << 20) % (room + 1)
    sizes = sizes.at[donor].add(-shifted).at[taker].add(shifted)
    items = jnp.searchsorted(jnp.cumsum(sizes), jnp.arange(rows * top), side="right").astype(jnp.int32)
    listing = items.reshape(top, rows).T
    listing = listing[jax.random.permutation(jax.random.fold_in(own, 1), rows)]
    offset_by = jax.random.randint(jax.random.fold_in(own, 2), (rows, 1), 0, top)
    return jnp.take_along_axis(listing, (jnp.arange(top)[None, :] + offset_by) % top, axis=1)


def portions_of(amount, total, limit, skew, full):
    portions = [(1 << 20) // math.isqrt(rank ** skew) + 1 for rank in range(1, amount + 1)]
    largest = limit if full else min(limit, max(-(-total // amount), total * portions[0] // sum(portions)))
    least = 1 if total - largest >= amount - 1 else 0
    counts, spare = [largest] + [least] * (amount - 1), total - largest - least * (amount - 1)
    while spare > 0:
        movable = [i for i in range(1, amount) if counts[i] < largest] or [i for i in range(1, amount) if counts[i] < limit]
        mass, left = sum([portions[i] for i in movable]), spare
        for i in movable:
            extra = min(limit - counts[i], max(1, left * portions[i] // mass), spare)
            counts[i] = counts[i] + extra
            spare = spare - extra
    return np.array(counts)


def setup_inputs(seed: int = 0) -> dict:
    streams_of = jax.random.split(jax.random.key(seed), 7)
    emission = jnp.clip(2.0 * jax.random.uniform(streams_of[0], (3, NZ, NX, NY), jnp.float32) ** shard_levels(streams_of[0], (3, NZ, NX, NY), ((1, 8), (2, 4), (3, 4)), -0.2, 0.2), 0.0, 2.0).astype(jnp.bfloat16)
    absorption = jnp.clip(jnp.exp(math.log(5.0) - 3.2227897 * jax.random.uniform(streams_of[1], (NZ, NX, NY), jnp.float32) ** shard_levels(streams_of[1], (NZ, NX, NY), ((0, 8), (1, 4), (2, 4)), -0.2, 0.2)), 0.19921875, 5.0).astype(jnp.bfloat16)
    target_z = jnp.clip(jax.random.uniform(streams_of[2], (3, NX, IMY), jnp.float32, 0.0, 2.0), 0.0, 2.0).astype(jnp.bfloat16)
    target_x = jnp.clip(jax.random.uniform(streams_of[3], (3, NZ, IMY), jnp.float32, 0.0, 2.0), 0.0, 2.0).astype(jnp.bfloat16)
    owner_z_keys = jax.random.split(jax.random.fold_in(streams_of[4], 1), GX_COUNT * GY_COUNT * BX // BX)
    owner_z_turns = jax.random.permutation(jax.random.fold_in(streams_of[4], 3), GX_COUNT * GY_COUNT * BX // BX)
    owner_z = jax.vmap(lambda own, number: deal_out(jax.random.fold_in(streams_of[4], 2), own, number, BX, GROUP_Z, 1, SLOT_Z, 2))(owner_z_keys, owner_z_turns).reshape((GX_COUNT, GY_COUNT, BX, 1))
    owner_x_keys = jax.random.split(jax.random.fold_in(streams_of[5], 1), GY_COUNT * GZ_COUNT * BZ // BZ)
    owner_x_turns = jax.random.permutation(jax.random.fold_in(streams_of[5], 3), GY_COUNT * GZ_COUNT * BZ // BZ)
    owner_x = jax.vmap(lambda own, number: deal_out(jax.random.fold_in(streams_of[5], 2), own, number, BZ, GROUP_X, 1, SLOT_X, 2))(owner_x_keys, owner_x_turns).reshape((GY_COUNT, GZ_COUNT, BZ, 1))
    return dict(emission=emission, absorption=absorption, target_z=target_z, target_x=target_x, owner_z=owner_z, owner_x=owner_x)


OPTICAL = 1.5
BACKLIGHT = 1.0
HIGHEST = lax.Precision.HIGHEST

def interp_table(width):
    pixels = jnp.arange(2 * width, dtype=jnp.int32)
    nearest = pixels // 2
    second = jnp.clip(nearest + 2 * (pixels % 2) - 1, 0, width - 1)
    columns = jnp.arange(width, dtype=jnp.int32)
    first_hit = (columns[None, :] == nearest[:, None]).astype(jnp.float32)
    second_hit = (columns[None, :] == second[:, None]).astype(jnp.float32)
    return 0.75 * first_hit + 0.25 * second_hit

def upsample(sample_values, blend_weight):
    width = blend_weight.shape[1]
    leading = sample_values.shape[:-1]
    bricks = sample_values.shape[-1] // width
    result = jnp.dot(sample_values.reshape(-1, width), blend_weight.T.astype(sample_values.dtype), preferred_element_type=jnp.float32)
    return result.reshape(leading + (bricks * blend_weight.shape[0],))

def reduce_resolution(sample_values, blend_weight):
    span = blend_weight.shape[0]
    leading = sample_values.shape[:-1]
    bricks = sample_values.shape[-1] // span
    result = jnp.dot(sample_values.reshape(-1, span), blend_weight.astype(sample_values.dtype), precision=HIGHEST)
    return result.reshape(leading + (bricks * blend_weight.shape[1],))

def prefix_sum(sample_values, upper):
    length = sample_values.shape[0]
    indices = jnp.arange(length, dtype=jnp.int32)
    if upper:
        chosen = indices[None, :] > indices[:, None]
    else:
        chosen = indices[None, :] < indices[:, None]
    summing = chosen.astype(sample_values.dtype)
    result = jnp.dot(summing, sample_values.reshape(length, -1), precision=HIGHEST)
    return result.reshape(sample_values.shape)

def view_grad(emission_part, sigma_part, target_part, blend_weight, march_step):
    emis_up = upsample(emission_part, blend_weight)
    sigma_up = upsample(sigma_part, blend_weight)
    optical = march_step * sigma_up
    depth_sum = prefix_sum(optical, False)
    through = jnp.exp(-depth_sum)
    beyond = jnp.exp(-(depth_sum + optical))
    shares = through - beyond
    rendered = lax.optimization_barrier(jnp.sum(shares[None] * emis_up, axis=1)) + beyond[-1][None] * BACKLIGHT
    render_residual = rendered - target_part.astype(rendered.dtype)
    g_image = render_residual / march_step
    gradient_emission_fine = g_image[:, None] * shares[None]
    inner_sum = lax.optimization_barrier(jnp.sum(g_image[:, None] * emis_up, axis=0))
    behind = prefix_sum(shares * inner_sum, True)
    gradient_optical_depth = beyond * inner_sum - behind - (beyond[-1] * lax.optimization_barrier(jnp.sum(g_image, axis=0)) * BACKLIGHT)[None]
    return (reduce_resolution(gradient_emission_fine, blend_weight), reduce_resolution(march_step * gradient_optical_depth, blend_weight), render_residual)

def reference(emission, absorption, target_z, target_x, owner_z, owner_x):
    blend_weight = interp_table(BY)
    step_z = OPTICAL / NZ
    step_x = OPTICAL / NX
    stride = 16
    grad_e = jnp.zeros((3, NZ, NX, NY), jnp.float32)
    grad_s = jnp.zeros((NZ, NX, NY), jnp.float32)
    resid_z = jnp.zeros((3, NX, IMY), jnp.float32)
    resid_x = jnp.zeros((3, NZ, IMY), jnp.float32)

    def along_z(position, carried):
        grad_e, grad_s, resid_z = carried
        offset = (position * stride).astype(jnp.int32)
        emission_part = lax.dynamic_slice_in_dim(emission, offset, stride, 2)
        sigma_part = lax.dynamic_slice_in_dim(absorption, offset, stride, 1)
        target_part = lax.dynamic_slice_in_dim(target_z, offset, stride, 1)
        g_emis, g_sigma, render_residual = view_grad(emission_part, sigma_part, target_part, blend_weight, step_z)
        grad_e = lax.dynamic_update_slice_in_dim(grad_e, g_emis, offset, 2)
        grad_s = lax.dynamic_update_slice_in_dim(grad_s, g_sigma, offset, 1)
        resid_z = lax.dynamic_update_slice_in_dim(resid_z, render_residual, offset, 1)
        return (grad_e, grad_s, resid_z)
    grad_e, grad_s, resid_z = lax.fori_loop(0, NX // stride, along_z, (grad_e, grad_s, resid_z))

    def along_x(position, carried):
        grad_e, grad_s, resid_x = carried
        offset = (position * stride).astype(jnp.int32)
        emission_part = jnp.swapaxes(lax.dynamic_slice_in_dim(emission, offset, stride, 1), 1, 2)
        sigma_part = jnp.swapaxes(lax.dynamic_slice_in_dim(absorption, offset, stride, 0), 0, 1)
        target_part = lax.dynamic_slice_in_dim(target_x, offset, stride, 1)
        g_emis, g_sigma, render_residual = view_grad(emission_part, sigma_part, target_part, blend_weight, step_x)
        old_e = lax.dynamic_slice_in_dim(grad_e, offset, stride, 1)
        old_s = lax.dynamic_slice_in_dim(grad_s, offset, stride, 0)
        grad_e = lax.dynamic_update_slice_in_dim(grad_e, old_e + jnp.swapaxes(g_emis, 1, 2), offset, 1)
        grad_s = lax.dynamic_update_slice_in_dim(grad_s, old_s + jnp.swapaxes(g_sigma, 0, 1), offset, 0)
        resid_x = lax.dynamic_update_slice_in_dim(resid_x, render_residual, offset, 1)
        return (grad_e, grad_s, resid_x)
    grad_e, grad_s, resid_x = lax.fori_loop(0, NZ // stride, along_x, (grad_e, grad_s, resid_x))
    devices = GX_COUNT * GY_COUNT * GZ_COUNT
    tile_z = lax.optimization_barrier(jnp.sum((resid_z * resid_z).reshape(3, GX_COUNT, BX, GY_COUNT, PY), axis=(0, 4)))
    tile_z = jnp.transpose(tile_z, (0, 2, 1))
    slab_ids = jnp.arange(GX_COUNT, dtype=jnp.int32)[:, None, None]
    owner_id_z = slab_ids * GROUP_Z + owner_z[..., 0]
    tile_x = lax.optimization_barrier(jnp.sum((resid_x * resid_x).reshape(3, GZ_COUNT, BZ, GY_COUNT, PY), axis=(0, 4)))
    tile_x = jnp.transpose(tile_x, (2, 0, 1))
    depth_ids = jnp.arange(GZ_COUNT, dtype=jnp.int32)[None, :, None]
    owner_id_x = owner_x[..., 0] * GZ_COUNT + depth_ids
    owned = jax.ops.segment_sum(tile_z.reshape(-1), owner_id_z.reshape(-1).astype(jnp.int32), devices)
    owned = owned + jax.ops.segment_sum(tile_x.reshape(-1), owner_id_x.reshape(-1).astype(jnp.int32), devices)
    owned_error = (owned / (3.0 * PY * (SLOT_Z + SLOT_X))).reshape(GX_COUNT, GY_COUNT, GZ_COUNT)
    return (grad_e.astype(jnp.bfloat16), grad_s.astype(jnp.bfloat16), owned_error)
```

```python
import functools
import math

import jax
import jax.numpy as jnp
import numpy as np
from jax import lax
from jax.experimental import pallas as pl
from jax.experimental.pallas import tpu as pltpu
from jax.sharding import PartitionSpec as P

F32 = jnp.float32
BF16 = jnp.bfloat16
OPTICAL = 1.5
BACKLIGHT = 1.0

NSEG = 8
SEG = 32
HALF = 16
PITCH = 20
ZG = 4
NZ = 32
NZG = NZ // ZG
STEPS = 2 * NZG
XU = 4
LANE = 128


def interp_table(width):
    pixels = np.arange(2 * width)
    nearest = pixels // 2
    second = np.clip(nearest + 2 * (pixels % 2) - 1, 0, width - 1)
    columns = np.arange(width)
    return 0.75 * (columns[None, :] == nearest[:, None]) + 0.25 * (columns[None, :] == second[:, None])


def half(h):
    return slice(h * LANE, (h + 1) * LANE)


def upsample_store(fine, f, z, r):
    for s in range(NSEG):
        for h in range(2):
            fine[f, z, h, s * PITCH : s * PITCH + HALF] = r[s * HALF : (s + 1) * HALF, half(h)]


def upsample_part(ebuf, sbuf, tab, fine, h, z):
    rows = NSEG * HALF
    if h == 0:
        a = jnp.concatenate([ebuf[0, z].reshape(rows, LANE), ebuf[1, z].reshape(rows, LANE)], axis=0)
        r = jnp.dot(a, tab[0:LANE], preferred_element_type=F32)
        upsample_store(fine, 0, z, r[:rows])
        upsample_store(fine, 1, z, r[rows:])
    else:
        r = jnp.dot(ebuf[2, z].reshape(rows, LANE), tab[0:LANE], preferred_element_type=F32)
        upsample_store(fine, 2, z, r)
        s = sbuf[z].reshape(rows, LANE)
        r = jnp.dot(jnp.concatenate([s, s], axis=1), tab[LANE:], preferred_element_type=F32)
        upsample_store(fine, 3, z, r)


class Loader:
    def __init__(self, e_hbm, s_hbm, ebufs, sbufs, sems):
        self.refs = (e_hbm, s_hbm, ebufs, sbufs, sems)

    def copies(self, t, b):
        e_hbm, s_hbm, ebufs, sbufs, sems = self.refs
        k, zg = t // NZG, t % NZG
        zs, xs = pl.ds(zg * ZG, ZG), pl.ds(pl.multiple_of(k * HALF, HALF), HALF)
        return (
            pltpu.make_async_copy(e_hbm.at[:, zs, :, xs, :], ebufs[b], sems.at[b, 0]),
            pltpu.make_async_copy(s_hbm.at[zs, :, xs, :], sbufs[b], sems.at[b, 1]),
        )

    def start(self, t, b):
        for c in self.copies(t, b):
            c.start()

    def wait(self, t, b):
        for c in self.copies(t, b):
            c.wait()


def forward_scan(fine, zs, zc, xc, k, zg, extra):
    for h in range(2):
        hs = half(h)
        rows = [pl.ds(pl.multiple_of((zg * ZG + z) * NSEG, NSEG), NSEG) for z in range(ZG)]
        start = tuple(xc[i, h, rows[z], :] for z in range(ZG) for i in range(5))

        def step(j, carry):
            carry = list(carry)
            extra(h, j)
            for u in range(XU):
                xm = j * XU + u
                zr = k * HALF + xm
                s_z = zs[zr, :, hs]
                c0, c1, c2, t_z = [zc[zr, i, :, hs] for i in range(4)]
                for z in range(ZG):
                    e0, e1, e2, sg = [fine[f, z, h, pl.ds(xm, NSEG, stride=PITCH), :] for f in range(4)]
                    s_z = s_z + sg
                    t_new = jnp.exp2(s_z)
                    share = t_z - t_new
                    t_z = t_new
                    c0 = c0 + share * e0
                    c1 = c1 + share * e1
                    c2 = c2 + share * e2
                    s_x, t_x, d0, d1, d2 = carry[z * 5 : z * 5 + 5]
                    s_x = s_x + sg
                    t_new = jnp.exp2(s_x * 0.25)
                    share = t_x - t_new
                    carry[z * 5 : z * 5 + 5] = [s_x, t_new, d0 + share * e0, d1 + share * e1, d2 + share * e2]
                zs[zr, :, hs] = s_z
                for i, v in enumerate((c0, c1, c2, t_z)):
                    zc[zr, i, :, hs] = v
            return tuple(carry)

        carry = lax.fori_loop(0, HALF // XU, step, start)
        for z in range(ZG):
            for i in range(5):
                xc[i, h, rows[z], :] = carry[z * 5 + i]


def compose(front, back):
    c0, c1, c2, t = front
    d0, d1, d2, u = back
    return (c0 + t * d0, c1 + t * d1, c2 + t * d2, t * u)


def merge(bricks, target, inv_step):
    ahead = (jnp.zeros_like(target[0]),) * 3 + (jnp.ones_like(target[0]),)
    fronts = []
    for brick in bricks:
        fronts.append(ahead[3])
        ahead = compose(ahead, brick)
    resid = [ahead[c] + ahead[3] * BACKLIGHT - target[c] for c in range(3)]
    g = [r * inv_step for r in resid]
    behind = [jnp.full_like(target[0], BACKLIGHT)] * 3
    replies = []
    for front, brick in reversed(list(zip(fronts, bricks))):
        dot = g[0] * behind[0] + g[1] * behind[1] + g[2] * behind[2]
        replies.append([front * g[0], front * g[1], front * g[2], front * dot])
        behind = [brick[c] + brick[3] * behind[c] for c in range(3)]
    replies.reverse()
    return replies, resid[0] * resid[0] + resid[1] * resid[1] + resid[2] * resid[2]


def forward_kernel(
    inv_z, inv_x,
    e_hbm, s_hbm, tz_hbm, tx_hbm, tab,
    coz, cox, err,
    ebuf0, ebuf1, sbuf0, sbuf1, fine0, fine1, zs, zc, xc,
    tzb, txb, tzf, txf,
    sib, pc, got, rep, back, fin, finr,
    xloc, xgot, xrep, xback, xsuf,
    in_sem, t_sem, sem_sib, sem_chip, sem_rep, sem_fin, sem_x, sem_xr,
):
    ix, iy, iz = lax.axis_index("gx"), lax.axis_index("gy"), lax.axis_index("gz")
    chip, core = iz // 2, iz % 2
    load = Loader(e_hbm, s_hbm, (ebuf0, ebuf1), (sbuf0, sbuf1), in_sem)
    load.start(0, 0)
    load.start(1, 1)
    px = pl.ds(pl.multiple_of(iy * 256, 256), 256)
    tz_copy = pltpu.make_async_copy(tz_hbm.at[:, pl.ds(pl.multiple_of(ix * 256, 256), 256), px], tzb, t_sem.at[0])
    tx_copy = pltpu.make_async_copy(tx_hbm.at[:, pl.ds(pl.multiple_of(iz * NZ, NZ), NZ), px], txb, t_sem.at[1])
    tz_copy.start()
    tx_copy.start()

    sibling = {"gz": chip * 2 + 1 - core}
    chips = [{"gz": lax.rem(chip + d, 4) * 2 + core} for d in (1, 2, 3)]
    slabs = [{"gx": lax.rem(ix + d, 4)} for d in (1, 2, 3)]
    barrier = pltpu.get_barrier_semaphore()
    for peer in [sibling] + chips + slabs:
        pl.semaphore_signal(barrier, inc=1, device_id=peer, device_id_type=pl.DeviceIdType.MESH)

    def remote(src, dst, sems, peer):
        return pltpu.make_async_remote_copy(
            src_ref=src, dst_ref=dst, send_sem=sems.at[0], recv_sem=sems.at[1],
            device_id=peer, device_id_type=pl.DeviceIdType.MESH,
        )

    def sib_copy(k):
        return remote(zc.at[pl.ds(k * HALF + (1 - core) * 8, 8)], sib.at[k], sem_sib.at[k], sibling)

    def chip_copies(k):
        return [
            remote(pc.at[k, pl.ds(lax.rem(chip + d, 4) * 2, 2)], got.at[k, chip], sem_chip.at[k, d - 1], chips[d - 1])
            for d in (1, 2, 3)
        ]

    def rep_copies(k):
        return [
            remote(rep.at[k, lax.rem(chip + d, 4)], back.at[k, pl.ds(chip * 2, 2)], sem_rep.at[k, d - 1], chips[d - 1])
            for d in (1, 2, 3)
        ]

    def fin_copy(k):
        return remote(fin.at[k], finr.at[k], sem_fin.at[k], sibling)

    def x_copies():
        return [remote(xloc.at[lax.rem(ix + d, 4)], xgot.at[ix], sem_x.at[d - 1], slabs[d - 1]) for d in (1, 2, 3)]

    def xr_copies():
        return [remote(xrep.at[lax.rem(ix + d, 4)], xback.at[ix], sem_xr.at[d - 1], slabs[d - 1]) for d in (1, 2, 3)]

    def pair(k, m, hs):
        mine = [zc[k * HALF + core * 8 + m, i, :, hs] for i in range(4)]
        other = [sib[k, m, i, :, hs] for i in range(4)]
        first = core == 0
        return [jnp.where(first, a, b) for a, b in zip(mine, other)], [jnp.where(first, b, a) for a, b in zip(mine, other)]

    def z_compose(k):
        sib_copy(k).wait_recv()

        def body(m, _):
            for h in range(2):
                front, rear = pair(k, m, half(h))
                for i, v in enumerate(compose(front, rear)):
                    pc[k, m, i, :, half(h)] = v
            return 0

        lax.fori_loop(0, 8, body, 0)
        for c in chip_copies(k):
            c.start()

    def z_merge(k):
        for c in chip_copies(k):
            c.wait_recv()
        for i in range(2):
            m = chip * 2 + i
            got[k, chip, i] = pc[k, m]
            sq = jnp.zeros((8, LANE), F32)
            for h in range(2):
                bricks = [[got[k, o, i, f, :, half(h)] for f in range(4)] for o in range(4)]
                row = k * HALF + core * 8 + m
                target = [tzf[c, h, pl.ds(row, NSEG, stride=SEG + 4), :] for c in range(3)]
                replies, s = merge(bricks, target, inv_z)
                sq = sq + s
                for o in range(4):
                    for f in range(4):
                        rep[k, o, i, f, :, half(h)] = replies[o][f]
            err[k * 2 + i] = sq
        for c in rep_copies(k):
            c.start()
        back[k, pl.ds(chip * 2, 2)] = rep[k, chip]

    def z_split(k):
        for c in rep_copies(k):
            c.wait_recv()

        def body(m, _):
            for h in range(2):
                hs = half(h)
                a, b = pair(k, m, hs)
                g0, g1, g2, gt = [back[k, m, f, :, hs] for f in range(4)]
                inner_b = g0 * b[0] + g1 * b[1] + g2 * b[2] + gt * b[3]
                k_b = -(a[3] * inner_b)
                k_a = k_b - (g0 * a[0] + g1 * a[1] + g2 * a[2])
                part_a = (g0, g1, g2, k_a)
                part_b = (a[3] * g0, a[3] * g1, a[3] * g2, k_b)
                first = core == 0
                for f in range(4):
                    coz[k * HALF + core * 8 + m, f, :, hs] = jnp.where(first, part_a[f], part_b[f])
                    fin[k, m, f, :, hs] = jnp.where(first, part_b[f], part_a[f])
            return 0

        lax.fori_loop(0, 8, body, 0)
        fin_copy(k).start()

    def z_finish(k):
        fin_copy(k).wait_recv()
        coz[pl.ds(k * HALF + (1 - core) * 8, 8)] = finr[k]

    def x_compose():
        for g in range(4):
            for h in range(2):
                acc = None
                for s in range(NSEG):
                    rows = pl.ds(g * 64 + s, 8, stride=NSEG)
                    seg = tuple(xc[i, h, rows, :] for i in (2, 3, 4, 1))
                    acc = seg if acc is None else compose(acc, seg)
                for f in range(4):
                    xloc[g, f, :, half(h)] = acc[f]
        for c in x_copies():
            c.start()

    def x_merge():
        for c in x_copies():
            c.wait_recv()
        xgot[ix] = xloc[ix]
        sq = jnp.zeros((8, LANE), F32)
        for h in range(2):
            bricks = [[xgot[o, f, :, half(h)] for f in range(4)] for o in range(4)]
            target = [txf[c, pl.ds(pl.multiple_of(ix * 8, 8), 8), half(h)] for c in range(3)]
            replies, s = merge(bricks, target, inv_x)
            sq = sq + s
            for o in range(4):
                for f in range(4):
                    xrep[o, f, :, half(h)] = replies[o][f]
        err[4] = sq
        for c in xr_copies():
            c.start()
        xback[ix] = xrep[ix]

    def x_split():
        for c in xr_copies():
            c.wait_recv()
        for g in range(4):
            for h in range(2):
                g0, g1, g2, gt = [xback[g, f, :, half(h)] for f in range(4)]
                suffix = None
                for s in reversed(range(NSEG)):
                    rows = pl.ds(g * 64 + s, 8, stride=NSEG)
                    seg = tuple(xc[i, h, rows, :] for i in (2, 3, 4, 1))
                    suffix = seg if suffix is None else compose(seg, suffix)
                    xsuf[s] = g0 * suffix[0] + g1 * suffix[1] + g2 * suffix[2] + gt * suffix[3]
                front = jnp.ones((8, LANE), F32)
                for s in range(NSEG):
                    rows = pl.ds(g * 64 + s, 8, stride=NSEG)
                    cox[0, h, rows, :] = front * g0
                    cox[1, h, rows, :] = front * g1
                    cox[2, h, rows, :] = front * g2
                    cox[3, h, rows, :] = -(front * xsuf[s])
                    front = front * xc[1, h, rows, :]

    zs[...] = jnp.zeros_like(zs)
    xc[0] = jnp.zeros_like(xc[0])
    xc[1] = jnp.ones_like(xc[1])
    for i in (2, 3, 4):
        xc[i] = jnp.zeros_like(xc[i])

    def clear(m, _):
        for f in range(4):
            zc[m, f] = jnp.full((8, 256), float(f == 3), F32)
        return 0

    lax.fori_loop(0, SEG, clear, 0)
    load.wait(0, 0)

    def first(z, _):
        for h in range(2):
            upsample_part(ebuf0, sbuf0, tab, fine0, h, z)
        return 0

    lax.fori_loop(0, ZG, first, 0)

    bufs = ((ebuf0, sbuf0, fine0), (ebuf1, sbuf1, fine1))

    def pair_of_steps(i, _):
        for b in range(2):
            t = i * 2 + b
            k, zg = t // NZG, t % NZG
            other = bufs[1 - b]

            @pl.when(t + 2 < STEPS)
            def _():
                load.start(t + 2, b)

            @pl.when(t + 1 < STEPS)
            def _():
                load.wait(t + 1, 1 - b)

            forward_scan(
                bufs[b][2], zs, zc, xc, k, zg,
                lambda h, z: upsample_part(other[0], other[1], tab, other[2], h, z),
            )

        @pl.when(i == 3)
        def _():
            pl.semaphore_wait(barrier, 7)
            sib_copy(0).start()

        @pl.when(i == 5)
        def _():
            z_compose(0)

        return 0

    lax.fori_loop(0, STEPS // 2, pair_of_steps, 0)
    sib_copy(1).start()
    x_compose()
    tz_copy.wait()
    tx_copy.wait()

    def widen(c, _):
        for h in range(2):
            for s in range(NSEG):
                tzf[c, h, pl.ds(s * (SEG + 4), SEG), :] = tzb[c, pl.ds(s * SEG, SEG), half(h)].astype(F32)
        txf[c] = txb[c].astype(F32)
        return 0

    lax.fori_loop(0, 3, widen, 0)
    z_merge(0)
    z_compose(1)
    x_merge()
    z_split(0)
    x_split()
    z_merge(1)
    z_finish(0)
    z_split(1)
    z_finish(1)
    for k in range(2):
        for c in [sib_copy(k)] + chip_copies(k) + rep_copies(k) + [fin_copy(k)]:
            c.wait_send()
    for c in x_copies() + xr_copies():
        c.wait_send()


def backward_scan(fine, zcar, xcar, coz, cox, hl, k, zg, extra):
    for h in range(2):
        hs = half(h)
        rows = [pl.ds(pl.multiple_of((zg * ZG + z) * NSEG, NSEG), NSEG) for z in range(ZG)]
        start = tuple(xcar[i, h, rows[z], :] for z in range(ZG) for i in range(3))
        gx = [[cox[c, h, rows[z], :] for c in range(3)] for z in range(ZG)]

        def step(j, carry):
            carry = list(carry)
            extra(h, j)
            held = [[[None] * XU for _ in range(4)] for _ in range(ZG)]
            for u in range(XU):
                xm = j * XU + u
                zr = k * HALF + xm
                s_z, t_z, a_z = [zcar[i, zr, :, hs] for i in range(3)]
                g0, g1, g2 = [coz[zr, c, :, hs] for c in range(3)]
                for z in range(ZG):
                    e0, e1, e2, sg = [fine[f, z, h, pl.ds(xm, NSEG, stride=PITCH), :] for f in range(4)]
                    s_z = s_z + sg
                    t_new = jnp.exp2(s_z)
                    share_z = t_z - t_new
                    t_z = t_new
                    inner = g0 * e0 + g1 * e1 + g2 * e2
                    a_z = a_z + share_z * inner
                    grad = t_new * inner + a_z
                    h0, h1, h2 = gx[z]
                    s_x, t_x, a_x = carry[z * 3 : z * 3 + 3]
                    s_x = s_x + sg
                    t_new = jnp.exp2(s_x * 0.25)
                    share_x = t_x - t_new
                    inner = h0 * e0 + h1 * e1 + h2 * e2
                    a_x = a_x + share_x * inner
                    grad = grad + 0.25 * (t_new * inner + a_x)
                    carry[z * 3 : z * 3 + 3] = [s_x, t_new, a_x]
                    held[z][0][u] = g0 * share_z + h0 * share_x
                    held[z][1][u] = g1 * share_z + h1 * share_x
                    held[z][2][u] = g2 * share_z + h2 * share_x
                    held[z][3][u] = grad
                for i, v in enumerate((s_z, t_z, a_z)):
                    zcar[i, zr, :, hs] = v
                if u % 2:
                    for z in range(ZG):
                        for f in range(4):
                            v = jnp.concatenate(held[z][f][u - 1 : u + 1], axis=0)
                            hi = v.astype(BF16)
                            lo = (v - hi.astype(F32)).astype(BF16)
                            r = slice((u - 1) * 8, (u + 1) * 8)
                            hl[f, z, j, r, h * LANE : (h + 1) * LANE] = hi
                            hl[f, z, j, r, (h + 2) * LANE : (h + 3) * LANE] = lo
            return tuple(carry)

        carry = lax.fori_loop(0, HALF // XU, step, start)
        for z in range(ZG):
            for i in range(3):
                xcar[i, h, rows[z], :] = carry[z * 3 + i]


def down_part(hl, down, coarse, eout, sout, h, z):
    rows = NSEG * HALF
    for f in ((0, 1) if h == 0 else (2, 3)):
        a = hl[f, z].reshape(rows, 4 * LANE)
        r = jnp.dot(a, down[int(f == 3)], preferred_element_type=F32)
        for m in range(HALF):
            coarse[f, pl.ds(m, NSEG, stride=PITCH), :] = r[m * 8 : (m + 1) * 8]
        for s in range(NSEG):
            v = coarse[f, pl.ds(s * PITCH, HALF), :].astype(BF16)
            if f == 3:
                sout[z, s] = v
            else:
                eout[f, z, s] = v


def backward_kernel(
    e_hbm, s_hbm, tab, down, coz, cox,
    ge_hbm, gs_hbm,
    ebuf0, ebuf1, sbuf0, sbuf1, fine0, fine1, hl0, hl1, coarse,
    eout0, eout1, sout0, sout1, zcar, xcar,
    in_sem, out_sem,
):
    load = Loader(e_hbm, s_hbm, (ebuf0, ebuf1), (sbuf0, sbuf1), in_sem)
    load.start(0, 0)
    load.start(1, 1)
    eouts, souts = (eout0, eout1), (sout0, sout1)

    def stores(t, b):
        k, zg = t // NZG, t % NZG
        zr, xr = pl.ds(zg * ZG, ZG), pl.ds(pl.multiple_of(k * HALF, HALF), HALF)
        return (
            pltpu.make_async_copy(eouts[b], ge_hbm.at[:, zr, :, xr, :], out_sem.at[b, 0]),
            pltpu.make_async_copy(souts[b], gs_hbm.at[zr, :, xr, :], out_sem.at[b, 1]),
        )

    zcar[0] = jnp.zeros_like(zcar[0])
    zcar[1] = jnp.ones_like(zcar[1])
    zcar[2] = coz[:, 3]
    xcar[0] = jnp.zeros_like(xcar[0])
    xcar[1] = jnp.ones_like(xcar[1])
    xcar[2] = cox[3]
    load.wait(0, 0)

    def first(z, _):
        for h in range(2):
            upsample_part(ebuf0, sbuf0, tab, fine0, h, z)
        return 0

    lax.fori_loop(0, ZG, first, 0)
    bufs = ((ebuf0, sbuf0, fine0, hl0), (ebuf1, sbuf1, fine1, hl1))

    def pair_of_steps(i, _):
        for b in range(2):
            t = i * 2 + b
            k, zg = t // NZG, t % NZG
            other = bufs[1 - b]

            @pl.when(t + 2 < STEPS)
            def _():
                load.start(t + 2, b)

            @pl.when(t + 1 < STEPS)
            def _():
                load.wait(t + 1, 1 - b)

            @pl.when(t >= 3)
            def _():
                for c in stores(t - 3, 1 - b):
                    c.wait()

            def extra(h, z):
                upsample_part(other[0], other[1], tab, other[2], h, z)
                down_part(other[3], down, coarse, eouts[1 - b], souts[1 - b], h, z)

            backward_scan(bufs[b][2], zcar, xcar, coz, cox, bufs[b][3], k, zg, extra)

            @pl.when(t >= 1)
            def _():
                for c in stores(t - 1, 1 - b):
                    c.start()

        return 0

    lax.fori_loop(0, STEPS // 2, pair_of_steps, 0)
    last = (STEPS - 1) % 2
    for c in stores(STEPS - 3, last):
        c.wait()

    def final(z, _):
        for h in range(2):
            down_part(bufs[last][3], down, coarse, eouts[last], souts[last], h, z)
        return 0

    lax.fori_loop(0, ZG, final, 0)
    for c in stores(STEPS - 1, last):
        c.start()
    for t in (STEPS - 2, STEPS - 1):
        for c in stores(t, t % 2):
            c.wait()


def vmem(*shape, dtype=F32):
    return pltpu.VMEM(shape, dtype)


ANY = pl.BlockSpec(memory_space=pl.ANY)
IN_VMEM = pl.BlockSpec(memory_space=pltpu.VMEM)


def local(emission, absorption, target_z, target_x, owner_z, owner_x):
    depth_z, width_x, width_y = absorption.shape
    pixels = 2 * width_y
    count_x = lax.axis_size("gx")
    count_y = lax.axis_size("gy")
    count_z = lax.axis_size("gz")
    ix, iy, iz = lax.axis_index("gx"), lax.axis_index("gy"), lax.axis_index("gz")
    step_z = OPTICAL / (depth_z * count_z)
    step_x = OPTICAL / (width_x * count_x)
    interp = interp_table(width_y)
    rate = interp.T * (-step_z * math.log2(math.e))
    rate_hi = rate.astype(BF16)
    rate_lo = (rate - rate_hi.astype(np.float64)).astype(BF16)
    tab = np.concatenate([interp.T.astype(BF16), rate_hi, rate_lo], axis=0)
    down_e = np.concatenate([interp, interp], axis=0)
    down = np.stack([down_e, down_e * step_z]).astype(BF16)
    e5 = emission.reshape(3, depth_z, NSEG, SEG, width_y)
    s4 = absorption.reshape(depth_z, NSEG, SEG, width_y)

    buffers = [
        vmem(3, ZG, NSEG, HALF, LANE, dtype=BF16), vmem(3, ZG, NSEG, HALF, LANE, dtype=BF16),
        vmem(ZG, NSEG, HALF, LANE, dtype=BF16), vmem(ZG, NSEG, HALF, LANE, dtype=BF16),
        vmem(4, ZG, 2, NSEG * PITCH, LANE), vmem(4, ZG, 2, NSEG * PITCH, LANE),
    ]
    dma = pltpu.SemaphoreType.DMA
    coz, cox, err = pl.pallas_call(
        functools.partial(forward_kernel, 1.0 / step_z, 1.0 / step_x),
        out_shape=[
            jax.ShapeDtypeStruct((SEG, 4, NSEG, 256), F32),
            jax.ShapeDtypeStruct((4, 2, NZ * NSEG, LANE), F32),
            jax.ShapeDtypeStruct((5, 8, LANE), F32),
        ],
        in_specs=[ANY, ANY, ANY, ANY, IN_VMEM],
        out_specs=[IN_VMEM, IN_VMEM, IN_VMEM],
        scratch_shapes=buffers + [
            vmem(SEG, NSEG, 256), vmem(SEG, 4, NSEG, 256), vmem(5, 2, NZ * NSEG, LANE),
            vmem(3, 256, 256, dtype=BF16), vmem(3, NZ, 256, dtype=BF16),
            vmem(3, 2, NSEG * (SEG + 4), LANE), vmem(3, NZ, 256),
            vmem(2, 8, 4, 8, 256), vmem(2, 8, 4, 8, 256), vmem(2, 4, 2, 4, 8, 256), vmem(2, 4, 2, 4, 8, 256),
            vmem(2, 8, 4, 8, 256), vmem(2, 8, 4, 8, 256), vmem(2, 8, 4, 8, 256),
            vmem(4, 4, 8, 256), vmem(4, 4, 8, 256), vmem(4, 4, 8, 256), vmem(4, 4, 8, 256), vmem(NSEG, 8, LANE),
            dma((2, 2)), dma((2,)), dma((2, 2)), dma((2, 3, 2)), dma((2, 3, 2)), dma((2, 2)), dma((3, 2)), dma((3, 2)),
        ],
        compiler_params=pltpu.CompilerParams(
            collective_id=0, has_side_effects=True, vmem_limit_bytes=48 * 2**20
        ),
    )(e5, s4, target_z, target_x, tab)

    labels = jnp.arange(count_x * count_y * count_z, dtype=jnp.int32)
    group_z = count_y * count_z
    rows_z = lax.dynamic_index_in_dim(owner_z[..., 0], ix, 0, keepdims=False)
    rows_z = lax.dynamic_index_in_dim(rows_z, iy, 0, keepdims=False).reshape(NSEG, 2, 2, 4, 2)
    rows_z = lax.dynamic_index_in_dim(rows_z, iz % 2, 2, keepdims=False)
    rows_z = lax.dynamic_index_in_dim(rows_z, iz // 2, 2, keepdims=False)
    own_z = ix * group_z + jnp.transpose(rows_z, (1, 2, 0)).reshape(-1)
    rows_x = lax.dynamic_index_in_dim(owner_x[..., 0], iz, 1, keepdims=False)
    rows_x = lax.dynamic_index_in_dim(rows_x, iy, 0, keepdims=False)
    own_x = lax.dynamic_slice_in_dim(rows_x, ix * 8, 8, 0) * count_z + iz
    own = jnp.concatenate([own_z, own_x])
    tile_err = jnp.sum(err, axis=-1).reshape(-1)
    spread = jnp.sum(jnp.where(own[:, None] == labels[None, :], tile_err[:, None], 0.0), axis=0)
    owned = lax.psum_scatter(spread, ("gx", "gy", "gz"), scatter_dimension=0, tiled=True)
    slots = 2 * width_x // group_z + 2 * depth_z // (count_x * count_y)
    owned_error = (owned / (3.0 * pixels * slots)).reshape(1, 1, 1)

    grad_e, grad_s = pl.pallas_call(
        backward_kernel,
        out_shape=[jax.ShapeDtypeStruct(e5.shape, BF16), jax.ShapeDtypeStruct(s4.shape, BF16)],
        in_specs=[ANY, ANY, IN_VMEM, IN_VMEM, IN_VMEM, IN_VMEM],
        out_specs=[ANY, ANY],
        scratch_shapes=buffers + [
            vmem(4, ZG, HALF // XU, XU * 8, 4 * LANE, dtype=BF16), vmem(4, ZG, HALF // XU, XU * 8, 4 * LANE, dtype=BF16),
            vmem(4, NSEG * PITCH, LANE),
            vmem(3, ZG, NSEG, HALF, LANE, dtype=BF16), vmem(3, ZG, NSEG, HALF, LANE, dtype=BF16),
            vmem(ZG, NSEG, HALF, LANE, dtype=BF16), vmem(ZG, NSEG, HALF, LANE, dtype=BF16),
            vmem(3, SEG, NSEG, 256), vmem(3, 2, NZ * NSEG, LANE),
            dma((2, 2)), dma((2, 2)),
        ],
        compiler_params=pltpu.CompilerParams(vmem_limit_bytes=48 * 2**20),
        cost_estimate=pl.CostEstimate(flops=6 * 10**9, bytes_accessed=20 * 2**20, transcendentals=0),
    )(e5, s4, tab, down, coz, cox)
    return (grad_e.reshape(emission.shape), grad_s.reshape(absorption.shape), owned_error)


def solution(mesh):
    return jax.shard_map(
        local,
        mesh=mesh,
        in_specs=(P(None, "gz", "gx", "gy"), P("gz", "gx", "gy"), P(), P(), P(), P()),
        out_specs=(P(None, "gz", "gx", "gy"), P("gz", "gx", "gy"), P("gx", "gy", "gz")),
        check_vma=False,
    )
```

```python
import functools
import math

import jax
import jax.numpy as jnp
import numpy as np
from jax import lax
from jax.experimental import pallas as pl
from jax.experimental.pallas import tpu as pltpu
from jax.sharding import PartitionSpec as P

F32 = jnp.float32
BF16 = jnp.bfloat16
OPTICAL = 1.5
BACKLIGHT = 1.0

NSEG = 8
SEG = 32
HALF = 16
PITCH = 20
ZG = 4
NZ = 32
NZG = NZ // ZG
STEPS = 2 * NZG
LANE = 128


def interp_table(width):
    pixels = np.arange(2 * width)
    nearest = pixels // 2
    second = np.clip(nearest + 2 * (pixels % 2) - 1, 0, width - 1)
    columns = np.arange(width)
    return 0.75 * (columns[None, :] == nearest[:, None]) + 0.25 * (columns[None, :] == second[:, None])


def half(h):
    return slice(h * LANE, (h + 1) * LANE)


def upsample_store(fine, f, z, r):
    for s in range(NSEG):
        for h in range(2):
            fine[f, z, h, s * PITCH : s * PITCH + HALF] = r[s * HALF : (s + 1) * HALF, half(h)]


def upsample_part(ebuf, sbuf, tab, fine, part):
    rows = NSEG * HALF
    if part == 0:
        a = ebuf[0:2].reshape(2 * ZG * rows, LANE)
        r = jnp.dot(a, tab[0:LANE], preferred_element_type=F32)
        for f in range(2):
            for z in range(ZG):
                i = f * ZG + z
                upsample_store(fine, f, z, r[i * rows : (i + 1) * rows])
    else:
        r = jnp.dot(ebuf[2].reshape(ZG * rows, LANE), tab[0:LANE], preferred_element_type=F32)
        s = sbuf[...].reshape(ZG * rows, LANE)
        q = jnp.dot(jnp.concatenate([s, s], axis=1), tab[LANE:], preferred_element_type=F32)
        for z in range(ZG):
            upsample_store(fine, 2, z, r[z * rows : (z + 1) * rows])
            upsample_store(fine, 3, z, q[z * rows : (z + 1) * rows])


class Loader:
    def __init__(self, e_hbm, s_hbm, ebufs, sbufs, sems):
        self.refs = (e_hbm, s_hbm, ebufs, sbufs, sems)

    def copies(self, t, b):
        e_hbm, s_hbm, ebufs, sbufs, sems = self.refs
        k, zg = t // NZG, t % NZG
        zs, xs = pl.ds(zg * ZG, ZG), pl.ds(pl.multiple_of(k * HALF, HALF), HALF)
        return (
            pltpu.make_async_copy(e_hbm.at[:, zs, :, xs, :], ebufs[b], sems.at[b, 0]),
            pltpu.make_async_copy(s_hbm.at[zs, :, xs, :], sbufs[b], sems.at[b, 1]),
        )

    def start(self, t, b):
        for c in self.copies(t, b):
            c.start()

    def wait(self, t, b):
        for c in self.copies(t, b):
            c.wait()


def forward_scan(fine, zs, zc, xc, k, zg, extra):
    for h in range(2):
        hs = half(h)
        rows = [pl.ds(pl.multiple_of((zg * ZG + z) * NSEG, NSEG), NSEG) for z in range(ZG)]
        carry = [xc[i, h, rows[z], :] for z in range(ZG) for i in range(5)]
        extra(h)
        for xm in range(HALF):
            zr = k * HALF + xm
            s_z = zs[zr, :, hs]
            c0, c1, c2, t_z = [zc[zr, i, :, hs] for i in range(4)]
            for z in range(ZG):
                e0, e1, e2, sg = [fine[f, z, h, pl.ds(xm, NSEG, stride=PITCH), :] for f in range(4)]
                s_z = s_z + sg
                t_new = jnp.exp2(s_z)
                share = t_z - t_new
                t_z = t_new
                c0 = c0 + share * e0
                c1 = c1 + share * e1
                c2 = c2 + share * e2
                s_x, t_x, d0, d1, d2 = carry[z * 5 : z * 5 + 5]
                s_x = s_x + sg
                t_new = jnp.exp2(s_x * 0.25)
                share = t_x - t_new
                carry[z * 5 : z * 5 + 5] = [s_x, t_new, d0 + share * e0, d1 + share * e1, d2 + share * e2]
            zs[zr, :, hs] = s_z
            for i, v in enumerate((c0, c1, c2, t_z)):
                zc[zr, i, :, hs] = v
        for z in range(ZG):
            for i in range(5):
                xc[i, h, rows[z], :] = carry[z * 5 + i]


def compose(front, back):
    c0, c1, c2, t = front
    d0, d1, d2, u = back
    return (c0 + t * d0, c1 + t * d1, c2 + t * d2, t * u)


def merge(bricks, target, inv_step):
    ahead = (jnp.zeros_like(target[0]),) * 3 + (jnp.ones_like(target[0]),)
    fronts = []
    for brick in bricks:
        fronts.append(ahead[3])
        ahead = compose(ahead, brick)
    resid = [ahead[c] + ahead[3] * BACKLIGHT - target[c] for c in range(3)]
    g = [r * inv_step for r in resid]
    behind = [jnp.full_like(target[0], BACKLIGHT)] * 3
    replies = []
    for front, brick in reversed(list(zip(fronts, bricks))):
        dot = g[0] * behind[0] + g[1] * behind[1] + g[2] * behind[2]
        replies.append([front * g[0], front * g[1], front * g[2], front * dot])
        behind = [brick[c] + brick[3] * behind[c] for c in range(3)]
    replies.reverse()
    return replies, resid[0] * resid[0] + resid[1] * resid[1] + resid[2] * resid[2]


def forward_kernel(
    inv_z, inv_x, share,
    e_hbm, s_hbm, tz_hbm, tx_hbm, oz_hbm, ox_hbm, tab_hbm, perm_hbm,
    coz, cox, owned,
    ebuf0, ebuf1, sbuf0, sbuf1, fine0, fine1, zs, zc, xc,
    tzb, txb, tzf, txf,
    sib, pc, got, rep, back, fin, finr,
    xloc, xgot, xrep, xback, xsuf,
    tab, perm, err, ozb, oxb, ez, ex, ey,
    in_sem, t_sem, sem_sib, sem_chip, sem_rep, sem_fin, sem_x, sem_xr, sem_ez, sem_ex, sem_ey,
):
    ix, iy, iz = lax.axis_index("gx"), lax.axis_index("gy"), lax.axis_index("gz")
    chip, core = iz // 2, iz % 2
    load = Loader(e_hbm, s_hbm, (ebuf0, ebuf1), (sbuf0, sbuf1), in_sem)
    load.start(0, 0)
    load.start(1, 1)
    px = pl.ds(pl.multiple_of(iy * 256, 256), 256)
    tz_copy = pltpu.make_async_copy(tz_hbm.at[:, pl.ds(pl.multiple_of(ix * 256, 256), 256), px], tzb, t_sem.at[0])
    tx_copy = pltpu.make_async_copy(tx_hbm.at[:, pl.ds(pl.multiple_of(iz * NZ, NZ), NZ), px], txb, t_sem.at[1])
    oz_copy = pltpu.make_async_copy(oz_hbm.at[ix, iy], ozb, t_sem.at[2])
    ox_copy = pltpu.make_async_copy(ox_hbm.at[iy, iz], oxb, t_sem.at[3])
    tab_copy = pltpu.make_async_copy(tab_hbm, tab, t_sem.at[4])
    perm_copy = pltpu.make_async_copy(perm_hbm, perm, t_sem.at[5])
    tab_copy.start()
    late = (tz_copy, tx_copy, oz_copy, ox_copy, perm_copy)
    for c in late:
        c.start()

    sibling = {"gz": chip * 2 + 1 - core}
    chips = [{"gz": lax.rem(chip + d, 4) * 2 + core} for d in (1, 2, 3)]
    slabs = [{"gx": lax.rem(ix + d, 4)} for d in (1, 2, 3)]
    barrier = pltpu.get_barrier_semaphore()
    row = [{"gz": lax.rem(iz + d, 8)} for d in range(1, 8)]
    column = [{"gy": lax.rem(iy + d, 4)} for d in (1, 2, 3)]
    for peer in row + slabs + column:
        pl.semaphore_signal(barrier, inc=1, device_id=peer, device_id_type=pl.DeviceIdType.MESH)

    def remote(src, dst, sems, peer):
        return pltpu.make_async_remote_copy(
            src_ref=src, dst_ref=dst, send_sem=sems.at[0], recv_sem=sems.at[1],
            device_id=peer, device_id_type=pl.DeviceIdType.MESH,
        )

    def sib_copy(k):
        return remote(zc.at[pl.ds(k * HALF + (1 - core) * 8, 8)], sib.at[k], sem_sib.at[k], sibling)

    def chip_copies(k):
        return [
            remote(pc.at[k, pl.ds(lax.rem(chip + d, 4) * 2, 2)], got.at[k, chip], sem_chip.at[k, d - 1], chips[d - 1])
            for d in (1, 2, 3)
        ]

    def rep_copies(k):
        return [
            remote(rep.at[k, lax.rem(chip + d, 4)], back.at[k, pl.ds(chip * 2, 2)], sem_rep.at[k, d - 1], chips[d - 1])
            for d in (1, 2, 3)
        ]

    def fin_copy(k):
        return remote(fin.at[k], finr.at[k], sem_fin.at[k], sibling)

    def x_copies():
        return [remote(xloc.at[lax.rem(ix + d, 4)], xgot.at[ix], sem_x.at[d - 1], slabs[d - 1]) for d in (1, 2, 3)]

    def xr_copies():
        return [remote(xrep.at[lax.rem(ix + d, 4)], xback.at[ix], sem_xr.at[d - 1], slabs[d - 1]) for d in (1, 2, 3)]

    def pair(k, m, hs):
        mine = [zc[k * HALF + core * 8 + m, i, :, hs] for i in range(4)]
        other = [sib[k, m, i, :, hs] for i in range(4)]
        first = core == 0
        return [jnp.where(first, a, b) for a, b in zip(mine, other)], [jnp.where(first, b, a) for a, b in zip(mine, other)]

    def z_compose(k):
        sib_copy(k).wait_recv()

        def body(m, _):
            for h in range(2):
                front, rear = pair(k, m, half(h))
                for i, v in enumerate(compose(front, rear)):
                    pc[k, m, i, :, half(h)] = v
            return 0

        lax.fori_loop(0, 8, body, 0)
        for c in chip_copies(k):
            c.start()

    def z_merge(k):
        for c in chip_copies(k):
            c.wait_recv()
        for i in range(2):
            m = chip * 2 + i
            got[k, chip, i] = pc[k, m]
            sq = jnp.zeros((8, LANE), F32)
            for h in range(2):
                bricks = [[got[k, o, i, f, :, half(h)] for f in range(4)] for o in range(4)]
                row = k * HALF + core * 8 + m
                target = [tzf[c, h, pl.ds(row, NSEG, stride=SEG + 4), :] for c in range(3)]
                replies, s = merge(bricks, target, inv_z)
                sq = sq + s
                for o in range(4):
                    for f in range(4):
                        rep[k, o, i, f, :, half(h)] = replies[o][f]
            err[k * 2 + i] = sq
        for c in rep_copies(k):
            c.start()
        back[k, pl.ds(chip * 2, 2)] = rep[k, chip]

    def z_split(k):
        for c in rep_copies(k):
            c.wait_recv()

        def body(m, _):
            for h in range(2):
                hs = half(h)
                a, b = pair(k, m, hs)
                g0, g1, g2, gt = [back[k, m, f, :, hs] for f in range(4)]
                inner_b = g0 * b[0] + g1 * b[1] + g2 * b[2] + gt * b[3]
                k_b = -(a[3] * inner_b)
                k_a = k_b - (g0 * a[0] + g1 * a[1] + g2 * a[2])
                part_a = (g0, g1, g2, k_a)
                part_b = (a[3] * g0, a[3] * g1, a[3] * g2, k_b)
                first = core == 0
                for f in range(4):
                    coz[k * HALF + core * 8 + m, f, :, hs] = jnp.where(first, part_a[f], part_b[f])
                    fin[k, m, f, :, hs] = jnp.where(first, part_b[f], part_a[f])
            return 0

        lax.fori_loop(0, 8, body, 0)
        fin_copy(k).start()

    def z_finish(k):
        fin_copy(k).wait_recv()
        coz[pl.ds(k * HALF + (1 - core) * 8, 8)] = finr[k]

    def x_compose():
        for g in range(4):
            for h in range(2):
                acc = None
                for s in range(NSEG):
                    rows = pl.ds(g * 64 + s, 8, stride=NSEG)
                    seg = tuple(xc[i, h, rows, :] for i in (2, 3, 4, 1))
                    acc = seg if acc is None else compose(acc, seg)
                for f in range(4):
                    xloc[g, f, :, half(h)] = acc[f]
        for c in x_copies():
            c.start()

    def x_merge():
        for c in x_copies():
            c.wait_recv()
        xgot[ix] = xloc[ix]
        sq = jnp.zeros((8, LANE), F32)
        for h in range(2):
            bricks = [[xgot[o, f, :, half(h)] for f in range(4)] for o in range(4)]
            target = [txf[c, pl.ds(pl.multiple_of(ix * 8, 8), 8), half(h)] for c in range(3)]
            replies, s = merge(bricks, target, inv_x)
            sq = sq + s
            for o in range(4):
                for f in range(4):
                    xrep[o, f, :, half(h)] = replies[o][f]
        err[4] = sq
        for c in xr_copies():
            c.start()
        xback[ix] = xrep[ix]

    def x_split():
        for c in xr_copies():
            c.wait_recv()
        for g in range(4):
            for h in range(2):
                g0, g1, g2, gt = [xback[g, f, :, half(h)] for f in range(4)]
                suffix = None
                for s in reversed(range(NSEG)):
                    rows = pl.ds(g * 64 + s, 8, stride=NSEG)
                    seg = tuple(xc[i, h, rows, :] for i in (2, 3, 4, 1))
                    suffix = seg if suffix is None else compose(seg, suffix)
                    xsuf[s] = g0 * suffix[0] + g1 * suffix[1] + g2 * suffix[2] + gt * suffix[3]
                front = jnp.ones((8, LANE), F32)
                for s in range(NSEG):
                    rows = pl.ds(g * 64 + s, 8, stride=NSEG)
                    cox[0, h, rows, :] = front * g0
                    cox[1, h, rows, :] = front * g1
                    cox[2, h, rows, :] = front * g2
                    cox[3, h, rows, :] = -(front * xsuf[s])
                    front = front * xc[1, h, rows, :]

    lane = lax.broadcasted_iota(jnp.int32, (8, LANE), 1)
    sub = lax.broadcasted_iota(jnp.int32, (8, LANE), 0)

    def scatter(sq, ids):
        owner = jnp.zeros((8, LANE), jnp.int32)
        for s, o in enumerate(ids):
            owner = jnp.where(sub == s, o, owner)
        return jnp.where(lane == owner, jnp.sum(sq, axis=1, keepdims=True), 0.0)

    def ez_copies():
        return [remote(ez.at[7], ez.at[d - 1], sem_ez.at[d - 1], row[d - 1]) for d in range(1, 8)]

    def ex_copies():
        return [remote(ex.at[3], ex.at[d - 1], sem_ex.at[d - 1], slabs[d - 1]) for d in (1, 2, 3)]

    def ey_copies():
        return [remote(ey.at[3], ey.at[d - 1], sem_ey.at[d - 1], column[d - 1]) for d in (1, 2, 3)]

    def err_start():
        total = jnp.zeros((8, LANE), F32)
        for k in range(2):
            for i in range(2):
                cell = k * HALF + core * 8 + chip * 2 + i
                total = total + scatter(err[k * 2 + i], [ix * 32 + ozb[0, s * SEG + cell] for s in range(NSEG)])
        ez[7] = total
        ex[3] = scatter(err[4], [oxb[0, ix * 8 + s] * 8 + iz for s in range(8)])
        for c in ez_copies() + ex_copies():
            c.start()

    def err_middle():
        for c in ez_copies() + ex_copies():
            c.wait_recv()
        total = ez[7] + ex[3]
        for d in range(7):
            total = total + ez[d]
        for d in range(3):
            total = total + ex[d]
        ey[3] = total
        for c in ey_copies():
            c.start()

    def err_finish():
        for c in ey_copies():
            c.wait_recv()
        total = ey[0] + ey[1] + ey[2] + ey[3]
        mine = jnp.where(lane == ix * 32 + iy * 8 + iz, total, 0.0)
        owned[0, 0] = jnp.sum(mine) * share

    zs[...] = jnp.zeros_like(zs)
    xc[0] = jnp.zeros_like(xc[0])
    xc[1] = jnp.ones_like(xc[1])
    for i in (2, 3, 4):
        xc[i] = jnp.zeros_like(xc[i])

    def clear(m, _):
        for f in range(4):
            zc[m, f] = jnp.full((8, 256), float(f == 3), F32)
        return 0

    lax.fori_loop(0, SEG, clear, 0)
    load.wait(0, 0)
    tab_copy.wait()
    for part in range(2):
        upsample_part(ebuf0, sbuf0, tab, fine0, part)

    bufs = ((ebuf0, sbuf0, fine0), (ebuf1, sbuf1, fine1))

    def pair_of_steps(i, _):
        for b in range(2):
            t = i * 2 + b
            k, zg = t // NZG, t % NZG
            other = bufs[1 - b]

            @pl.when(t + 2 < STEPS)
            def _():
                load.start(t + 2, b)

            @pl.when(t + 1 < STEPS)
            def _():
                load.wait(t + 1, 1 - b)

            forward_scan(
                bufs[b][2], zs, zc, xc, k, zg,
                lambda part: upsample_part(other[0], other[1], tab, other[2], part),
            )

        @pl.when(i == 3)
        def _():
            pl.semaphore_wait(barrier, 13)
            sib_copy(0).start()

        @pl.when(i == 4)
        def _():
            z_compose(0)

        return 0

    lax.fori_loop(0, STEPS // 2, pair_of_steps, 0)
    sib_copy(1).start()
    x_compose()
    for c in late:
        c.wait()

    def widen(c, _):
        r = jnp.dot(tzb[c], perm[...], preferred_element_type=F32)
        for h in range(2):
            for s in range(NSEG):
                tzf[c, h, pl.ds(s * (SEG + 4), SEG), :] = r[s * SEG : (s + 1) * SEG, half(h)]
        txf[c] = jnp.dot(txb[c], perm[...], preferred_element_type=F32)
        return 0

    lax.fori_loop(0, 3, widen, 0)
    z_merge(0)
    z_compose(1)
    x_merge()
    z_split(0)
    z_merge(1)
    err_start()
    x_split()
    z_finish(0)
    z_split(1)
    err_middle()
    z_finish(1)
    err_finish()
    for k in range(2):
        for c in [sib_copy(k)] + chip_copies(k) + rep_copies(k) + [fin_copy(k)]:
            c.wait_send()
    for c in x_copies() + xr_copies() + ez_copies() + ex_copies() + ey_copies():
        c.wait_send()


def project_down(even, odd, first, last, near, far):
    side = jnp.where(first, even, pltpu.roll(odd, 1, axis=1)) + jnp.where(last, odd, pltpu.roll(even, LANE - 1, axis=1))
    return near * (even + odd) + (side if far is None else far * side)


def backward_scan(fine, zcar, xcar, coz, cox, coarse, k, zg, pair, far):
    lanes = lax.broadcasted_iota(jnp.int32, (NSEG, LANE), 1)
    first, last = lanes == 0, lanes == LANE - 1
    planes = [pair * 2 + i for i in range(2)]
    rows = [pl.ds(pl.multiple_of((zg * ZG + z) * NSEG, NSEG), NSEG) for z in planes]
    carry = [[[xcar[i, h, r, :] for i in range(3)] for h in range(2)] for r in rows]
    gx = [[[cox[c, h, r, :] for c in range(3)] for h in range(2)] for r in rows]
    for xm in range(HALF):
        zr = k * HALF + xm
        z_carry = [[zcar[i, zr, :, half(h)] for i in range(3)] for h in range(2)]
        gz = [[coz[zr, c, :, half(h)] for c in range(3)] for h in range(2)]
        for n, z in enumerate(planes):
            out = [[None] * 2 for _ in range(4)]
            for h in range(2):
                e0, e1, e2, sg = [fine[f, z, h, pl.ds(xm, NSEG, stride=PITCH), :] for f in range(4)]
                g0, g1, g2 = gz[h]
                s_z, t_z, a_z = z_carry[h]
                s_z = s_z + sg
                t_new = jnp.exp2(s_z)
                share_z = t_z - t_new
                inner = g0 * e0 + g1 * e1 + g2 * e2
                a_z = a_z + share_z * inner
                grad = t_new * inner + a_z
                z_carry[h] = [s_z, t_new, a_z]
                h0, h1, h2 = gx[n][h]
                s_x, t_x, a_x = carry[n][h]
                s_x = s_x + sg
                t_new = jnp.exp2(s_x * 0.25)
                share_x = t_x - t_new
                inner = h0 * e0 + h1 * e1 + h2 * e2
                a_x = a_x + share_x * inner
                out[3][h] = grad + 0.25 * (t_new * inner + a_x)
                carry[n][h] = [s_x, t_new, a_x]
                out[0][h] = g0 * share_z + h0 * share_x
                out[1][h] = g1 * share_z + h1 * share_x
                out[2][h] = g2 * share_z + h2 * share_x
            for f in range(4):
                v = project_down(out[f][0], out[f][1], first, last, 3.0 * far if f == 3 else 3.0, far if f == 3 else None)
                coarse[f, z, pl.ds(xm, NSEG, stride=PITCH), :] = v
        for h in range(2):
            for i in range(3):
                zcar[i, zr, :, half(h)] = z_carry[h][i]
    for n, r in enumerate(rows):
        for h in range(2):
            for i in range(3):
                xcar[i, h, r, :] = carry[n][h][i]


def narrow_part(coarse, eout, sout, part):
    for z in (2 * part, 2 * part + 1):
        for f in range(4):
            for s in range(NSEG):
                v = coarse[f, z, pl.ds(s * PITCH, HALF), :].astype(BF16)
                if f == 3:
                    sout[z, s] = v
                else:
                    eout[f, z, s] = v


def backward_kernel(
    far,
    e_hbm, s_hbm, tab_hbm, coz, cox,
    ge_hbm, gs_hbm,
    ebuf0, ebuf1, sbuf0, sbuf1, fine0, fine1, tab, coarse0, coarse1,
    eout0, eout1, sout0, sout1, zcar, xcar,
    in_sem, out_sem, tab_sem,
):
    tab_copy = pltpu.make_async_copy(tab_hbm, tab, tab_sem)
    tab_copy.start()
    load = Loader(e_hbm, s_hbm, (ebuf0, ebuf1), (sbuf0, sbuf1), in_sem)
    load.start(0, 0)
    load.start(1, 1)
    eouts, souts = (eout0, eout1), (sout0, sout1)

    def stores(t, b):
        k, zg = t // NZG, t % NZG
        zr, xr = pl.ds(zg * ZG, ZG), pl.ds(pl.multiple_of(k * HALF, HALF), HALF)
        return (
            pltpu.make_async_copy(eouts[b], ge_hbm.at[:, zr, :, xr, :], out_sem.at[b, 0]),
            pltpu.make_async_copy(souts[b], gs_hbm.at[zr, :, xr, :], out_sem.at[b, 1]),
        )

    zcar[0] = jnp.zeros_like(zcar[0])
    zcar[1] = jnp.ones_like(zcar[1])
    zcar[2] = coz[:, 3]
    xcar[0] = jnp.zeros_like(xcar[0])
    xcar[1] = jnp.ones_like(xcar[1])
    xcar[2] = cox[3]
    load.wait(0, 0)
    tab_copy.wait()
    for part in range(2):
        upsample_part(ebuf0, sbuf0, tab, fine0, part)
    bufs = ((ebuf0, sbuf0, fine0, coarse0), (ebuf1, sbuf1, fine1, coarse1))

    def pair_of_steps(i, _):
        for b in range(2):
            t = i * 2 + b
            k, zg = t // NZG, t % NZG
            other = bufs[1 - b]

            @pl.when(t + 2 < STEPS)
            def _():
                load.start(t + 2, b)

            @pl.when(t + 1 < STEPS)
            def _():
                load.wait(t + 1, 1 - b)

            @pl.when(t >= 3)
            def _():
                for c in stores(t - 3, 1 - b):
                    c.wait()

            for part in range(2):
                upsample_part(other[0], other[1], tab, other[2], part)
                narrow_part(other[3], eouts[1 - b], souts[1 - b], part)
                backward_scan(bufs[b][2], zcar, xcar, coz, cox, bufs[b][3], k, zg, part, far)

            @pl.when(t >= 1)
            def _():
                for c in stores(t - 1, 1 - b):
                    c.start()

        return 0

    lax.fori_loop(0, STEPS // 2, pair_of_steps, 0)
    last = (STEPS - 1) % 2
    for c in stores(STEPS - 3, last):
        c.wait()
    for part in range(2):
        narrow_part(bufs[last][3], eouts[last], souts[last], part)
    for c in stores(STEPS - 1, last):
        c.start()
    for t in (STEPS - 2, STEPS - 1):
        for c in stores(t, t % 2):
            c.wait()


def vmem(*shape, dtype=F32):
    return pltpu.VMEM(shape, dtype)


HBM = pl.BlockSpec(memory_space=pltpu.HBM)
IN_VMEM = pl.BlockSpec(memory_space=pltpu.VMEM)


def local(emission, absorption, target_z, target_x, owner_z, owner_x):
    depth_z, width_x, width_y = absorption.shape
    pixels = 2 * width_y
    count_x = lax.axis_size("gx")
    count_y = lax.axis_size("gy")
    count_z = lax.axis_size("gz")
    step_z = OPTICAL / (depth_z * count_z)
    step_x = OPTICAL / (width_x * count_x)
    interp = interp_table(width_y)
    rate = interp.T * (-step_z * math.log2(math.e))
    order = np.concatenate([np.arange(0, pixels, 2), np.arange(1, pixels, 2)])
    rate_hi = rate.astype(BF16)
    rate_lo = (rate - rate_hi.astype(np.float64)).astype(BF16)
    tab = np.concatenate([interp.T.astype(BF16), rate_hi, rate_lo], axis=0)[:, order]
    perm = np.eye(pixels)[:, order].astype(BF16)
    slots = 2 * width_x // (count_y * count_z) + 2 * depth_z // (count_x * count_y)
    e5 = emission.reshape(3, depth_z, NSEG, SEG, width_y)
    s4 = absorption.reshape(depth_z, NSEG, SEG, width_y)

    buffers = [
        vmem(3, ZG, NSEG, HALF, LANE, dtype=BF16), vmem(3, ZG, NSEG, HALF, LANE, dtype=BF16),
        vmem(ZG, NSEG, HALF, LANE, dtype=BF16), vmem(ZG, NSEG, HALF, LANE, dtype=BF16),
        vmem(4, ZG, 2, NSEG * PITCH, LANE), vmem(4, ZG, 2, NSEG * PITCH, LANE),
    ]
    dma = pltpu.SemaphoreType.DMA
    coz, cox, owned = pl.pallas_call(
        functools.partial(forward_kernel, 0.25 / step_z, 0.25 / step_x, 1.0 / (3.0 * pixels * slots)),
        out_shape=[
            jax.ShapeDtypeStruct((SEG, 4, NSEG, 256), F32),
            jax.ShapeDtypeStruct((4, 2, NZ * NSEG, LANE), F32),
            jax.ShapeDtypeStruct((1, 1), F32),
        ],
        in_specs=[HBM] * 8,
        out_specs=[IN_VMEM, IN_VMEM, pl.BlockSpec(memory_space=pltpu.SMEM)],
        scratch_shapes=buffers + [
            vmem(SEG, NSEG, 256), vmem(SEG, 4, NSEG, 256), vmem(5, 2, NZ * NSEG, LANE),
            vmem(3, 256, 256, dtype=BF16), vmem(3, NZ, 256, dtype=BF16),
            vmem(3, 2, NSEG * (SEG + 4), LANE), vmem(3, NZ, 256),
            vmem(2, 8, 4, 8, 256), vmem(2, 8, 4, 8, 256), vmem(2, 4, 2, 4, 8, 256), vmem(2, 4, 2, 4, 8, 256),
            vmem(2, 8, 4, 8, 256), vmem(2, 8, 4, 8, 256), vmem(2, 8, 4, 8, 256),
            vmem(4, 4, 8, 256), vmem(4, 4, 8, 256), vmem(4, 4, 8, 256), vmem(4, 4, 8, 256), vmem(NSEG, 8, LANE),
            vmem(3 * LANE, 256, dtype=BF16), vmem(256, 256, dtype=BF16), vmem(5, 8, LANE),
            pltpu.SMEM((1, 256), jnp.int32), pltpu.SMEM((1, NZ), jnp.int32),
            vmem(8, 8, LANE), vmem(4, 8, LANE), vmem(4, 8, LANE),
            dma((2, 2)), dma((6,)), dma((2, 2)), dma((2, 3, 2)), dma((2, 3, 2)), dma((2, 2)), dma((3, 2)), dma((3, 2)),
            dma((7, 2)), dma((3, 2)), dma((3, 2)),
        ],
        compiler_params=pltpu.CompilerParams(
            collective_id=0, has_side_effects=True, vmem_limit_bytes=48 * 2**20
        ),
    )(
        e5, s4, target_z, target_x, owner_z.reshape(count_x, count_y, 1, width_x),
        owner_x.reshape(count_y, count_z, 1, depth_z), tab, perm,
    )

    grad_e, grad_s = pl.pallas_call(
        functools.partial(backward_kernel, step_z),
        out_shape=[jax.ShapeDtypeStruct(e5.shape, BF16), jax.ShapeDtypeStruct(s4.shape, BF16)],
        in_specs=[HBM, HBM, HBM, IN_VMEM, IN_VMEM],
        out_specs=[HBM, HBM],
        scratch_shapes=buffers + [
            vmem(3 * LANE, 256, dtype=BF16), vmem(4, ZG, NSEG * PITCH, LANE), vmem(4, ZG, NSEG * PITCH, LANE),
            vmem(3, ZG, NSEG, HALF, LANE, dtype=BF16), vmem(3, ZG, NSEG, HALF, LANE, dtype=BF16),
            vmem(ZG, NSEG, HALF, LANE, dtype=BF16), vmem(ZG, NSEG, HALF, LANE, dtype=BF16),
            vmem(3, SEG, NSEG, 256), vmem(3, 2, NZ * NSEG, LANE),
            dma((2, 2)), dma((2, 2)), dma(()),
        ],
        compiler_params=pltpu.CompilerParams(vmem_limit_bytes=48 * 2**20),
        cost_estimate=pl.CostEstimate(flops=6 * 10**9, bytes_accessed=20 * 2**20, transcendentals=0),
    )(e5, s4, tab, coz, cox)
    return (grad_e.reshape(emission.shape), grad_s.reshape(absorption.shape), owned.reshape(1, 1, 1))


def solution(mesh):
    return jax.shard_map(
        local,
        mesh=mesh,
        in_specs=(P(None, "gz", "gx", "gy"), P("gz", "gx", "gy"), P(), P(), P(), P()),
        out_specs=(P(None, "gz", "gx", "gy"), P("gz", "gx", "gy"), P("gx", "gy", "gz")),
        check_vma=False,
    )
```

```python
import functools
import math

import jax
import jax.numpy as jnp
import numpy as np
from jax import lax
from jax.experimental import pallas as pl
from jax.experimental.pallas import tpu as pltpu
from jax.sharding import PartitionSpec as P

F32 = jnp.float32
BF16 = jnp.bfloat16
OPTICAL = 1.5
BACKLIGHT = 1.0

NSEG = 8
SEG = 32
HALF = 16
PITCH = 20
ZG = 4
NZ = 32
NZG = NZ // ZG
STEPS = 2 * NZG
LANE = 128
VMEM_LIMIT = 61 * 2**20 + 2**19


def interp_table(width):
    pixels = np.arange(2 * width)
    nearest = pixels // 2
    second = np.clip(nearest + 2 * (pixels % 2) - 1, 0, width - 1)
    columns = np.arange(width)
    return 0.75 * (columns[None, :] == nearest[:, None]) + 0.25 * (columns[None, :] == second[:, None])


def half(h):
    return slice(h * LANE, (h + 1) * LANE)


def upsample_store(fine, f, z, r):
    for s in range(NSEG):
        for h in range(2):
            fine[f, z, h, s * PITCH : s * PITCH + HALF] = r[s * HALF : (s + 1) * HALF, half(h)]


def upsample_part(ebuf, sbuf, t, tab, fine, part):
    rows = NSEG * HALF
    if part == 0:
        a = ebuf[t, 0:2].reshape(2 * ZG * rows, LANE)
        r = jnp.dot(a, tab[0:LANE], preferred_element_type=F32)
        for f in range(2):
            for z in range(ZG):
                i = f * ZG + z
                upsample_store(fine, f, z, r[i * rows : (i + 1) * rows])
    else:
        r = jnp.dot(ebuf[t, 2].reshape(ZG * rows, LANE), tab[0:LANE], preferred_element_type=F32)
        s = sbuf[t].reshape(ZG * rows, LANE)
        q = jnp.dot(jnp.concatenate([s, s], axis=1), tab[LANE:], preferred_element_type=F32)
        for z in range(ZG):
            upsample_store(fine, 2, z, r[z * rows : (z + 1) * rows])
            upsample_store(fine, 3, z, q[z * rows : (z + 1) * rows])


class Loader:
    def __init__(self, e_hbm, s_hbm, ebuf, sbuf, sems):
        self.refs = (e_hbm, s_hbm, ebuf, sbuf, sems)

    def copies(self, t):
        e_hbm, s_hbm, ebuf, sbuf, sems = self.refs
        k, zg = t // NZG, t % NZG
        zs, xs = pl.ds(zg * ZG, ZG), pl.ds(pl.multiple_of(k * HALF, HALF), HALF)
        return (
            pltpu.make_async_copy(e_hbm.at[:, zs, :, xs, :], ebuf.at[t], sems.at[t, 0]),
            pltpu.make_async_copy(s_hbm.at[zs, :, xs, :], sbuf.at[t], sems.at[t, 1]),
        )

    def start(self):
        def one(t, _):
            for c in self.copies(t):
                c.start()
            return 0

        lax.fori_loop(0, STEPS, one, 0)

    def wait(self, t):
        for c in self.copies(t):
            c.wait()


def forward_scan(fine, zc, xc, k, zg, extra):
    for h in range(2):
        hs = half(h)
        rows = [pl.ds(pl.multiple_of((zg * ZG + z) * NSEG, NSEG), NSEG) for z in range(ZG)]
        carry = [[xc[i, h, r, :] for i in range(4)] for r in rows]
        extra(h)
        for xm in range(HALF):
            zr = k * HALF + xm
            c0, c1, c2, t_z = [zc[zr, i, :, hs] for i in range(4)]
            for z in range(ZG):
                e0, e1, e2, sg = [fine[f, z, h, pl.ds(xm, NSEG, stride=PITCH), :] for f in range(4)]
                t_new = t_z * jnp.exp2(sg)
                share = t_z - t_new
                t_z = t_new
                c0 = c0 + share * e0
                c1 = c1 + share * e1
                c2 = c2 + share * e2
                d0, d1, d2, t_x = carry[z]
                t_new = t_x * jnp.exp2(sg * 0.25)
                share = t_x - t_new
                carry[z] = [d0 + share * e0, d1 + share * e1, d2 + share * e2, t_new]
            for i, v in enumerate((c0, c1, c2, t_z)):
                zc[zr, i, :, hs] = v
        for z in range(ZG):
            for i in range(4):
                xc[i, h, rows[z], :] = carry[z][i]


def compose(front, back):
    c0, c1, c2, t = front
    d0, d1, d2, u = back
    return (c0 + t * d0, c1 + t * d1, c2 + t * d2, t * u)


def merge(bricks, target, inv_step):
    ahead = (jnp.zeros_like(target[0]),) * 3 + (jnp.ones_like(target[0]),)
    fronts = []
    for brick in bricks:
        fronts.append(ahead[3])
        ahead = compose(ahead, brick)
    resid = [ahead[c] + ahead[3] * BACKLIGHT - target[c] for c in range(3)]
    g = [r * inv_step for r in resid]
    behind = [jnp.full_like(target[0], BACKLIGHT)] * 3
    replies = []
    for front, brick in reversed(list(zip(fronts, bricks))):
        dot = g[0] * behind[0] + g[1] * behind[1] + g[2] * behind[2]
        replies.append([front * g[0], front * g[1], front * g[2], front * dot])
        behind = [brick[c] + brick[3] * behind[c] for c in range(3)]
    replies.reverse()
    return replies, resid[0] * resid[0] + resid[1] * resid[1] + resid[2] * resid[2]


def forward_kernel(
    step_z, step_x, share,
    e_hbm, s_hbm, tz_hbm, tx_hbm, oz_hbm, ox_hbm, tab_hbm, perm_hbm,
    coz_hbm, cox_hbm, owned,
    ebuf, sbuf, fine0, fine1, zc, xc, coz, cox,
    tzb, txb, tzf, txf,
    sib, pc, got, rep, back, fin, finr,
    xloc, xgot, xrep, xback, xsuf,
    tab, perm, err, ozb, oxb, ez, ex, ey,
    in_sem, t_sem, sem_sib, sem_chip, sem_rep, sem_fin, sem_x, sem_xr, sem_ez, sem_ex, sem_ey, sem_co,
):
    ix, iy, iz = lax.axis_index("gx"), lax.axis_index("gy"), lax.axis_index("gz")
    chip, core = iz // 2, iz % 2
    load = Loader(e_hbm, s_hbm, ebuf, sbuf, in_sem)
    load.start()
    lane = lax.broadcasted_iota(jnp.int32, (8, LANE), 1)
    sub = lax.broadcasted_iota(jnp.int32, (8, LANE), 0)
    weight = jnp.where(lane == 0, 1.0, 0.75)
    px = pl.ds(pl.multiple_of(iy * 256, 256), 256)
    tz_copy = pltpu.make_async_copy(tz_hbm.at[:, pl.ds(pl.multiple_of(ix * 256, 256), 256), px], tzb, t_sem.at[0])
    tx_copy = pltpu.make_async_copy(tx_hbm.at[:, pl.ds(pl.multiple_of(iz * NZ, NZ), NZ), px], txb, t_sem.at[1])
    oz_copy = pltpu.make_async_copy(oz_hbm.at[ix, iy], ozb, t_sem.at[2])
    ox_copy = pltpu.make_async_copy(ox_hbm.at[iy, iz], oxb, t_sem.at[3])
    tab_copy = pltpu.make_async_copy(tab_hbm, tab, t_sem.at[4])
    perm_copy = pltpu.make_async_copy(perm_hbm, perm, t_sem.at[5])
    tab_copy.start()
    late = (tz_copy, tx_copy, oz_copy, ox_copy, perm_copy)
    for c in late:
        c.start()

    sibling = {"gz": chip * 2 + 1 - core}
    chips = [{"gz": lax.rem(chip + d, 4) * 2 + core} for d in (1, 2, 3)]
    slabs = [{"gx": lax.rem(ix + d, 4)} for d in (1, 2, 3)]
    barrier = pltpu.get_barrier_semaphore()
    row = [{"gz": lax.rem(iz + d, 8)} for d in range(1, 8)]
    column = [{"gy": lax.rem(iy + d, 4)} for d in (1, 2, 3)]
    for peer in row + slabs + column:
        pl.semaphore_signal(barrier, inc=1, device_id=peer, device_id_type=pl.DeviceIdType.MESH)

    def remote(src, dst, sems, peer):
        return pltpu.make_async_remote_copy(
            src_ref=src, dst_ref=dst, send_sem=sems.at[0], recv_sem=sems.at[1],
            device_id=peer, device_id_type=pl.DeviceIdType.MESH,
        )

    def sib_copy(k):
        return remote(zc.at[pl.ds(k * HALF + (1 - core) * 8, 8)], sib.at[k], sem_sib.at[k], sibling)

    def chip_copies(k):
        return [
            remote(pc.at[k, pl.ds(lax.rem(chip + d, 4) * 2, 2)], got.at[k, chip], sem_chip.at[k, d - 1], chips[d - 1])
            for d in (1, 2, 3)
        ]

    def rep_copies(k):
        return [
            remote(rep.at[k, lax.rem(chip + d, 4)], back.at[k, pl.ds(chip * 2, 2)], sem_rep.at[k, d - 1], chips[d - 1])
            for d in (1, 2, 3)
        ]

    def fin_copy(k):
        return remote(fin.at[k], finr.at[k], sem_fin.at[k], sibling)

    def x_copies():
        return [remote(xloc.at[lax.rem(ix + d, 4)], xgot.at[ix], sem_x.at[d - 1], slabs[d - 1]) for d in (1, 2, 3)]

    def xr_copies():
        return [remote(xrep.at[lax.rem(ix + d, 4)], xback.at[ix], sem_xr.at[d - 1], slabs[d - 1]) for d in (1, 2, 3)]

    def pair(k, m, hs):
        mine = [zc[k * HALF + core * 8 + m, i, :, hs] for i in range(4)]
        other = [sib[k, m, i, :, hs] for i in range(4)]
        first = core == 0
        return [jnp.where(first, a, b) for a, b in zip(mine, other)], [jnp.where(first, b, a) for a, b in zip(mine, other)]

    def z_compose(k):
        sib_copy(k).wait_recv()

        def body(m, _):
            for h in range(2):
                front, rear = pair(k, m, half(h))
                for i, v in enumerate(compose(front, rear)):
                    pc[k, m, i, :, half(h)] = v
            return 0

        lax.fori_loop(0, 8, body, 0)
        for c in chip_copies(k):
            c.start()

    def z_merge(k):
        for c in chip_copies(k):
            c.wait_recv()
        for i in range(2):
            m = chip * 2 + i
            got[k, chip, i] = pc[k, m]
            sq = jnp.zeros((8, LANE), F32)
            for h in range(2):
                bricks = [[got[k, o, i, f, :, half(h)] for f in range(4)] for o in range(4)]
                row = k * HALF + core * 8 + m
                target = [tzf[c, h, pl.ds(row, NSEG, stride=SEG + 4), :] for c in range(3)]
                replies, s = merge(bricks, target, weight * (1.0 / step_z))
                sq = sq + s
                for o in range(4):
                    for f in range(4):
                        rep[k, o, i, f, :, half(h)] = replies[o][f]
            err[k * 2 + i] = sq
        for c in rep_copies(k):
            c.start()
        back[k, pl.ds(chip * 2, 2)] = rep[k, chip]

    def z_split(k):
        for c in rep_copies(k):
            c.wait_recv()

        def body(m, _):
            for h in range(2):
                hs = half(h)
                a, b = pair(k, m, hs)
                g0, g1, g2, gt = [back[k, m, f, :, hs] for f in range(4)]
                inner_b = g0 * b[0] + g1 * b[1] + g2 * b[2] + gt * b[3]
                k_b = -(a[3] * inner_b)
                k_a = k_b - (g0 * a[0] + g1 * a[1] + g2 * a[2])
                part_a = (g0, g1, g2, k_a * step_z)
                part_b = (a[3] * g0, a[3] * g1, a[3] * g2, k_b * step_z)
                first = core == 0
                for f in range(4):
                    coz[k * HALF + core * 8 + m, f, :, hs] = jnp.where(first, part_a[f], part_b[f])
                    fin[k, m, f, :, hs] = jnp.where(first, part_b[f], part_a[f])
            return 0

        lax.fori_loop(0, 8, body, 0)
        fin_copy(k).start()
        out_copies(k)[0].start()

    def out_copies(k):
        mine, other = pl.ds(k * HALF + core * 8, 8), pl.ds(k * HALF + (1 - core) * 8, 8)
        return (
            pltpu.make_async_copy(coz.at[mine], coz_hbm.at[mine], sem_co.at[k]),
            pltpu.make_async_copy(finr.at[k], coz_hbm.at[other], sem_co.at[2 + k]),
        )

    def z_finish(k):
        fin_copy(k).wait_recv()
        out_copies(k)[1].start()

    def x_compose():
        for g in range(4):
            for h in range(2):
                acc = None
                for s in range(NSEG):
                    rows = pl.ds(g * 64 + s, 8, stride=NSEG)
                    seg = tuple(xc[i, h, rows, :] for i in range(4))
                    acc = seg if acc is None else compose(acc, seg)
                for f in range(4):
                    xloc[g, f, :, half(h)] = acc[f]
        for c in x_copies():
            c.start()

    def x_merge():
        for c in x_copies():
            c.wait_recv()
        xgot[ix] = xloc[ix]
        sq = jnp.zeros((8, LANE), F32)
        for h in range(2):
            bricks = [[xgot[o, f, :, half(h)] for f in range(4)] for o in range(4)]
            target = [txf[c, pl.ds(pl.multiple_of(ix * 8, 8), 8), half(h)] for c in range(3)]
            replies, s = merge(bricks, target, weight * (1.0 / step_x))
            sq = sq + s
            for o in range(4):
                for f in range(4):
                    xrep[o, f, :, half(h)] = replies[o][f]
        err[4] = sq
        for c in xr_copies():
            c.start()
        xback[ix] = xrep[ix]

    cox_copy = pltpu.make_async_copy(cox, cox_hbm, sem_co.at[4])

    def x_split():
        for c in xr_copies():
            c.wait_recv()
        for g in range(4):
            for h in range(2):
                g0, g1, g2, gt = [xback[g, f, :, half(h)] for f in range(4)]
                suffix = None
                for s in reversed(range(NSEG)):
                    rows = pl.ds(g * 64 + s, 8, stride=NSEG)
                    seg = tuple(xc[i, h, rows, :] for i in range(4))
                    suffix = seg if suffix is None else compose(seg, suffix)
                    xsuf[s] = g0 * suffix[0] + g1 * suffix[1] + g2 * suffix[2] + gt * suffix[3]
                front = jnp.ones((8, LANE), F32)
                for s in range(NSEG):
                    rows = pl.ds(g * 64 + s, 8, stride=NSEG)
                    cox[0, h, rows, :] = front * g0
                    cox[1, h, rows, :] = front * g1
                    cox[2, h, rows, :] = front * g2
                    cox[3, h, rows, :] = front * xsuf[s] * (-step_x)
                    front = front * xc[3, h, rows, :]
        cox_copy.start()

    def scatter(sq, ids):
        owner = jnp.zeros((8, LANE), jnp.int32)
        for s, o in enumerate(ids):
            owner = jnp.where(sub == s, o, owner)
        return jnp.where(lane == owner, jnp.sum(sq, axis=1, keepdims=True), 0.0)

    def ez_copies():
        return [remote(ez.at[7], ez.at[d - 1], sem_ez.at[d - 1], row[d - 1]) for d in range(1, 8)]

    def ex_copies():
        return [remote(ex.at[3], ex.at[d - 1], sem_ex.at[d - 1], slabs[d - 1]) for d in (1, 2, 3)]

    def ey_copies():
        return [remote(ey.at[3], ey.at[d - 1], sem_ey.at[d - 1], column[d - 1]) for d in (1, 2, 3)]

    def err_start():
        total = jnp.zeros((8, LANE), F32)
        for k in range(2):
            for i in range(2):
                cell = k * HALF + core * 8 + chip * 2 + i
                total = total + scatter(err[k * 2 + i], [ix * 32 + ozb[0, s * SEG + cell] for s in range(NSEG)])
        ez[7] = total
        ex[3] = scatter(err[4], [oxb[0, ix * 8 + s] * 8 + iz for s in range(8)])
        for c in ez_copies() + ex_copies():
            c.start()

    def err_middle():
        for c in ez_copies() + ex_copies():
            c.wait_recv()
        total = ez[7] + ex[3]
        for d in range(7):
            total = total + ez[d]
        for d in range(3):
            total = total + ex[d]
        ey[3] = total
        for c in ey_copies():
            c.start()

    def err_finish():
        for c in ey_copies():
            c.wait_recv()
        total = ey[0] + ey[1] + ey[2] + ey[3]
        mine = jnp.where(lane == ix * 32 + iy * 8 + iz, total, 0.0)
        owned[0, 0] = jnp.sum(mine) * share

    for i in range(3):
        xc[i] = jnp.zeros_like(xc[i])
    xc[3] = jnp.ones_like(xc[3])

    def clear(m, _):
        for f in range(4):
            zc[m, f] = jnp.full((8, 256), float(f == 3), F32)
        return 0

    lax.fori_loop(0, SEG, clear, 0)
    tab_copy.wait()
    load.wait(0)
    for part in range(2):
        upsample_part(ebuf, sbuf, 0, tab, fine0, part)

    def pair_of_steps(i, _):
        t = i * 2
        load.wait(t + 1)

        @pl.when(t + 2 < STEPS)
        def _():
            load.wait(t + 2)

        for b, (fine, ahead) in enumerate(((fine0, fine1), (fine1, fine0))):
            forward_scan(
                fine, zc, xc, t // NZG, t % NZG + b,
                lambda part: upsample_part(ebuf, sbuf, t + b + 1, tab, ahead, part),
            )

        @pl.when(i == 3)
        def _():
            pl.semaphore_wait(barrier, 13)
            sib_copy(0).start()

        @pl.when(i == 4)
        def _():
            z_compose(0)

        return 0

    lax.fori_loop(0, STEPS // 2, pair_of_steps, 0)
    sib_copy(1).start()
    x_compose()
    for c in late:
        c.wait()

    def widen(c, _):
        r = jnp.dot(tzb[c], perm[...], preferred_element_type=F32)
        for h in range(2):
            for s in range(NSEG):
                tzf[c, h, pl.ds(s * (SEG + 4), SEG), :] = r[s * SEG : (s + 1) * SEG, half(h)]
        txf[c] = jnp.dot(txb[c], perm[...], preferred_element_type=F32)
        return 0

    lax.fori_loop(0, 3, widen, 0)
    z_merge(0)
    z_compose(1)
    x_merge()
    z_split(0)
    z_merge(1)
    err_start()
    x_split()
    z_finish(0)
    z_split(1)
    err_middle()
    z_finish(1)
    err_finish()
    for k in range(2):
        for c in [sib_copy(k)] + chip_copies(k) + rep_copies(k) + [fin_copy(k)]:
            c.wait_send()
    for c in x_copies() + xr_copies() + ez_copies() + ex_copies() + ey_copies():
        c.wait_send()
    for c in out_copies(0) + out_copies(1) + (cox_copy,):
        c.wait()


def project_down(even, odd, third):
    return even + third * odd + pltpu.roll(odd + third * even, LANE - 1, axis=1)


def backward_scan(fine, zcar, xcar, coz, cox, coarse, k, zg, pair, third):
    planes = [pair * 2 + i for i in range(2)]
    rows = [pl.ds(pl.multiple_of((zg * ZG + z) * NSEG, NSEG), NSEG) for z in planes]
    carry = [[[xcar[i, h, r, :] for i in range(2)] for h in range(2)] for r in rows]
    gx = [[[cox[c, h, r, :] for c in range(3)] for h in range(2)] for r in rows]
    for xm in range(HALF):
        zr = k * HALF + xm
        z_carry = [[zcar[i, zr, :, half(h)] for i in range(2)] for h in range(2)]
        gz = [[coz[zr, c, :, half(h)] for c in range(3)] for h in range(2)]
        for n, z in enumerate(planes):
            out = [[None] * 2 for _ in range(4)]
            for h in range(2):
                e0, e1, e2, sg = [fine[f, z, h, pl.ds(xm, NSEG, stride=PITCH), :] for f in range(4)]
                g0, g1, g2 = gz[h]
                t_z, a_z = z_carry[h]
                t_new = t_z * jnp.exp2(sg)
                share_z = t_z - t_new
                inner = g0 * e0 + g1 * e1 + g2 * e2
                a_z = a_z + share_z * inner
                grad = t_new * inner + a_z
                z_carry[h] = [t_new, a_z]
                h0, h1, h2 = gx[n][h]
                t_x, a_x = carry[n][h]
                t_new = t_x * jnp.exp2(sg * 0.25)
                share_x = t_x - t_new
                q0, q1, q2 = [cox[4 + c, h, rows[n], :] for c in range(3)]
                inner = q0 * e0 + q1 * e1 + q2 * e2
                a_x = a_x + share_x * inner
                out[3][h] = (grad + a_x) + t_new * inner
                carry[n][h] = [t_new, a_x]
                out[0][h] = g0 * share_z + h0 * share_x
                out[1][h] = g1 * share_z + h1 * share_x
                out[2][h] = g2 * share_z + h2 * share_x
            for f in range(4):
                coarse[f, z, pl.ds(xm, NSEG, stride=PITCH), :] = project_down(out[f][0], out[f][1], third)
        for h in range(2):
            for i in range(2):
                zcar[i, zr, :, half(h)] = z_carry[h][i]
    for n, r in enumerate(rows):
        for h in range(2):
            for i in range(2):
                xcar[i, h, r, :] = carry[n][h][i]


def narrow_part(coarse, eout, sout, t, part):
    for z in (2 * part, 2 * part + 1):
        for f in range(4):
            for s in range(NSEG):
                v = coarse[f, z, pl.ds(s * PITCH, HALF), :].astype(BF16)
                if f == 3:
                    sout[t, z, s] = v
                else:
                    eout[t, f, z, s] = v


def backward_kernel(
    e_hbm, s_hbm, tab_hbm, coz_hbm, cox_hbm,
    ge_hbm, gs_hbm,
    ebuf, sbuf, fine0, fine1, tab, coarse0, coarse1,
    eout, sout, zcar, xcar, coz, cox,
    in_sem, out_sem, co_sem,
):
    tab_copy = pltpu.make_async_copy(tab_hbm, tab, co_sem.at[0])
    coz_copy = pltpu.make_async_copy(coz_hbm, coz, co_sem.at[1])
    cox_copy = pltpu.make_async_copy(cox_hbm, cox.at[pl.ds(0, 4)], co_sem.at[2])
    tab_copy.start()
    load = Loader(e_hbm, s_hbm, ebuf, sbuf, in_sem)
    for c in load.copies(0):
        c.start()
    coz_copy.start()
    cox_copy.start()

    def rest(t, _):
        for c in load.copies(t):
            c.start()
        return 0

    lax.fori_loop(1, STEPS, rest, 0)

    def stores(t):
        k, zg = t // NZG, t % NZG
        zr, xr = pl.ds(zg * ZG, ZG), pl.ds(pl.multiple_of(k * HALF, HALF), HALF)
        return (
            pltpu.make_async_copy(eout.at[t], ge_hbm.at[:, zr, :, xr, :], out_sem.at[t, 0]),
            pltpu.make_async_copy(sout.at[t], gs_hbm.at[zr, :, xr, :], out_sem.at[t, 1]),
        )

    def store(t):
        for c in stores(t):
            c.start()

    zcar[0] = jnp.ones_like(zcar[0])
    xcar[0] = jnp.ones_like(xcar[0])
    third = jnp.where(lax.broadcasted_iota(jnp.int32, (NSEG, LANE), 1) == 0, 0.0, 1.0 / 3.0)
    tab_copy.wait()
    load.wait(0)
    for part in range(2):
        upsample_part(ebuf, sbuf, 0, tab, fine0, part)
    coz_copy.wait()
    cox_copy.wait()
    zcar[1] = coz[:, 3]
    xcar[1] = cox[3]
    for c in range(3):
        cox[4 + c] = 0.25 * cox[c]

    def pair_of_steps(i, _):
        t = i * 2
        load.wait(t + 1)

        @pl.when(t + 2 < STEPS)
        def _():
            load.wait(t + 2)

        for b, (fine, ahead, new, old) in enumerate(((fine0, fine1, coarse0, coarse1), (fine1, fine0, coarse1, coarse0))):
            before = lax.rem(t + b + STEPS, STEPS + 1)
            for part in range(2):
                upsample_part(ebuf, sbuf, t + b + 1, tab, ahead, part)
                narrow_part(old, eout, sout, before, part)
                backward_scan(fine, zcar, xcar, coz, cox, new, t // NZG, t % NZG + b, part, third)

        @pl.when(i > 0)
        def _():
            store(t - 1)

        store(t)
        return 0

    lax.fori_loop(0, STEPS // 2, pair_of_steps, 0)
    for part in range(2):
        narrow_part(coarse1, eout, sout, STEPS - 1, part)
    store(STEPS - 1)

    def finish(t, _):
        for c in stores(t):
            c.wait()
        return 0

    lax.fori_loop(0, STEPS, finish, 0)


def vmem(*shape, dtype=F32):
    return pltpu.VMEM(shape, dtype)


HBM = pl.BlockSpec(memory_space=pltpu.HBM)


def local(emission, absorption, target_z, target_x, owner_z, owner_x):
    depth_z, width_x, width_y = absorption.shape
    pixels = 2 * width_y
    count_x = lax.axis_size("gx")
    count_y = lax.axis_size("gy")
    count_z = lax.axis_size("gz")
    step_z = OPTICAL / (depth_z * count_z)
    step_x = OPTICAL / (width_x * count_x)
    interp = interp_table(width_y)
    rate = interp.T * (-step_z * math.log2(math.e))
    order = np.concatenate([np.arange(0, pixels, 2), np.roll(np.arange(1, pixels, 2), 1)])
    rate_hi = rate.astype(BF16)
    rate_lo = (rate - rate_hi.astype(np.float64)).astype(BF16)
    tab = np.concatenate([interp.T.astype(BF16), rate_hi, rate_lo], axis=0)[:, order]
    tab_back = np.concatenate([(interp.T * step_z).astype(BF16), rate_hi, rate_lo], axis=0)[:, order]
    perm = np.eye(pixels)[:, order].astype(BF16)
    slots = 2 * width_x // (count_y * count_z) + 2 * depth_z // (count_x * count_y)
    e5 = emission.reshape(3, depth_z, NSEG, SEG, width_y)
    s4 = absorption.reshape(depth_z, NSEG, SEG, width_y)

    buffers = [
        vmem(STEPS + 1, 3, ZG, NSEG, HALF, LANE, dtype=BF16), vmem(STEPS + 1, ZG, NSEG, HALF, LANE, dtype=BF16),
        vmem(4, ZG, 2, NSEG * PITCH, LANE), vmem(4, ZG, 2, NSEG * PITCH, LANE),
    ]
    dma = pltpu.SemaphoreType.DMA
    coz, cox, owned = pl.pallas_call(
        functools.partial(forward_kernel, step_z, step_x, 1.0 / (3.0 * pixels * slots)),
        out_shape=[
            jax.ShapeDtypeStruct((SEG, 4, NSEG, 256), F32),
            jax.ShapeDtypeStruct((4, 2, NZ * NSEG, LANE), F32),
            jax.ShapeDtypeStruct((1, 1), F32),
        ],
        in_specs=[HBM] * 8,
        out_specs=[HBM, HBM, pl.BlockSpec(memory_space=pltpu.SMEM)],
        scratch_shapes=buffers + [
            vmem(SEG, 4, NSEG, 256), vmem(4, 2, NZ * NSEG, LANE), vmem(SEG, 4, NSEG, 256), vmem(4, 2, NZ * NSEG, LANE),
            vmem(3, 256, 256, dtype=BF16), vmem(3, NZ, 256, dtype=BF16),
            vmem(3, 2, NSEG * (SEG + 4), LANE), vmem(3, NZ, 256),
            vmem(2, 8, 4, 8, 256), vmem(2, 8, 4, 8, 256), vmem(2, 4, 2, 4, 8, 256), vmem(2, 4, 2, 4, 8, 256),
            vmem(2, 8, 4, 8, 256), vmem(2, 8, 4, 8, 256), vmem(2, 8, 4, 8, 256),
            vmem(4, 4, 8, 256), vmem(4, 4, 8, 256), vmem(4, 4, 8, 256), vmem(4, 4, 8, 256), vmem(NSEG, 8, LANE),
            vmem(3 * LANE, 256, dtype=BF16), vmem(256, 256, dtype=BF16), vmem(5, 8, LANE),
            pltpu.SMEM((1, 256), jnp.int32), pltpu.SMEM((1, NZ), jnp.int32),
            vmem(8, 8, LANE), vmem(4, 8, LANE), vmem(4, 8, LANE),
            dma((STEPS, 2)), dma((6,)), dma((2, 2)), dma((2, 3, 2)), dma((2, 3, 2)), dma((2, 2)), dma((3, 2)), dma((3, 2)),
            dma((7, 2)), dma((3, 2)), dma((3, 2)), dma((5,)),
        ],
        compiler_params=pltpu.CompilerParams(
            collective_id=0, has_side_effects=True, vmem_limit_bytes=VMEM_LIMIT
        ),
    )(
        e5, s4, target_z, target_x, owner_z.reshape(count_x, count_y, 1, width_x),
        owner_x.reshape(count_y, count_z, 1, depth_z), tab, perm,
    )

    grad_e, grad_s = pl.pallas_call(
        backward_kernel,
        out_shape=[jax.ShapeDtypeStruct(e5.shape, BF16), jax.ShapeDtypeStruct(s4.shape, BF16)],
        in_specs=[HBM] * 5,
        out_specs=[HBM, HBM],
        scratch_shapes=buffers + [
            vmem(3 * LANE, 256, dtype=BF16), vmem(4, ZG, NSEG * PITCH, LANE), vmem(4, ZG, NSEG * PITCH, LANE),
            vmem(STEPS + 1, 3, ZG, NSEG, HALF, LANE, dtype=BF16), vmem(STEPS + 1, ZG, NSEG, HALF, LANE, dtype=BF16),
            vmem(2, SEG, NSEG, 256), vmem(2, 2, NZ * NSEG, LANE), vmem(SEG, 4, NSEG, 256), vmem(7, 2, NZ * NSEG, LANE),
            dma((STEPS, 2)), dma((STEPS, 2)), dma((3,)),
        ],
        compiler_params=pltpu.CompilerParams(vmem_limit_bytes=VMEM_LIMIT),
        cost_estimate=pl.CostEstimate(flops=6 * 10**9, bytes_accessed=20 * 2**20, transcendentals=0),
    )(e5, s4, tab_back, coz, cox)
    return (grad_e.reshape(emission.shape), grad_s.reshape(absorption.shape), owned.reshape(1, 1, 1))


def solution(mesh):
    return jax.shard_map(
        local,
        mesh=mesh,
        in_specs=(P(None, "gz", "gx", "gy"), P("gz", "gx", "gy"), P(), P(), P(), P()),
        out_specs=(P(None, "gz", "gx", "gy"), P("gz", "gx", "gy"), P("gx", "gy", "gz")),
        check_vma=False,
    )
```

```python
import functools
import math

import jax
import jax.numpy as jnp
import numpy as np
from jax import lax
from jax.experimental import pallas as pl
from jax.experimental.pallas import tpu as pltpu
from jax.sharding import PartitionSpec as P

F32 = jnp.float32
BF16 = jnp.bfloat16
OPTICAL = 1.5
BACKLIGHT = 1.0

NSEG = 8
SEG = 32
HALF = 16
PITCH = 20
ZG = 4
NZ = 32
NZG = NZ // ZG
STEPS = 2 * NZG
LANE = 128
VMEM_LIMIT = 61 * 2**20 + 2**19


def interp_table(width):
    pixels = np.arange(2 * width)
    nearest = pixels // 2
    second = np.clip(nearest + 2 * (pixels % 2) - 1, 0, width - 1)
    columns = np.arange(width)
    return 0.75 * (columns[None, :] == nearest[:, None]) + 0.25 * (columns[None, :] == second[:, None])


def half(h):
    return slice(h * LANE, (h + 1) * LANE)


def upsample_store(fine, f, z, r):
    for s in range(NSEG):
        for h in range(2):
            fine[f, z, h, s * PITCH : s * PITCH + HALF] = r[s * HALF : (s + 1) * HALF, half(h)]


def upsample_part(ebuf, sbuf, t, tab, fine, part):
    rows = NSEG * HALF
    if part == 0:
        a = ebuf[t, 0:2].reshape(2 * ZG * rows, LANE)
        r = jnp.dot(a, tab[0:LANE], preferred_element_type=F32)
        for f in range(2):
            for z in range(ZG):
                i = f * ZG + z
                upsample_store(fine, f, z, r[i * rows : (i + 1) * rows])
    else:
        r = jnp.dot(ebuf[t, 2].reshape(ZG * rows, LANE), tab[0:LANE], preferred_element_type=F32)
        s = sbuf[t].reshape(ZG * rows, LANE)
        q = jnp.dot(jnp.concatenate([s, s], axis=1), tab[LANE:], preferred_element_type=F32)
        for z in range(ZG):
            upsample_store(fine, 2, z, r[z * rows : (z + 1) * rows])
            upsample_store(fine, 3, z, q[z * rows : (z + 1) * rows])


class Loader:
    def __init__(self, e_hbm, s_hbm, ebuf, sbuf, sems, base):
        self.refs = (e_hbm, s_hbm, ebuf, sbuf, sems)
        self.base = base

    def copies(self, t):
        e_hbm, s_hbm, ebuf, sbuf, sems = self.refs
        k, zg = (self.base + t) // NZG, (self.base + t) % NZG
        zs, xs = pl.ds(zg * ZG, ZG), pl.ds(pl.multiple_of(k * HALF, HALF), HALF)
        return (
            pltpu.make_async_copy(e_hbm.at[:, zs, :, xs, :], ebuf.at[t], sems.at[t, 0]),
            pltpu.make_async_copy(s_hbm.at[zs, :, xs, :], sbuf.at[t], sems.at[t, 1]),
        )

    def start(self, first, end):
        def one(t, _):
            for c in self.copies(t):
                c.start()
            return 0

        lax.fori_loop(first, end, one, 0)

    def wait(self, t):
        for c in self.copies(t):
            c.wait()


def forward_scan(fine, zc, xc, k, zg, extra):
    for h in range(2):
        hs = half(h)
        rows = [pl.ds(pl.multiple_of((zg * ZG + z) * NSEG, NSEG), NSEG) for z in range(ZG)]
        carry = [[xc[i, h, r, :] for i in range(4)] for r in rows]
        extra(h)
        for xm in range(HALF):
            zr = k * HALF + xm
            c0, c1, c2, t_z = [zc[zr, i, :, hs] for i in range(4)]
            for z in range(ZG):
                e0, e1, e2, sg = [fine[f, z, h, pl.ds(xm, NSEG, stride=PITCH), :] for f in range(4)]
                t_new = t_z * jnp.exp2(sg)
                share = t_z - t_new
                t_z = t_new
                c0 = c0 + share * e0
                c1 = c1 + share * e1
                c2 = c2 + share * e2
                d0, d1, d2, t_x = carry[z]
                t_new = t_x * jnp.exp2(sg * 0.25)
                share = t_x - t_new
                carry[z] = [d0 + share * e0, d1 + share * e1, d2 + share * e2, t_new]
            for i, v in enumerate((c0, c1, c2, t_z)):
                zc[zr, i, :, hs] = v
        for z in range(ZG):
            for i in range(4):
                xc[i, h, rows[z], :] = carry[z][i]


def compose(front, back):
    c0, c1, c2, t = front
    d0, d1, d2, u = back
    return (c0 + t * d0, c1 + t * d1, c2 + t * d2, t * u)


def merge(bricks, target, inv_step):
    ahead = (jnp.zeros_like(target[0]),) * 3 + (jnp.ones_like(target[0]),)
    fronts = []
    for brick in bricks:
        fronts.append(ahead[3])
        ahead = compose(ahead, brick)
    resid = [ahead[c] + ahead[3] * BACKLIGHT - target[c] for c in range(3)]
    g = [r * inv_step for r in resid]
    behind = [jnp.full_like(target[0], BACKLIGHT)] * 3
    replies = []
    for front, brick in reversed(list(zip(fronts, bricks))):
        dot = g[0] * behind[0] + g[1] * behind[1] + g[2] * behind[2]
        replies.append([front * g[0], front * g[1], front * g[2], front * dot])
        behind = [brick[c] + brick[3] * behind[c] for c in range(3)]
    replies.reverse()
    return replies, resid[0] * resid[0] + resid[1] * resid[1] + resid[2] * resid[2]


def forward_kernel(
    step_z, step_x, share,
    e_hbm, s_hbm, tz_hbm, tx_hbm, oz_hbm, ox_hbm, tab_hbm, perm_hbm, back_hbm,
    coz_hbm, cox_hbm, xst_hbm, ge0_hbm, gs0_hbm, owned,
    ebuf, sbuf, fine0, fine1, zc, xc, coz, cox,
    tab_back, coarse0, coarse1, eout, sout, zcar, xcar,
    tzb, txb, tzf, txf,
    sib, pc, got, rep, back, fin, finr,
    xloc, xgot, xrep, xback, xsuf,
    tab, perm, err, ozb, oxb, ez, ex, ey,
    in_sem, t_sem, sem_sib, sem_chip, sem_rep, sem_fin, sem_x, sem_xr, sem_ez, sem_ex, sem_ey, sem_co, sem_out, sem_xst,
):
    ix, iy, iz = lax.axis_index("gx"), lax.axis_index("gy"), lax.axis_index("gz")
    chip, core = iz // 2, iz % 2
    load = Loader(e_hbm, s_hbm, ebuf, sbuf, in_sem, 0)
    load.start(0, STEPS)
    lane = lax.broadcasted_iota(jnp.int32, (8, LANE), 1)
    sub = lax.broadcasted_iota(jnp.int32, (8, LANE), 0)
    weight = jnp.where(lane == 0, 1.0, 0.75)
    px = pl.ds(pl.multiple_of(iy * 256, 256), 256)
    tz_copy = pltpu.make_async_copy(tz_hbm.at[:, pl.ds(pl.multiple_of(ix * 256, 256), 256), px], tzb, t_sem.at[0])
    tx_copy = pltpu.make_async_copy(tx_hbm.at[:, pl.ds(pl.multiple_of(iz * NZ, NZ), NZ), px], txb, t_sem.at[1])
    oz_copy = pltpu.make_async_copy(oz_hbm.at[ix, iy], ozb, t_sem.at[2])
    ox_copy = pltpu.make_async_copy(ox_hbm.at[iy, iz], oxb, t_sem.at[3])
    tab_copy = pltpu.make_async_copy(tab_hbm, tab, t_sem.at[4])
    perm_copy = pltpu.make_async_copy(perm_hbm, perm, t_sem.at[5])
    back_copy = pltpu.make_async_copy(back_hbm, tab_back, t_sem.at[6])
    tab_copy.start()
    late = (tz_copy, tx_copy, oz_copy, ox_copy, perm_copy, back_copy)
    for c in late:
        c.start()

    sibling = {"gz": chip * 2 + 1 - core}
    chips = [{"gz": lax.rem(chip + d, 4) * 2 + core} for d in (1, 2, 3)]
    slabs = [{"gx": lax.rem(ix + d, 4)} for d in (1, 2, 3)]
    barrier = pltpu.get_barrier_semaphore()
    row = [{"gz": lax.rem(iz + d, 8)} for d in range(1, 8)]
    column = [{"gy": lax.rem(iy + d, 4)} for d in (1, 2, 3)]
    for peer in row + slabs + column:
        pl.semaphore_signal(barrier, inc=1, device_id=peer, device_id_type=pl.DeviceIdType.MESH)

    def remote(src, dst, sems, peer):
        return pltpu.make_async_remote_copy(
            src_ref=src, dst_ref=dst, send_sem=sems.at[0], recv_sem=sems.at[1],
            device_id=peer, device_id_type=pl.DeviceIdType.MESH,
        )

    def sib_copy(k):
        return remote(zc.at[pl.ds(k * HALF + (1 - core) * 8, 8)], sib.at[k], sem_sib.at[k], sibling)

    def chip_copies(k):
        return [
            remote(pc.at[k, pl.ds(lax.rem(chip + d, 4) * 2, 2)], got.at[k, chip], sem_chip.at[k, d - 1], chips[d - 1])
            for d in (1, 2, 3)
        ]

    def rep_copies(k):
        return [
            remote(rep.at[k, lax.rem(chip + d, 4)], back.at[k, pl.ds(chip * 2, 2)], sem_rep.at[k, d - 1], chips[d - 1])
            for d in (1, 2, 3)
        ]

    def fin_copy(k):
        return remote(fin.at[k], finr.at[k], sem_fin.at[k], sibling)

    def x_copies():
        return [remote(xloc.at[lax.rem(ix + d, 4)], xgot.at[ix], sem_x.at[d - 1], slabs[d - 1]) for d in (1, 2, 3)]

    def xr_copies():
        return [remote(xrep.at[lax.rem(ix + d, 4)], xback.at[ix], sem_xr.at[d - 1], slabs[d - 1]) for d in (1, 2, 3)]

    def pair(k, m, hs):
        mine = [zc[k * HALF + core * 8 + m, i, :, hs] for i in range(4)]
        other = [sib[k, m, i, :, hs] for i in range(4)]
        first = core == 0
        return [jnp.where(first, a, b) for a, b in zip(mine, other)], [jnp.where(first, b, a) for a, b in zip(mine, other)]

    def z_compose(k):
        sib_copy(k).wait_recv()

        def body(m, _):
            for h in range(2):
                front, rear = pair(k, m, half(h))
                for i, v in enumerate(compose(front, rear)):
                    pc[k, m, i, :, half(h)] = v
            return 0

        lax.fori_loop(0, 8, body, 0)
        for c in chip_copies(k):
            c.start()

    def z_merge(k):
        for c in chip_copies(k):
            c.wait_recv()
        for i in range(2):
            m = chip * 2 + i
            got[k, chip, i] = pc[k, m]
            sq = jnp.zeros((8, LANE), F32)
            for h in range(2):
                bricks = [[got[k, o, i, f, :, half(h)] for f in range(4)] for o in range(4)]
                row = k * HALF + core * 8 + m
                target = [tzf[c, h, pl.ds(row, NSEG, stride=SEG + 4), :] for c in range(3)]
                replies, s = merge(bricks, target, weight * (1.0 / step_z))
                sq = sq + s
                for o in range(4):
                    for f in range(4):
                        rep[k, o, i, f, :, half(h)] = replies[o][f]
            err[k * 2 + i] = sq
        for c in rep_copies(k):
            c.start()
        back[k, pl.ds(chip * 2, 2)] = rep[k, chip]

    def z_split(k):
        for c in rep_copies(k):
            c.wait_recv()

        def body(m, _):
            for h in range(2):
                hs = half(h)
                a, b = pair(k, m, hs)
                g0, g1, g2, gt = [back[k, m, f, :, hs] for f in range(4)]
                inner_b = g0 * b[0] + g1 * b[1] + g2 * b[2] + gt * b[3]
                k_b = -(a[3] * inner_b)
                k_a = k_b - (g0 * a[0] + g1 * a[1] + g2 * a[2])
                part_a = (g0, g1, g2, k_a * step_z)
                part_b = (a[3] * g0, a[3] * g1, a[3] * g2, k_b * step_z)
                first = core == 0
                for f in range(4):
                    coz[k, core * 8 + m, f, :, hs] = jnp.where(first, part_a[f], part_b[f])
                    fin[k, m, f, :, hs] = jnp.where(first, part_b[f], part_a[f])
            return 0

        lax.fori_loop(0, 8, body, 0)
        fin_copy(k).start()

    mine, other = pl.ds(core * 8, 8), pl.ds((1 - core) * 8, 8)
    mine_copy = pltpu.make_async_copy(coz.at[1, mine], coz_hbm.at[mine], sem_co.at[0])
    other_copy = pltpu.make_async_copy(finr.at[1], coz_hbm.at[other], sem_co.at[1])

    def x_compose():
        for g in range(4):
            for h in range(2):
                acc = None
                for s in range(NSEG):
                    rows = pl.ds(g * 64 + s, 8, stride=NSEG)
                    seg = tuple(xc[i, h, rows, :] for i in range(4))
                    acc = seg if acc is None else compose(acc, seg)
                for f in range(4):
                    xloc[g, f, :, half(h)] = acc[f]
        for c in x_copies():
            c.start()

    def x_merge():
        for c in x_copies():
            c.wait_recv()
        xgot[ix] = xloc[ix]
        sq = jnp.zeros((8, LANE), F32)
        for h in range(2):
            bricks = [[xgot[o, f, :, half(h)] for f in range(4)] for o in range(4)]
            target = [txf[c, pl.ds(pl.multiple_of(ix * 8, 8), 8), half(h)] for c in range(3)]
            replies, s = merge(bricks, target, weight * (1.0 / step_x))
            sq = sq + s
            for o in range(4):
                for f in range(4):
                    xrep[o, f, :, half(h)] = replies[o][f]
        err[4] = sq
        for c in xr_copies():
            c.start()
        xback[ix] = xrep[ix]

    cox_copy = pltpu.make_async_copy(cox, cox_hbm, sem_co.at[2])

    def x_split():
        for c in xr_copies():
            c.wait_recv()
        for g in range(4):
            for h in range(2):
                g0, g1, g2, gt = [xback[g, f, :, half(h)] for f in range(4)]
                suffix = None
                for s in reversed(range(NSEG)):
                    rows = pl.ds(g * 64 + s, 8, stride=NSEG)
                    seg = tuple(xc[i, h, rows, :] for i in range(4))
                    suffix = seg if suffix is None else compose(seg, suffix)
                    xsuf[s] = g0 * suffix[0] + g1 * suffix[1] + g2 * suffix[2] + gt * suffix[3]
                front = jnp.ones((8, LANE), F32)
                for s in range(NSEG):
                    rows = pl.ds(g * 64 + s, 8, stride=NSEG)
                    cox[0, h, rows, :] = front * g0
                    cox[1, h, rows, :] = front * g1
                    cox[2, h, rows, :] = front * g2
                    cox[3, h, rows, :] = front * xsuf[s] * (-step_x)
                    for c in range(3):
                        cox[4 + c, h, rows, :] = 0.25 * cox[c, h, rows, :]
                    front = front * xc[3, h, rows, :]
        cox_copy.start()

    def scatter(sq, ids):
        owner = jnp.zeros((8, LANE), jnp.int32)
        for s, o in enumerate(ids):
            owner = jnp.where(sub == s, o, owner)
        return jnp.where(lane == owner, jnp.sum(sq, axis=1, keepdims=True), 0.0)

    def ez_copies():
        return [remote(ez.at[7], ez.at[d - 1], sem_ez.at[d - 1], row[d - 1]) for d in range(1, 8)]

    def ex_copies():
        return [remote(ex.at[3], ex.at[d - 1], sem_ex.at[d - 1], slabs[d - 1]) for d in (1, 2, 3)]

    def ey_copies():
        return [remote(ey.at[3], ey.at[d - 1], sem_ey.at[d - 1], column[d - 1]) for d in (1, 2, 3)]

    def err_start():
        total = jnp.zeros((8, LANE), F32)
        for k in range(2):
            for i in range(2):
                cell = k * HALF + core * 8 + chip * 2 + i
                total = total + scatter(err[k * 2 + i], [ix * 32 + ozb[0, s * SEG + cell] for s in range(NSEG)])
        ez[7] = total
        ex[3] = scatter(err[4], [oxb[0, ix * 8 + s] * 8 + iz for s in range(8)])
        for c in ez_copies() + ex_copies():
            c.start()

    def err_middle():
        for c in ez_copies() + ex_copies():
            c.wait_recv()
        total = ez[7] + ex[3]
        for d in range(7):
            total = total + ez[d]
        for d in range(3):
            total = total + ex[d]
        ey[3] = total
        for c in ey_copies():
            c.start()

    def err_finish():
        for c in ey_copies():
            c.wait_recv()
        total = ey[0] + ey[1] + ey[2] + ey[3]
        mine = jnp.where(lane == ix * 32 + iy * 8 + iz, total, 0.0)
        owned[0, 0] = jnp.sum(mine) * share

    for i in range(3):
        xc[i] = jnp.zeros_like(xc[i])
    xc[3] = jnp.ones_like(xc[3])

    def clear(m, _):
        for f in range(4):
            zc[m, f] = jnp.full((8, 256), float(f == 3), F32)
        return 0

    lax.fori_loop(0, SEG, clear, 0)
    tab_copy.wait()
    load.wait(0)
    for part in range(2):
        upsample_part(ebuf, sbuf, 0, tab, fine0, part)

    def pair_of_steps(i, _):
        for b, (fine, ahead) in enumerate(((fine0, fine1), (fine1, fine0))):
            t = i * 2 + b

            @pl.when(t + 1 < STEPS)
            def _():
                load.wait(t + 1)

            forward_scan(
                fine, zc, xc, t // NZG, t % NZG,
                lambda part: upsample_part(ebuf, sbuf, t + 1, tab, ahead, part),
            )

        @pl.when(i == 3)
        def _():
            pl.semaphore_wait(barrier, 13)
            sib_copy(0).start()

        @pl.when(i == 4)
        def _():
            z_compose(0)

        return 0

    lax.fori_loop(0, STEPS // 2, pair_of_steps, 0)
    sib_copy(1).start()
    x_compose()
    for c in late:
        c.wait()

    def widen(c, _):
        r = jnp.dot(tzb[c], perm[...], preferred_element_type=F32)
        for h in range(2):
            for s in range(NSEG):
                tzf[c, h, pl.ds(s * (SEG + 4), SEG), :] = r[s * SEG : (s + 1) * SEG, half(h)]
        txf[c] = jnp.dot(txb[c], perm[...], preferred_element_type=F32)
        return 0

    lax.fori_loop(0, 3, widen, 0)
    z_merge(0)
    z_compose(1)
    for part in range(2):
        upsample_part(ebuf, sbuf, 0, tab_back, fine0, part)
    zcar[0] = jnp.ones_like(zcar[0])
    xcar[0] = jnp.ones_like(xcar[0])
    x_merge()
    z_split(0)
    z_merge(1)
    err_start()
    x_split()
    xcar[1] = cox[3]
    fin_copy(0).wait_recv()
    coz[0, other] = finr[0]
    zcar[1] = coz[0, :, 3]

    def stores(t):
        return store_copies(eout, sout, ge0_hbm, gs0_hbm, sem_out, t)

    def store(t):
        for c in stores(t):
            c.start()

    def state_copy(i):
        rows = pl.ds(pl.multiple_of(i * 2 * ZG * NSEG, 2 * ZG * NSEG), 2 * ZG * NSEG)
        return pltpu.make_async_copy(xcar.at[:, :, rows, :], xst_hbm.at[:, :, rows, :], sem_xst.at[i])

    def after(i):
        state_copy(i).start()

        @pl.when(i == 1)
        def _():
            z_split(1)
            mine_copy.start()
            err_middle()

    backward_steps(
        lambda t: None, after, store, ebuf, sbuf, tab_back, (fine0, fine1), (coarse0, coarse1),
        eout, sout, zcar, xcar, coz.at[0], cox,
    )
    fin_copy(1).wait_recv()
    other_copy.start()
    err_finish()
    for k in range(2):
        for c in [sib_copy(k)] + chip_copies(k) + rep_copies(k) + [fin_copy(k)]:
            c.wait_send()
    for c in x_copies() + xr_copies() + ez_copies() + ex_copies() + ey_copies():
        c.wait_send()
    for c in (mine_copy, other_copy, cox_copy):
        c.wait()

    def finish(t, _):
        for c in stores(t):
            c.wait()
        return 0

    lax.fori_loop(0, NZG, finish, 0)
    for i in range(NZG // 2):
        state_copy(i).wait()


def project_down(even, odd, third):
    return even + third * odd + pltpu.roll(odd + third * even, LANE - 1, axis=1)


def backward_scan(fine, zcar, xcar, coz, cox, coarse, zg, pair, third):
    planes = [pair * 2 + i for i in range(2)]
    rows = [pl.ds(pl.multiple_of((zg * ZG + z) * NSEG, NSEG), NSEG) for z in planes]
    carry = [[[xcar[i, h, r, :] for i in range(2)] for h in range(2)] for r in rows]
    gx = [[[cox[c, h, r, :] for c in range(3)] for h in range(2)] for r in rows]
    for xm in range(HALF):
        z_carry = [[zcar[i, xm, :, half(h)] for i in range(2)] for h in range(2)]
        gz = [[coz[xm, c, :, half(h)] for c in range(3)] for h in range(2)]
        for n, z in enumerate(planes):
            out = [[None] * 2 for _ in range(4)]
            for h in range(2):
                e0, e1, e2, sg = [fine[f, z, h, pl.ds(xm, NSEG, stride=PITCH), :] for f in range(4)]
                g0, g1, g2 = gz[h]
                t_z, a_z = z_carry[h]
                t_new = t_z * jnp.exp2(sg)
                share_z = t_z - t_new
                inner = g0 * e0 + g1 * e1 + g2 * e2
                a_z = a_z + share_z * inner
                grad = t_new * inner + a_z
                z_carry[h] = [t_new, a_z]
                h0, h1, h2 = gx[n][h]
                t_x, a_x = carry[n][h]
                t_new = t_x * jnp.exp2(sg * 0.25)
                share_x = t_x - t_new
                q0, q1, q2 = [cox[4 + c, h, rows[n], :] for c in range(3)]
                inner = q0 * e0 + q1 * e1 + q2 * e2
                a_x = a_x + share_x * inner
                out[3][h] = (grad + a_x) + t_new * inner
                carry[n][h] = [t_new, a_x]
                out[0][h] = g0 * share_z + h0 * share_x
                out[1][h] = g1 * share_z + h1 * share_x
                out[2][h] = g2 * share_z + h2 * share_x
            for f in range(4):
                coarse[f, z, pl.ds(xm, NSEG, stride=PITCH), :] = project_down(out[f][0], out[f][1], third)
        for h in range(2):
            for i in range(2):
                zcar[i, xm, :, half(h)] = z_carry[h][i]
    for n, r in enumerate(rows):
        for h in range(2):
            for i in range(2):
                xcar[i, h, r, :] = carry[n][h][i]


def narrow_part(coarse, eout, sout, t, part):
    for z in (2 * part, 2 * part + 1):
        for f in range(4):
            for s in range(NSEG):
                v = coarse[f, z, pl.ds(s * PITCH, HALF), :].astype(BF16)
                if f == 3:
                    sout[t, z, s] = v
                else:
                    eout[t, f, z, s] = v


def lane_third():
    return jnp.where(lax.broadcasted_iota(jnp.int32, (NSEG, LANE), 1) == 0, 0.0, 1.0 / 3.0)


def backward_steps(ahead_wait, after, store, ebuf, sbuf, tab, fines, coarses, eout, sout, zcar, xcar, coz, cox):
    third = lane_third()
    fine0, fine1 = fines
    coarse0, coarse1 = coarses

    def pair_of_steps(i, _):
        for b, (fine, ahead, new, old) in enumerate(((fine0, fine1, coarse0, coarse1), (fine1, fine0, coarse1, coarse0))):
            t = i * 2 + b
            ahead_wait(t + 1)
            for part in range(2):
                upsample_part(ebuf, sbuf, t + 1, tab, ahead, part)
                narrow_part(old, eout, sout, lax.rem(t + NZG, NZG + 1), part)
                backward_scan(fine, zcar, xcar, coz, cox, new, t, part, third)

            @pl.when(t > 0)
            def _():
                store(t - 1)

        after(i)
        return 0

    lax.fori_loop(0, NZG // 2, pair_of_steps, 0)
    for part in range(2):
        narrow_part(coarse1, eout, sout, NZG - 1, part)
    store(NZG - 1)


def store_copies(eout, sout, ge, gs, sems, t):
    zr = pl.ds(t * ZG, ZG)
    return (
        pltpu.make_async_copy(eout.at[t], ge.at[:, zr], sems.at[t, 0]),
        pltpu.make_async_copy(sout.at[t], gs.at[zr], sems.at[t, 1]),
    )


def backward_kernel(
    e_hbm, s_hbm, tab_hbm, coz_hbm, cox_hbm, xst_hbm, ge0_hbm, gs0_hbm,
    ge_hbm, gs_hbm,
    ebuf, sbuf, fine0, fine1, tab, coarse0, coarse1,
    eout, sout, zcar, xcar, coz, cox,
    in_sem, out_sem, co_sem, pass_sem,
):
    load = Loader(e_hbm, s_hbm, ebuf, sbuf, in_sem, NZG)
    tab_copy = pltpu.make_async_copy(tab_hbm, tab, co_sem.at[0])
    handed = (
        pltpu.make_async_copy(coz_hbm, coz, co_sem.at[1]),
        pltpu.make_async_copy(cox_hbm, cox, co_sem.at[2]),
        pltpu.make_async_copy(xst_hbm, xcar, co_sem.at[3]),
    )
    passed = [
        pltpu.make_async_copy(ge0_hbm.at[c], ge_hbm.at[c, :, :, pl.ds(0, HALF), :], pass_sem.at[c]) for c in range(3)
    ] + [pltpu.make_async_copy(gs0_hbm, gs_hbm.at[:, :, pl.ds(0, HALF), :], pass_sem.at[3])]
    tab_copy.start()
    load.start(0, 1)
    for c in handed:
        c.start()
    load.start(1, NZG)
    for c in passed:
        c.start()

    def stores(t):
        xr = pl.ds(HALF, HALF)
        return store_copies(eout, sout, ge_hbm.at[:, :, :, xr, :], gs_hbm.at[:, :, xr, :], out_sem, t)

    def store(t):
        for c in stores(t):
            c.start()

    def ahead_wait(t):
        @pl.when(t < NZG)
        def _():
            load.wait(t)

    zcar[0] = jnp.ones_like(zcar[0])
    tab_copy.wait()
    load.wait(0)
    for part in range(2):
        upsample_part(ebuf, sbuf, 0, tab, fine0, part)
    for c in handed:
        c.wait()
    zcar[1] = coz[:, 3]
    backward_steps(
        ahead_wait, lambda i: None, store, ebuf, sbuf, tab, (fine0, fine1), (coarse0, coarse1),
        eout, sout, zcar, xcar, coz, cox,
    )

    def finish(t, _):
        for c in stores(t):
            c.wait()
        return 0

    lax.fori_loop(0, NZG, finish, 0)
    for c in passed:
        c.wait()


def vmem(*shape, dtype=F32):
    return pltpu.VMEM(shape, dtype)


HBM = pl.BlockSpec(memory_space=pltpu.HBM)


def local(emission, absorption, target_z, target_x, owner_z, owner_x):
    depth_z, width_x, width_y = absorption.shape
    pixels = 2 * width_y
    count_x = lax.axis_size("gx")
    count_y = lax.axis_size("gy")
    count_z = lax.axis_size("gz")
    step_z = OPTICAL / (depth_z * count_z)
    step_x = OPTICAL / (width_x * count_x)
    interp = interp_table(width_y)
    rate = interp.T * (-step_z * math.log2(math.e))
    order = np.concatenate([np.arange(0, pixels, 2), np.roll(np.arange(1, pixels, 2), 1)])
    rate_hi = rate.astype(BF16)
    rate_lo = (rate - rate_hi.astype(np.float64)).astype(BF16)
    tab = np.concatenate([interp.T.astype(BF16), rate_hi, rate_lo], axis=0)[:, order]
    tab_back = np.concatenate([(interp.T * step_z).astype(BF16), rate_hi, rate_lo], axis=0)[:, order]
    perm = np.eye(pixels)[:, order].astype(BF16)
    slots = 2 * width_x // (count_y * count_z) + 2 * depth_z // (count_x * count_y)
    e5 = emission.reshape(3, depth_z, NSEG, SEG, width_y)
    s4 = absorption.reshape(depth_z, NSEG, SEG, width_y)

    def buffers(steps):
        return [
            vmem(steps + 1, 3, ZG, NSEG, HALF, LANE, dtype=BF16), vmem(steps + 1, ZG, NSEG, HALF, LANE, dtype=BF16),
            vmem(4, ZG, 2, NSEG * PITCH, LANE), vmem(4, ZG, 2, NSEG * PITCH, LANE),
        ]

    back_buffers = [
        vmem(3 * LANE, 256, dtype=BF16), vmem(4, ZG, NSEG * PITCH, LANE), vmem(4, ZG, NSEG * PITCH, LANE),
        vmem(NZG + 1, 3, ZG, NSEG, HALF, LANE, dtype=BF16), vmem(NZG + 1, ZG, NSEG, HALF, LANE, dtype=BF16),
        vmem(2, HALF, NSEG, 256), vmem(2, 2, NZ * NSEG, LANE),
    ]
    dma = pltpu.SemaphoreType.DMA
    coz, cox, xst, ge0, gs0, owned = pl.pallas_call(
        functools.partial(forward_kernel, step_z, step_x, 1.0 / (3.0 * pixels * slots)),
        out_shape=[
            jax.ShapeDtypeStruct((HALF, 4, NSEG, 256), F32),
            jax.ShapeDtypeStruct((7, 2, NZ * NSEG, LANE), F32),
            jax.ShapeDtypeStruct((2, 2, NZ * NSEG, LANE), F32),
            jax.ShapeDtypeStruct((3, NZ, NSEG, HALF, LANE), BF16),
            jax.ShapeDtypeStruct((NZ, NSEG, HALF, LANE), BF16),
            jax.ShapeDtypeStruct((1, 1), F32),
        ],
        in_specs=[HBM] * 9,
        out_specs=[HBM] * 5 + [pl.BlockSpec(memory_space=pltpu.SMEM)],
        scratch_shapes=buffers(STEPS) + [
            vmem(SEG, 4, NSEG, 256), vmem(4, 2, NZ * NSEG, LANE), vmem(2, HALF, 4, NSEG, 256), vmem(7, 2, NZ * NSEG, LANE),
        ] + back_buffers + [
            vmem(3, 256, 256, dtype=BF16), vmem(3, NZ, 256, dtype=BF16),
            vmem(3, 2, NSEG * (SEG + 4), LANE), vmem(3, NZ, 256),
            vmem(2, 8, 4, 8, 256), vmem(2, 8, 4, 8, 256), vmem(2, 4, 2, 4, 8, 256), vmem(2, 4, 2, 4, 8, 256),
            vmem(2, 8, 4, 8, 256), vmem(2, 8, 4, 8, 256), vmem(2, 8, 4, 8, 256),
            vmem(4, 4, 8, 256), vmem(4, 4, 8, 256), vmem(4, 4, 8, 256), vmem(4, 4, 8, 256), vmem(NSEG, 8, LANE),
            vmem(3 * LANE, 256, dtype=BF16), vmem(256, 256, dtype=BF16), vmem(5, 8, LANE),
            pltpu.SMEM((1, 256), jnp.int32), pltpu.SMEM((1, NZ), jnp.int32),
            vmem(8, 8, LANE), vmem(4, 8, LANE), vmem(4, 8, LANE),
            dma((STEPS, 2)), dma((7,)), dma((2, 2)), dma((2, 3, 2)), dma((2, 3, 2)), dma((2, 2)), dma((3, 2)), dma((3, 2)),
            dma((7, 2)), dma((3, 2)), dma((3, 2)), dma((3,)), dma((NZG, 2)), dma((NZG // 2,)),
        ],
        compiler_params=pltpu.CompilerParams(
            collective_id=0, has_side_effects=True, vmem_limit_bytes=VMEM_LIMIT
        ),
    )(
        e5, s4, target_z, target_x, owner_z.reshape(count_x, count_y, 1, width_x),
        owner_x.reshape(count_y, count_z, 1, depth_z), tab, perm, tab_back,
    )

    grad_e, grad_s = pl.pallas_call(
        backward_kernel,
        out_shape=[jax.ShapeDtypeStruct(e5.shape, BF16), jax.ShapeDtypeStruct(s4.shape, BF16)],
        in_specs=[HBM] * 8,
        out_specs=[HBM, HBM],
        scratch_shapes=buffers(NZG) + back_buffers + [
            vmem(HALF, 4, NSEG, 256), vmem(7, 2, NZ * NSEG, LANE),
            dma((NZG, 2)), dma((NZG, 2)), dma((4,)), dma((4,)),
        ],
        compiler_params=pltpu.CompilerParams(vmem_limit_bytes=VMEM_LIMIT),
        cost_estimate=pl.CostEstimate(flops=6 * 10**9, bytes_accessed=20 * 2**20, transcendentals=0),
    )(e5, s4, tab_back, coz, cox, xst, ge0, gs0)
    return (grad_e.reshape(emission.shape), grad_s.reshape(absorption.shape), owned.reshape(1, 1, 1))


def solution(mesh):
    return jax.shard_map(
        local,
        mesh=mesh,
        in_specs=(P(None, "gz", "gx", "gy"), P("gz", "gx", "gy"), P(), P(), P(), P()),
        out_specs=(P(None, "gz", "gx", "gy"), P("gz", "gx", "gy"), P("gx", "gy", "gz")),
        check_vma=False,
    )
```

```python
import functools
import math

import jax
import jax.numpy as jnp
import numpy as np
from jax import lax
from jax.experimental import pallas as pl
from jax.experimental.pallas import tpu as pltpu
from jax.sharding import PartitionSpec as P

F32 = jnp.float32
BF16 = jnp.bfloat16
OPTICAL = 1.5
BACKLIGHT = 1.0

NSEG = 8
SEG = 32
HALF = 16
PITCH = 20
ZG = 4
NZ = 32
NZG = NZ // ZG
STEPS = 2 * NZG
LANE = 128
VMEM_LIMIT = 61 * 2**20 + 2**19


def interp_table(width):
    pixels = np.arange(2 * width)
    nearest = pixels // 2
    second = np.clip(nearest + 2 * (pixels % 2) - 1, 0, width - 1)
    columns = np.arange(width)
    return 0.75 * (columns[None, :] == nearest[:, None]) + 0.25 * (columns[None, :] == second[:, None])


def half(h):
    return slice(h * LANE, (h + 1) * LANE)


def upsample_store(fine, f, z, r):
    for s in range(NSEG):
        for h in range(2):
            fine[f, z, h, s * PITCH : s * PITCH + HALF] = r[s * HALF : (s + 1) * HALF, half(h)]


def upsample_part(ebuf, sbuf, t, tab, fine, part):
    rows = NSEG * HALF
    if part == 0:
        a = ebuf[t, 0:2].reshape(2 * ZG * rows, LANE)
        r = jnp.dot(a, tab[0:LANE], preferred_element_type=F32)
        for f in range(2):
            for z in range(ZG):
                i = f * ZG + z
                upsample_store(fine, f, z, r[i * rows : (i + 1) * rows])
    else:
        r = jnp.dot(ebuf[t, 2].reshape(ZG * rows, LANE), tab[0:LANE], preferred_element_type=F32)
        s = sbuf[t].reshape(ZG * rows, LANE)
        q = jnp.dot(jnp.concatenate([s, s], axis=1), tab[LANE:], preferred_element_type=F32)
        for z in range(ZG):
            upsample_store(fine, 2, z, r[z * rows : (z + 1) * rows])
            upsample_store(fine, 3, z, q[z * rows : (z + 1) * rows])


class Loader:
    def __init__(self, e_hbm, s_hbm, ebuf, sbuf, sems, base):
        self.refs = (e_hbm, s_hbm, ebuf, sbuf, sems)
        self.base = base

    def copies(self, t):
        e_hbm, s_hbm, ebuf, sbuf, sems = self.refs
        k, zg = (self.base + t) // NZG, (self.base + t) % NZG
        zs, xs = pl.ds(zg * ZG, ZG), pl.ds(pl.multiple_of(k * HALF, HALF), HALF)
        return (
            pltpu.make_async_copy(e_hbm.at[:, zs, :, xs, :], ebuf.at[t], sems.at[t, 0]),
            pltpu.make_async_copy(s_hbm.at[zs, :, xs, :], sbuf.at[t], sems.at[t, 1]),
        )

    def start(self, first, end):
        def one(t, _):
            for c in self.copies(t):
                c.start()
            return 0

        lax.fori_loop(first, end, one, 0)

    def wait(self, t):
        for c in self.copies(t):
            c.wait()


def forward_scan(fine, zc, xc, k, zg, extra):
    for h in range(2):
        hs = half(h)
        rows = [pl.ds(pl.multiple_of((zg * ZG + z) * NSEG, NSEG), NSEG) for z in range(ZG)]
        carry = [[xc[i, h, r, :] for i in range(4)] for r in rows]
        extra(h)
        for xm in range(HALF):
            zr = k * HALF + xm
            c0, c1, c2, t_z = [zc[zr, i, :, hs] for i in range(4)]
            for z in range(ZG):
                e0, e1, e2, sg = [fine[f, z, h, pl.ds(xm, NSEG, stride=PITCH), :] for f in range(4)]
                t_new = t_z * jnp.exp2(sg)
                share = t_z - t_new
                t_z = t_new
                c0 = c0 + share * e0
                c1 = c1 + share * e1
                c2 = c2 + share * e2
                d0, d1, d2, t_x = carry[z]
                t_new = t_x * jnp.exp2(sg * 0.25)
                share = t_x - t_new
                carry[z] = [d0 + share * e0, d1 + share * e1, d2 + share * e2, t_new]
            for i, v in enumerate((c0, c1, c2, t_z)):
                zc[zr, i, :, hs] = v
        for z in range(ZG):
            for i in range(4):
                xc[i, h, rows[z], :] = carry[z][i]


def compose(front, back):
    c0, c1, c2, t = front
    d0, d1, d2, u = back
    return (c0 + t * d0, c1 + t * d1, c2 + t * d2, t * u)


def merge(bricks, target, inv_step):
    ahead = (jnp.zeros_like(target[0]),) * 3 + (jnp.ones_like(target[0]),)
    fronts = []
    for brick in bricks:
        fronts.append(ahead[3])
        ahead = compose(ahead, brick)
    resid = [ahead[c] + ahead[3] * BACKLIGHT - target[c] for c in range(3)]
    g = [r * inv_step for r in resid]
    behind = [jnp.full_like(target[0], BACKLIGHT)] * 3
    replies = []
    for front, brick in reversed(list(zip(fronts, bricks))):
        dot = g[0] * behind[0] + g[1] * behind[1] + g[2] * behind[2]
        replies.append([front * g[0], front * g[1], front * g[2], front * dot])
        behind = [brick[c] + brick[3] * behind[c] for c in range(3)]
    replies.reverse()
    return replies, resid[0] * resid[0] + resid[1] * resid[1] + resid[2] * resid[2]


def forward_kernel(
    step_z, step_x, share,
    e_hbm, s_hbm, tz_hbm, tx_hbm, oz_hbm, ox_hbm, tab_hbm, perm_hbm, back_hbm,
    coz_hbm, cox_hbm, xst_hbm, ge0_hbm, gs0_hbm, owned,
    ebuf, sbuf, fine0, fine1, zc, xc, coz, cox,
    tab_back, coarse0, coarse1, eout, sout, zcar, xcar,
    tzb, txb, tzf, txf,
    sib, pc, got, rep, back, fin, finr,
    xloc, xgot, xrep, xback, xsuf,
    tab, perm, err, ozb, oxb, ez, ex, ey,
    in_sem, t_sem, sem_sib, sem_chip, sem_rep, sem_fin, sem_x, sem_xr, sem_ez, sem_ex, sem_ey, sem_co, sem_out, sem_xst,
):
    ix, iy, iz = lax.axis_index("gx"), lax.axis_index("gy"), lax.axis_index("gz")
    chip, core = iz // 2, iz % 2
    load = Loader(e_hbm, s_hbm, ebuf, sbuf, in_sem, 0)
    load.start(0, STEPS)
    lane = lax.broadcasted_iota(jnp.int32, (8, LANE), 1)
    sub = lax.broadcasted_iota(jnp.int32, (8, LANE), 0)
    weight = jnp.where(lane == 0, 1.0, 0.75)
    px = pl.ds(pl.multiple_of(iy * 256, 256), 256)
    tz_copy = pltpu.make_async_copy(tz_hbm.at[:, pl.ds(pl.multiple_of(ix * 256, 256), 256), px], tzb, t_sem.at[0])
    tx_copy = pltpu.make_async_copy(tx_hbm.at[:, pl.ds(pl.multiple_of(iz * NZ, NZ), NZ), px], txb, t_sem.at[1])
    oz_copy = pltpu.make_async_copy(oz_hbm.at[ix, iy], ozb, t_sem.at[2])
    ox_copy = pltpu.make_async_copy(ox_hbm.at[iy, iz], oxb, t_sem.at[3])
    tab_copy = pltpu.make_async_copy(tab_hbm, tab, t_sem.at[4])
    perm_copy = pltpu.make_async_copy(perm_hbm, perm, t_sem.at[5])
    back_copy = pltpu.make_async_copy(back_hbm, tab_back, t_sem.at[6])
    tab_copy.start()
    late = (tz_copy, tx_copy, oz_copy, ox_copy, perm_copy, back_copy)
    for c in late:
        c.start()

    sibling = {"gz": chip * 2 + 1 - core}
    chips = [{"gz": lax.rem(chip + d, 4) * 2 + core} for d in (1, 2, 3)]
    slabs = [{"gx": lax.rem(ix + d, 4)} for d in (1, 2, 3)]
    barrier = pltpu.get_barrier_semaphore()
    row = [{"gz": lax.rem(iz + d, 8)} for d in range(1, 8)]
    column = [{"gy": lax.rem(iy + d, 4)} for d in (1, 2, 3)]
    for peer in row + slabs + column:
        pl.semaphore_signal(barrier, inc=1, device_id=peer, device_id_type=pl.DeviceIdType.MESH)

    def remote(src, dst, sems, peer):
        return pltpu.make_async_remote_copy(
            src_ref=src, dst_ref=dst, send_sem=sems.at[0], recv_sem=sems.at[1],
            device_id=peer, device_id_type=pl.DeviceIdType.MESH,
        )

    def sib_copy(k):
        return remote(zc.at[pl.ds(k * HALF + (1 - core) * 8, 8)], sib.at[k], sem_sib.at[k], sibling)

    def chip_copies(k):
        return [
            remote(pc.at[k, pl.ds(lax.rem(chip + d, 4) * 2, 2)], got.at[k, chip], sem_chip.at[k, d - 1], chips[d - 1])
            for d in (1, 2, 3)
        ]

    def rep_copies(k):
        return [
            remote(rep.at[k, lax.rem(chip + d, 4)], back.at[k, pl.ds(chip * 2, 2)], sem_rep.at[k, d - 1], chips[d - 1])
            for d in (1, 2, 3)
        ]

    def fin_copy(k):
        return remote(fin.at[k], finr.at[k], sem_fin.at[k], sibling)

    def x_copies():
        return [remote(xloc.at[lax.rem(ix + d, 4)], xgot.at[ix], sem_x.at[d - 1], slabs[d - 1]) for d in (1, 2, 3)]

    def xr_copies():
        return [remote(xrep.at[lax.rem(ix + d, 4)], xback.at[ix], sem_xr.at[d - 1], slabs[d - 1]) for d in (1, 2, 3)]

    def pair(k, m, hs):
        mine = [zc[k * HALF + core * 8 + m, i, :, hs] for i in range(4)]
        other = [sib[k, m, i, :, hs] for i in range(4)]
        first = core == 0
        return [jnp.where(first, a, b) for a, b in zip(mine, other)], [jnp.where(first, b, a) for a, b in zip(mine, other)]

    def z_compose(k):
        sib_copy(k).wait_recv()

        def body(m, _):
            for h in range(2):
                front, rear = pair(k, m, half(h))
                for i, v in enumerate(compose(front, rear)):
                    pc[k, m, i, :, half(h)] = v
            return 0

        lax.fori_loop(0, 8, body, 0)
        for c in chip_copies(k):
            c.start()

    def z_merge(k):
        for c in chip_copies(k):
            c.wait_recv()
        for i in range(2):
            m = chip * 2 + i
            got[k, chip, i] = pc[k, m]
            sq = jnp.zeros((8, LANE), F32)
            for h in range(2):
                bricks = [[got[k, o, i, f, :, half(h)] for f in range(4)] for o in range(4)]
                row = k * HALF + core * 8 + m
                target = [tzf[c, h, pl.ds(row, NSEG, stride=SEG + 4), :] for c in range(3)]
                replies, s = merge(bricks, target, weight * (1.0 / step_z))
                sq = sq + s
                for o in range(4):
                    for f in range(4):
                        rep[k, o, i, f, :, half(h)] = replies[o][f]
            err[k * 2 + i] = sq
        for c in rep_copies(k):
            c.start()
        back[k, pl.ds(chip * 2, 2)] = rep[k, chip]

    def z_split(k):
        for c in rep_copies(k):
            c.wait_recv()

        def body(m, _):
            for h in range(2):
                hs = half(h)
                a, b = pair(k, m, hs)
                g0, g1, g2, gt = [back[k, m, f, :, hs] for f in range(4)]
                inner_b = g0 * b[0] + g1 * b[1] + g2 * b[2] + gt * b[3]
                k_b = -(a[3] * inner_b)
                k_a = k_b - (g0 * a[0] + g1 * a[1] + g2 * a[2])
                part_a = (g0, g1, g2, k_a * step_z)
                part_b = (a[3] * g0, a[3] * g1, a[3] * g2, k_b * step_z)
                first = core == 0
                for f in range(4):
                    coz[k, core * 8 + m, f, :, hs] = jnp.where(first, part_a[f], part_b[f])
                    fin[k, m, f, :, hs] = jnp.where(first, part_b[f], part_a[f])
            return 0

        lax.fori_loop(0, 8, body, 0)
        fin_copy(k).start()

    mine, other = pl.ds(core * 8, 8), pl.ds((1 - core) * 8, 8)
    mine_copy = pltpu.make_async_copy(coz.at[1, mine], coz_hbm.at[mine], sem_co.at[0])
    other_copy = pltpu.make_async_copy(finr.at[1], coz_hbm.at[other], sem_co.at[1])

    def x_compose():
        for g in range(4):
            for h in range(2):
                acc = None
                for s in range(NSEG):
                    rows = pl.ds(g * 64 + s, 8, stride=NSEG)
                    seg = tuple(xc[i, h, rows, :] for i in range(4))
                    acc = seg if acc is None else compose(acc, seg)
                for f in range(4):
                    xloc[g, f, :, half(h)] = acc[f]
        for c in x_copies():
            c.start()

    def x_merge():
        for c in x_copies():
            c.wait_recv()
        xgot[ix] = xloc[ix]
        sq = jnp.zeros((8, LANE), F32)
        for h in range(2):
            bricks = [[xgot[o, f, :, half(h)] for f in range(4)] for o in range(4)]
            target = [txf[c, pl.ds(pl.multiple_of(ix * 8, 8), 8), half(h)] for c in range(3)]
            replies, s = merge(bricks, target, weight * (1.0 / step_x))
            sq = sq + s
            for o in range(4):
                for f in range(4):
                    xrep[o, f, :, half(h)] = replies[o][f]
        err[4] = sq
        for c in xr_copies():
            c.start()
        xback[ix] = xrep[ix]

    cox_copy = pltpu.make_async_copy(cox, cox_hbm, sem_co.at[2])

    def x_split():
        for c in xr_copies():
            c.wait_recv()
        for g in range(4):
            for h in range(2):
                g0, g1, g2, gt = [xback[g, f, :, half(h)] for f in range(4)]
                suffix = None
                for s in reversed(range(NSEG)):
                    rows = pl.ds(g * 64 + s, 8, stride=NSEG)
                    seg = tuple(xc[i, h, rows, :] for i in range(4))
                    suffix = seg if suffix is None else compose(seg, suffix)
                    xsuf[s] = g0 * suffix[0] + g1 * suffix[1] + g2 * suffix[2] + gt * suffix[3]
                front = jnp.ones((8, LANE), F32)
                for s in range(NSEG):
                    rows = pl.ds(g * 64 + s, 8, stride=NSEG)
                    cox[0, h, rows, :] = front * g0
                    cox[1, h, rows, :] = front * g1
                    cox[2, h, rows, :] = front * g2
                    cox[3, h, rows, :] = front * xsuf[s] * (-step_x)
                    for c in range(3):
                        cox[4 + c, h, rows, :] = 0.25 * cox[c, h, rows, :]
                    front = front * xc[3, h, rows, :]
        cox_copy.start()

    def scatter(sq, ids):
        owner = jnp.zeros((8, LANE), jnp.int32)
        for s, o in enumerate(ids):
            owner = jnp.where(sub == s, o, owner)
        return jnp.where(lane == owner, jnp.sum(sq, axis=1, keepdims=True), 0.0)

    def ez_copies():
        return [remote(ez.at[7], ez.at[d - 1], sem_ez.at[d - 1], row[d - 1]) for d in range(1, 8)]

    def ex_copies():
        return [remote(ex.at[3], ex.at[d - 1], sem_ex.at[d - 1], slabs[d - 1]) for d in (1, 2, 3)]

    def ey_copies():
        return [remote(ey.at[3], ey.at[d - 1], sem_ey.at[d - 1], column[d - 1]) for d in (1, 2, 3)]

    def err_start():
        total = jnp.zeros((8, LANE), F32)
        for k in range(2):
            for i in range(2):
                cell = k * HALF + core * 8 + chip * 2 + i
                total = total + scatter(err[k * 2 + i], [ix * 32 + ozb[0, s * SEG + cell] for s in range(NSEG)])
        ez[7] = total
        ex[3] = scatter(err[4], [oxb[0, ix * 8 + s] * 8 + iz for s in range(8)])
        for c in ez_copies() + ex_copies():
            c.start()

    def err_middle():
        for c in ez_copies() + ex_copies():
            c.wait_recv()
        total = ez[7] + ex[3]
        for d in range(7):
            total = total + ez[d]
        for d in range(3):
            total = total + ex[d]
        ey[3] = total
        for c in ey_copies():
            c.start()

    def err_finish():
        for c in ey_copies():
            c.wait_recv()
        total = ey[0] + ey[1] + ey[2] + ey[3]
        mine = jnp.where(lane == ix * 32 + iy * 8 + iz, total, 0.0)
        owned[0, 0] = jnp.sum(mine) * share

    for i in range(3):
        xc[i] = jnp.zeros_like(xc[i])
    xc[3] = jnp.ones_like(xc[3])

    def clear(m, _):
        for f in range(4):
            zc[m, f] = jnp.full((8, 256), float(f == 3), F32)
        return 0

    lax.fori_loop(0, SEG, clear, 0)
    tab_copy.wait()
    load.wait(0)
    for part in range(2):
        upsample_part(ebuf, sbuf, 0, tab, fine0, part)

    def pair_of_steps(i, _):
        for b, (fine, ahead) in enumerate(((fine0, fine1), (fine1, fine0))):
            t = i * 2 + b

            @pl.when(t + 1 < STEPS)
            def _():
                load.wait(t + 1)

            forward_scan(
                fine, zc, xc, t // NZG, t % NZG,
                lambda part: upsample_part(ebuf, sbuf, t + 1, tab, ahead, part),
            )

        @pl.when(i == 3)
        def _():
            pl.semaphore_wait(barrier, 13)
            sib_copy(0).start()

        @pl.when(i == 4)
        def _():
            z_compose(0)

        return 0

    lax.fori_loop(0, STEPS // 2, pair_of_steps, 0)
    sib_copy(1).start()
    x_compose()
    for c in late:
        c.wait()

    def widen(c, _):
        r = jnp.dot(tzb[c], perm[...], preferred_element_type=F32)
        for h in range(2):
            for s in range(NSEG):
                tzf[c, h, pl.ds(s * (SEG + 4), SEG), :] = r[s * SEG : (s + 1) * SEG, half(h)]
        txf[c] = jnp.dot(txb[c], perm[...], preferred_element_type=F32)
        return 0

    lax.fori_loop(0, 3, widen, 0)
    z_merge(0)
    z_compose(1)
    for part in range(2):
        upsample_part(ebuf, sbuf, 0, tab_back, fine0, part)
    zcar[0] = jnp.ones_like(zcar[0])
    xcar[0] = jnp.ones_like(xcar[0])
    x_merge()
    z_split(0)
    z_merge(1)
    err_start()
    x_split()
    xcar[1] = cox[3]
    fin_copy(0).wait_recv()
    coz[0, other] = finr[0]
    zcar[1] = coz[0, :, 3]

    def stores(t):
        return store_copies(eout, sout, ge0_hbm, gs0_hbm, sem_out, t)

    def store(t):
        for c in stores(t):
            c.start()

    def state_copy(i):
        rows = pl.ds(pl.multiple_of(i * 2 * ZG * NSEG, 2 * ZG * NSEG), 2 * ZG * NSEG)
        return pltpu.make_async_copy(xcar.at[:, :, rows, :], xst_hbm.at[:, :, rows, :], sem_xst.at[i])

    def after(i):
        state_copy(i).start()

        @pl.when(i == 1)
        def _():
            z_split(1)
            mine_copy.start()
            err_middle()

    backward_steps(
        lambda t: None, after, store, ebuf, sbuf, tab_back, (fine0, fine1), (coarse0, coarse1),
        eout, sout, zcar, xcar, coz.at[0], cox,
    )
    fin_copy(1).wait_recv()
    other_copy.start()
    err_finish()
    for k in range(2):
        for c in [sib_copy(k)] + chip_copies(k) + rep_copies(k) + [fin_copy(k)]:
            c.wait_send()
    for c in x_copies() + xr_copies() + ez_copies() + ex_copies() + ey_copies():
        c.wait_send()
    for c in (mine_copy, other_copy, cox_copy):
        c.wait()

    def finish(t, _):
        for c in stores(t):
            c.wait()
        return 0

    lax.fori_loop(0, NZG, finish, 0)
    for i in range(NZG // 2):
        state_copy(i).wait()


def project_down(even, odd, third):
    return even + third * odd + pltpu.roll(odd + third * even, LANE - 1, axis=1)


def backward_scan(fine, zcar, xcar, coz, cox, coarse, zg, pair, third):
    planes = [pair * 2 + i for i in range(2)]
    rows = [pl.ds(pl.multiple_of((zg * ZG + z) * NSEG, NSEG), NSEG) for z in planes]
    carry = [[[xcar[i, h, r, :] for i in range(2)] for h in range(2)] for r in rows]
    gx = [[[cox[c, h, r, :] for c in range(3)] for h in range(2)] for r in rows]
    for xm in range(HALF):
        z_carry = [[zcar[i, xm, :, half(h)] for i in range(2)] for h in range(2)]
        gz = [[coz[xm, c, :, half(h)] for c in range(3)] for h in range(2)]
        for n, z in enumerate(planes):
            out = [[None] * 2 for _ in range(4)]
            for h in range(2):
                e0, e1, e2, sg = [fine[f, z, h, pl.ds(xm, NSEG, stride=PITCH), :] for f in range(4)]
                g0, g1, g2 = gz[h]
                t_z, a_z = z_carry[h]
                t_new = t_z * jnp.exp2(sg)
                share_z = t_z - t_new
                inner = g0 * e0 + g1 * e1 + g2 * e2
                a_z = a_z + share_z * inner
                grad = t_new * inner + a_z
                z_carry[h] = [t_new, a_z]
                h0, h1, h2 = gx[n][h]
                t_x, a_x = carry[n][h]
                t_new = t_x * jnp.exp2(sg * 0.25)
                share_x = t_x - t_new
                q0, q1, q2 = [cox[4 + c, h, rows[n], :] for c in range(3)]
                inner = q0 * e0 + q1 * e1 + q2 * e2
                a_x = a_x + share_x * inner
                out[3][h] = (grad + a_x) + t_new * inner
                carry[n][h] = [t_new, a_x]
                out[0][h] = g0 * share_z + h0 * share_x
                out[1][h] = g1 * share_z + h1 * share_x
                out[2][h] = g2 * share_z + h2 * share_x
            for f in range(4):
                coarse[f, z, pl.ds(xm, NSEG, stride=PITCH), :] = project_down(out[f][0], out[f][1], third)
        for h in range(2):
            for i in range(2):
                zcar[i, xm, :, half(h)] = z_carry[h][i]
    for n, r in enumerate(rows):
        for h in range(2):
            for i in range(2):
                xcar[i, h, r, :] = carry[n][h][i]


def narrow_part(coarse, eout, sout, t, part):
    for z in (2 * part, 2 * part + 1):
        for f in range(4):
            for s in range(NSEG):
                v = coarse[f, z, pl.ds(s * PITCH, HALF), :].astype(BF16)
                if f == 3:
                    sout[t, z, s] = v
                else:
                    eout[t, f, z, s] = v


def lane_third():
    return jnp.where(lax.broadcasted_iota(jnp.int32, (NSEG, LANE), 1) == 0, 0.0, 1.0 / 3.0)


def backward_steps(ahead_wait, after, store, ebuf, sbuf, tab, fines, coarses, eout, sout, zcar, xcar, coz, cox):
    third = lane_third()
    fine0, fine1 = fines
    coarse0, coarse1 = coarses

    def pair_of_steps(i, _):
        for b, (fine, ahead, new, old) in enumerate(((fine0, fine1, coarse0, coarse1), (fine1, fine0, coarse1, coarse0))):
            t = i * 2 + b
            ahead_wait(t + 1)
            for part in range(2):
                upsample_part(ebuf, sbuf, t + 1, tab, ahead, part)
                narrow_part(old, eout, sout, lax.rem(t + NZG, NZG + 1), part)
                backward_scan(fine, zcar, xcar, coz, cox, new, t, part, third)

            @pl.when(t > 0)
            def _():
                store(t - 1)

        after(i)
        return 0

    lax.fori_loop(0, NZG // 2, pair_of_steps, 0)
    for part in range(2):
        narrow_part(coarse1, eout, sout, NZG - 1, part)
    store(NZG - 1)


def store_copies(eout, sout, ge, gs, sems, t):
    zr = pl.ds(t * ZG, ZG)
    return (
        pltpu.make_async_copy(eout.at[t], ge.at[:, zr], sems.at[t, 0]),
        pltpu.make_async_copy(sout.at[t], gs.at[zr], sems.at[t, 1]),
    )


def backward_kernel(
    e_hbm, s_hbm, tab_hbm, coz_hbm, cox_hbm, xst_hbm, ge0_hbm, gs0_hbm,
    ge_hbm, gs_hbm,
    ebuf, sbuf, fine0, fine1, tab, coarse0, coarse1,
    eout, sout, zcar, xcar, coz, cox, epass, spass,
    in_sem, out_sem, co_sem, pass_sem, on_sem,
):
    load = Loader(e_hbm, s_hbm, ebuf, sbuf, in_sem, NZG)
    tab_copy = pltpu.make_async_copy(tab_hbm, tab, co_sem.at[0])
    handed = (
        pltpu.make_async_copy(coz_hbm, coz, co_sem.at[1]),
        pltpu.make_async_copy(cox_hbm, cox, co_sem.at[2]),
        pltpu.make_async_copy(xst_hbm, xcar, co_sem.at[3]),
    )

    def fetches(t):
        zr = pl.ds(t * ZG, ZG)
        return (
            pltpu.make_async_copy(ge0_hbm.at[:, zr], epass.at[t], pass_sem.at[t, 0]),
            pltpu.make_async_copy(gs0_hbm.at[zr], spass.at[t], pass_sem.at[t, 1]),
        )

    def passes(t):
        xr = pl.ds(0, HALF)
        return store_copies(epass, spass, ge_hbm.at[:, :, :, xr, :], gs_hbm.at[:, :, xr, :], on_sem, t)

    tab_copy.start()
    load.start(0, 1)
    for c in handed:
        c.start()
    load.start(1, NZG)

    def fetch(t, _):
        for c in fetches(t):
            c.start()
        return 0

    lax.fori_loop(0, NZG, fetch, 0)

    def stores(t):
        xr = pl.ds(HALF, HALF)
        return store_copies(eout, sout, ge_hbm.at[:, :, :, xr, :], gs_hbm.at[:, :, xr, :], out_sem, t)

    def store(t):
        for c in stores(t):
            c.start()
        for c in fetches(t):
            c.wait()
        for c in passes(t):
            c.start()

    def ahead_wait(t):
        @pl.when(t < NZG)
        def _():
            load.wait(t)

    zcar[0] = jnp.ones_like(zcar[0])
    tab_copy.wait()
    load.wait(0)
    for part in range(2):
        upsample_part(ebuf, sbuf, 0, tab, fine0, part)
    for c in handed:
        c.wait()
    zcar[1] = coz[:, 3]
    backward_steps(
        ahead_wait, lambda i: None, store, ebuf, sbuf, tab, (fine0, fine1), (coarse0, coarse1),
        eout, sout, zcar, xcar, coz, cox,
    )

    def finish(t, _):
        for c in stores(t) + passes(t):
            c.wait()
        return 0

    lax.fori_loop(0, NZG, finish, 0)


def vmem(*shape, dtype=F32):
    return pltpu.VMEM(shape, dtype)


HBM = pl.BlockSpec(memory_space=pltpu.HBM)


def local(emission, absorption, target_z, target_x, owner_z, owner_x):
    depth_z, width_x, width_y = absorption.shape
    pixels = 2 * width_y
    count_x = lax.axis_size("gx")
    count_y = lax.axis_size("gy")
    count_z = lax.axis_size("gz")
    step_z = OPTICAL / (depth_z * count_z)
    step_x = OPTICAL / (width_x * count_x)
    interp = interp_table(width_y)
    rate = interp.T * (-step_z * math.log2(math.e))
    order = np.concatenate([np.arange(0, pixels, 2), np.roll(np.arange(1, pixels, 2), 1)])
    rate_hi = rate.astype(BF16)
    rate_lo = (rate - rate_hi.astype(np.float64)).astype(BF16)
    tab = np.concatenate([interp.T.astype(BF16), rate_hi, rate_lo], axis=0)[:, order]
    tab_back = np.concatenate([(interp.T * step_z).astype(BF16), rate_hi, rate_lo], axis=0)[:, order]
    perm = np.eye(pixels)[:, order].astype(BF16)
    slots = 2 * width_x // (count_y * count_z) + 2 * depth_z // (count_x * count_y)
    e5 = emission.reshape(3, depth_z, NSEG, SEG, width_y)
    s4 = absorption.reshape(depth_z, NSEG, SEG, width_y)

    def buffers(steps):
        return [
            vmem(steps + 1, 3, ZG, NSEG, HALF, LANE, dtype=BF16), vmem(steps + 1, ZG, NSEG, HALF, LANE, dtype=BF16),
            vmem(4, ZG, 2, NSEG * PITCH, LANE), vmem(4, ZG, 2, NSEG * PITCH, LANE),
        ]

    back_buffers = [
        vmem(3 * LANE, 256, dtype=BF16), vmem(4, ZG, NSEG * PITCH, LANE), vmem(4, ZG, NSEG * PITCH, LANE),
        vmem(NZG + 1, 3, ZG, NSEG, HALF, LANE, dtype=BF16), vmem(NZG + 1, ZG, NSEG, HALF, LANE, dtype=BF16),
        vmem(2, HALF, NSEG, 256), vmem(2, 2, NZ * NSEG, LANE),
    ]
    dma = pltpu.SemaphoreType.DMA
    coz, cox, xst, ge0, gs0, owned = pl.pallas_call(
        functools.partial(forward_kernel, step_z, step_x, 1.0 / (3.0 * pixels * slots)),
        out_shape=[
            jax.ShapeDtypeStruct((HALF, 4, NSEG, 256), F32),
            jax.ShapeDtypeStruct((7, 2, NZ * NSEG, LANE), F32),
            jax.ShapeDtypeStruct((2, 2, NZ * NSEG, LANE), F32),
            jax.ShapeDtypeStruct((3, NZ, NSEG, HALF, LANE), BF16),
            jax.ShapeDtypeStruct((NZ, NSEG, HALF, LANE), BF16),
            jax.ShapeDtypeStruct((1, 1), F32),
        ],
        in_specs=[HBM] * 9,
        out_specs=[HBM] * 5 + [pl.BlockSpec(memory_space=pltpu.SMEM)],
        scratch_shapes=buffers(STEPS) + [
            vmem(SEG, 4, NSEG, 256), vmem(4, 2, NZ * NSEG, LANE), vmem(2, HALF, 4, NSEG, 256), vmem(7, 2, NZ * NSEG, LANE),
        ] + back_buffers + [
            vmem(3, 256, 256, dtype=BF16), vmem(3, NZ, 256, dtype=BF16),
            vmem(3, 2, NSEG * (SEG + 4), LANE), vmem(3, NZ, 256),
            vmem(2, 8, 4, 8, 256), vmem(2, 8, 4, 8, 256), vmem(2, 4, 2, 4, 8, 256), vmem(2, 4, 2, 4, 8, 256),
            vmem(2, 8, 4, 8, 256), vmem(2, 8, 4, 8, 256), vmem(2, 8, 4, 8, 256),
            vmem(4, 4, 8, 256), vmem(4, 4, 8, 256), vmem(4, 4, 8, 256), vmem(4, 4, 8, 256), vmem(NSEG, 8, LANE),
            vmem(3 * LANE, 256, dtype=BF16), vmem(256, 256, dtype=BF16), vmem(5, 8, LANE),
            pltpu.SMEM((1, 256), jnp.int32), pltpu.SMEM((1, NZ), jnp.int32),
            vmem(8, 8, LANE), vmem(4, 8, LANE), vmem(4, 8, LANE),
            dma((STEPS, 2)), dma((7,)), dma((2, 2)), dma((2, 3, 2)), dma((2, 3, 2)), dma((2, 2)), dma((3, 2)), dma((3, 2)),
            dma((7, 2)), dma((3, 2)), dma((3, 2)), dma((3,)), dma((NZG, 2)), dma((NZG // 2,)),
        ],
        compiler_params=pltpu.CompilerParams(
            collective_id=0, has_side_effects=True, vmem_limit_bytes=VMEM_LIMIT
        ),
    )(
        e5, s4, target_z, target_x, owner_z.reshape(count_x, count_y, 1, width_x),
        owner_x.reshape(count_y, count_z, 1, depth_z), tab, perm, tab_back,
    )

    grad_e, grad_s = pl.pallas_call(
        backward_kernel,
        out_shape=[jax.ShapeDtypeStruct(e5.shape, BF16), jax.ShapeDtypeStruct(s4.shape, BF16)],
        in_specs=[HBM] * 8,
        out_specs=[HBM, HBM],
        scratch_shapes=buffers(NZG) + back_buffers + [
            vmem(HALF, 4, NSEG, 256), vmem(7, 2, NZ * NSEG, LANE),
            vmem(NZG, 3, ZG, NSEG, HALF, LANE, dtype=BF16), vmem(NZG, ZG, NSEG, HALF, LANE, dtype=BF16),
            dma((NZG, 2)), dma((NZG, 2)), dma((4,)), dma((NZG, 2)), dma((NZG, 2)),
        ],
        compiler_params=pltpu.CompilerParams(vmem_limit_bytes=VMEM_LIMIT),
        cost_estimate=pl.CostEstimate(flops=6 * 10**9, bytes_accessed=20 * 2**20, transcendentals=0),
    )(e5, s4, tab_back, coz, cox, xst, ge0, gs0)
    return (grad_e.reshape(emission.shape), grad_s.reshape(absorption.shape), owned.reshape(1, 1, 1))


def solution(mesh):
    return jax.shard_map(
        local,
        mesh=mesh,
        in_specs=(P(None, "gz", "gx", "gy"), P("gz", "gx", "gy"), P(), P(), P(), P()),
        out_specs=(P(None, "gz", "gx", "gy"), P("gz", "gx", "gy"), P("gx", "gy", "gz")),
        check_vma=False,
    )
```

```python
import functools
import math

import jax
import jax.numpy as jnp
import numpy as np
from jax import lax
from jax.experimental import pallas as pl
from jax.experimental.pallas import tpu as pltpu
from jax.sharding import PartitionSpec as P

F32 = jnp.float32
BF16 = jnp.bfloat16
OPTICAL = 1.5
BACKLIGHT = 1.0

NSEG = 8
SEG = 32
HALF = 16
PITCH = 20
ZG = 4
NZ = 32
NZG = NZ // ZG
STEPS = 2 * NZG
LANE = 128
VMEM_LIMIT = 61 * 2**20 + 2**19


def interp_table(width):
    pixels = np.arange(2 * width)
    nearest = pixels // 2
    second = np.clip(nearest + 2 * (pixels % 2) - 1, 0, width - 1)
    columns = np.arange(width)
    return 0.75 * (columns[None, :] == nearest[:, None]) + 0.25 * (columns[None, :] == second[:, None])


def half(h):
    return slice(h * LANE, (h + 1) * LANE)


def upsample_store(fine, f, z, r):
    for s in range(NSEG):
        for h in range(2):
            fine[f, z, h, s * PITCH : s * PITCH + HALF] = r[s * HALF : (s + 1) * HALF, half(h)]


def upsample_part(ebuf, sbuf, t, tab, fine, part):
    rows = NSEG * HALF
    if part == 0:
        a = ebuf[t, 0:2].reshape(2 * ZG * rows, LANE)
        r = jnp.dot(a, tab[0:LANE], preferred_element_type=F32)
        for f in range(2):
            for z in range(ZG):
                i = f * ZG + z
                upsample_store(fine, f, z, r[i * rows : (i + 1) * rows])
    else:
        r = jnp.dot(ebuf[t, 2].reshape(ZG * rows, LANE), tab[0:LANE], preferred_element_type=F32)
        s = sbuf[t].reshape(ZG * rows, LANE)
        q = jnp.dot(jnp.concatenate([s, s], axis=1), tab[LANE:], preferred_element_type=F32)
        for z in range(ZG):
            upsample_store(fine, 2, z, r[z * rows : (z + 1) * rows])
            upsample_store(fine, 3, z, q[z * rows : (z + 1) * rows])


class Loader:
    def __init__(self, e_hbm, s_hbm, ebuf, sbuf, sems, base):
        self.refs = (e_hbm, s_hbm, ebuf, sbuf, sems)
        self.base = base

    def copies(self, t):
        e_hbm, s_hbm, ebuf, sbuf, sems = self.refs
        k, zg = (self.base + t) // NZG, (self.base + t) % NZG
        zs, xs = pl.ds(zg * ZG, ZG), pl.ds(pl.multiple_of(k * HALF, HALF), HALF)
        return (
            pltpu.make_async_copy(e_hbm.at[:, zs, :, xs, :], ebuf.at[t], sems.at[t, 0]),
            pltpu.make_async_copy(s_hbm.at[zs, :, xs, :], sbuf.at[t], sems.at[t, 1]),
        )

    def start(self, first, end):
        def one(t, _):
            for c in self.copies(t):
                c.start()
            return 0

        lax.fori_loop(first, end, one, 0)

    def wait(self, t):
        for c in self.copies(t):
            c.wait()


def forward_scan(fine, zc, xc, k, zg, extra):
    for h in range(2):
        hs = half(h)
        rows = [pl.ds(pl.multiple_of((zg * ZG + z) * NSEG, NSEG), NSEG) for z in range(ZG)]
        carry = [[xc[i, h, r, :] for i in range(4)] for r in rows]
        extra(h)
        for xm in range(HALF):
            zr = k * HALF + xm
            c0, c1, c2, t_z = [zc[zr, i, :, hs] for i in range(4)]
            for z in range(ZG):
                e0, e1, e2, sg = [fine[f, z, h, pl.ds(xm, NSEG, stride=PITCH), :] for f in range(4)]
                t_new = t_z * jnp.exp2(sg)
                share = t_z - t_new
                t_z = t_new
                c0 = c0 + share * e0
                c1 = c1 + share * e1
                c2 = c2 + share * e2
                d0, d1, d2, t_x = carry[z]
                t_new = t_x * jnp.exp2(sg * 0.25)
                share = t_x - t_new
                carry[z] = [d0 + share * e0, d1 + share * e1, d2 + share * e2, t_new]
            for i, v in enumerate((c0, c1, c2, t_z)):
                zc[zr, i, :, hs] = v
        for z in range(ZG):
            for i in range(4):
                xc[i, h, rows[z], :] = carry[z][i]


def compose(front, back):
    c0, c1, c2, t = front
    d0, d1, d2, u = back
    return (c0 + t * d0, c1 + t * d1, c2 + t * d2, t * u)


def merge(bricks, target, inv_step):
    ahead = (jnp.zeros_like(target[0]),) * 3 + (jnp.ones_like(target[0]),)
    fronts = []
    for brick in bricks:
        fronts.append(ahead[3])
        ahead = compose(ahead, brick)
    resid = [ahead[c] + ahead[3] * BACKLIGHT - target[c] for c in range(3)]
    g = [r * inv_step for r in resid]
    behind = [jnp.full_like(target[0], BACKLIGHT)] * 3
    replies = []
    for front, brick in reversed(list(zip(fronts, bricks))):
        dot = g[0] * behind[0] + g[1] * behind[1] + g[2] * behind[2]
        replies.append([front * g[0], front * g[1], front * g[2], front * dot])
        behind = [brick[c] + brick[3] * behind[c] for c in range(3)]
    replies.reverse()
    return replies, resid[0] * resid[0] + resid[1] * resid[1] + resid[2] * resid[2]


def forward_kernel(
    step_z, step_x, share,
    e_hbm, s_hbm, tz_hbm, tx_hbm, oz_hbm, ox_hbm, tab_hbm, perm_hbm, back_hbm,
    coz_hbm, cox_hbm, xst_hbm, ge0_hbm, gs0_hbm, owned,
    ebuf, sbuf, fine0, fine1, zc, xc, coz, cox,
    tab_back, coarse0, coarse1, eout, sout, zcar, xcar,
    tzb, txb, tzf, txf,
    sib, pc, got, rep, back, fin, finr,
    xloc, xgot, xrep, xback, xsuf,
    tab, perm, err, ozb, oxb, ez, ex, ey,
    in_sem, t_sem, sem_sib, sem_chip, sem_rep, sem_fin, sem_x, sem_xr, sem_ez, sem_ex, sem_ey, sem_co, sem_out, sem_xst,
):
    ix, iy, iz = lax.axis_index("gx"), lax.axis_index("gy"), lax.axis_index("gz")
    chip, core = iz // 2, iz % 2
    load = Loader(e_hbm, s_hbm, ebuf, sbuf, in_sem, 0)
    tab_copy = pltpu.make_async_copy(tab_hbm, tab, t_sem.at[4])
    tab_copy.start()
    load.start(0, STEPS)
    lane = lax.broadcasted_iota(jnp.int32, (8, LANE), 1)
    sub = lax.broadcasted_iota(jnp.int32, (8, LANE), 0)
    weight = jnp.where(lane == 0, 1.0, 0.75)
    px = pl.ds(pl.multiple_of(iy * 256, 256), 256)
    tz_copy = pltpu.make_async_copy(tz_hbm.at[:, pl.ds(pl.multiple_of(ix * 256, 256), 256), px], tzb, t_sem.at[0])
    tx_copy = pltpu.make_async_copy(tx_hbm.at[:, pl.ds(pl.multiple_of(iz * NZ, NZ), NZ), px], txb, t_sem.at[1])
    oz_copy = pltpu.make_async_copy(oz_hbm.at[ix, iy], ozb, t_sem.at[2])
    ox_copy = pltpu.make_async_copy(ox_hbm.at[iy, iz], oxb, t_sem.at[3])
    perm_copy = pltpu.make_async_copy(perm_hbm, perm, t_sem.at[5])
    back_copy = pltpu.make_async_copy(back_hbm, tab_back, t_sem.at[6])
    late = (tz_copy, tx_copy, oz_copy, ox_copy, perm_copy, back_copy)
    for c in late:
        c.start()

    sibling = {"gz": chip * 2 + 1 - core}
    chips = [{"gz": lax.rem(chip + d, 4) * 2 + core} for d in (1, 2, 3)]
    slabs = [{"gx": lax.rem(ix + d, 4)} for d in (1, 2, 3)]
    barrier = pltpu.get_barrier_semaphore()
    row = [{"gz": lax.rem(iz + d, 8)} for d in range(1, 8)]
    column = [{"gy": lax.rem(iy + d, 4)} for d in (1, 2, 3)]
    for peer in row + slabs + column:
        pl.semaphore_signal(barrier, inc=1, device_id=peer, device_id_type=pl.DeviceIdType.MESH)

    def remote(src, dst, sems, peer):
        return pltpu.make_async_remote_copy(
            src_ref=src, dst_ref=dst, send_sem=sems.at[0], recv_sem=sems.at[1],
            device_id=peer, device_id_type=pl.DeviceIdType.MESH,
        )

    def sib_copy(k):
        return remote(zc.at[pl.ds(k * HALF + (1 - core) * 8, 8)], sib.at[k], sem_sib.at[k], sibling)

    def chip_copies(k):
        return [
            remote(pc.at[k, pl.ds(lax.rem(chip + d, 4) * 2, 2)], got.at[k, chip], sem_chip.at[k, d - 1], chips[d - 1])
            for d in (1, 2, 3)
        ]

    def rep_copies(k):
        return [
            remote(rep.at[k, lax.rem(chip + d, 4)], back.at[k, pl.ds(chip * 2, 2)], sem_rep.at[k, d - 1], chips[d - 1])
            for d in (1, 2, 3)
        ]

    def fin_copy(k):
        return remote(fin.at[k], finr.at[k], sem_fin.at[k], sibling)

    def x_copies():
        return [remote(xloc.at[lax.rem(ix + d, 4)], xgot.at[ix], sem_x.at[d - 1], slabs[d - 1]) for d in (1, 2, 3)]

    def xr_copies():
        return [remote(xrep.at[lax.rem(ix + d, 4)], xback.at[ix], sem_xr.at[d - 1], slabs[d - 1]) for d in (1, 2, 3)]

    def pair(k, m, hs):
        mine = [zc[k * HALF + core * 8 + m, i, :, hs] for i in range(4)]
        other = [sib[k, m, i, :, hs] for i in range(4)]
        first = core == 0
        return [jnp.where(first, a, b) for a, b in zip(mine, other)], [jnp.where(first, b, a) for a, b in zip(mine, other)]

    def z_compose(k):
        sib_copy(k).wait_recv()

        def body(m, _):
            for h in range(2):
                front, rear = pair(k, m, half(h))
                for i, v in enumerate(compose(front, rear)):
                    pc[k, m, i, :, half(h)] = v
            return 0

        lax.fori_loop(0, 8, body, 0)
        for c in chip_copies(k):
            c.start()

    def z_merge(k):
        for c in chip_copies(k):
            c.wait_recv()
        for i in range(2):
            m = chip * 2 + i
            got[k, chip, i] = pc[k, m]
            sq = jnp.zeros((8, LANE), F32)
            for h in range(2):
                bricks = [[got[k, o, i, f, :, half(h)] for f in range(4)] for o in range(4)]
                row = k * HALF + core * 8 + m
                target = [tzf[c, h, pl.ds(row, NSEG, stride=SEG + 4), :] for c in range(3)]
                replies, s = merge(bricks, target, weight * (1.0 / step_z))
                sq = sq + s
                for o in range(4):
                    for f in range(4):
                        rep[k, o, i, f, :, half(h)] = replies[o][f]
            err[k * 2 + i] = sq
        for c in rep_copies(k):
            c.start()
        back[k, pl.ds(chip * 2, 2)] = rep[k, chip]

    def z_split(k):
        for c in rep_copies(k):
            c.wait_recv()

        def body(m, _):
            for h in range(2):
                hs = half(h)
                a, b = pair(k, m, hs)
                g0, g1, g2, gt = [back[k, m, f, :, hs] for f in range(4)]
                inner_b = g0 * b[0] + g1 * b[1] + g2 * b[2] + gt * b[3]
                k_b = -(a[3] * inner_b)
                k_a = k_b - (g0 * a[0] + g1 * a[1] + g2 * a[2])
                part_a = (g0, g1, g2, k_a * step_z)
                part_b = (a[3] * g0, a[3] * g1, a[3] * g2, k_b * step_z)
                first = core == 0
                for f in range(4):
                    coz[k, core * 8 + m, f, :, hs] = jnp.where(first, part_a[f], part_b[f])
                    fin[k, m, f, :, hs] = jnp.where(first, part_b[f], part_a[f])
            return 0

        lax.fori_loop(0, 8, body, 0)
        fin_copy(k).start()

    mine, other = pl.ds(core * 8, 8), pl.ds((1 - core) * 8, 8)
    mine_copy = pltpu.make_async_copy(coz.at[1, mine], coz_hbm.at[mine], sem_co.at[0])
    other_copy = pltpu.make_async_copy(finr.at[1], coz_hbm.at[other], sem_co.at[1])

    def x_compose():
        for g in range(4):
            for h in range(2):
                acc = None
                for s in range(NSEG):
                    rows = pl.ds(g * 64 + s, 8, stride=NSEG)
                    seg = tuple(xc[i, h, rows, :] for i in range(4))
                    acc = seg if acc is None else compose(acc, seg)
                for f in range(4):
                    xloc[g, f, :, half(h)] = acc[f]
        for c in x_copies():
            c.start()

    def x_merge():
        for c in x_copies():
            c.wait_recv()
        xgot[ix] = xloc[ix]
        sq = jnp.zeros((8, LANE), F32)
        for h in range(2):
            bricks = [[xgot[o, f, :, half(h)] for f in range(4)] for o in range(4)]
            target = [txf[c, pl.ds(pl.multiple_of(ix * 8, 8), 8), half(h)] for c in range(3)]
            replies, s = merge(bricks, target, weight * (1.0 / step_x))
            sq = sq + s
            for o in range(4):
                for f in range(4):
                    xrep[o, f, :, half(h)] = replies[o][f]
        err[4] = sq
        for c in xr_copies():
            c.start()
        xback[ix] = xrep[ix]

    cox_copy = pltpu.make_async_copy(cox, cox_hbm, sem_co.at[2])

    def x_split():
        for c in xr_copies():
            c.wait_recv()
        for g in range(4):
            for h in range(2):
                g0, g1, g2, gt = [xback[g, f, :, half(h)] for f in range(4)]
                suffix = None
                for s in reversed(range(NSEG)):
                    rows = pl.ds(g * 64 + s, 8, stride=NSEG)
                    seg = tuple(xc[i, h, rows, :] for i in range(4))
                    suffix = seg if suffix is None else compose(seg, suffix)
                    xsuf[s] = g0 * suffix[0] + g1 * suffix[1] + g2 * suffix[2] + gt * suffix[3]
                front = jnp.ones((8, LANE), F32)
                for s in range(NSEG):
                    rows = pl.ds(g * 64 + s, 8, stride=NSEG)
                    cox[0, h, rows, :] = front * g0
                    cox[1, h, rows, :] = front * g1
                    cox[2, h, rows, :] = front * g2
                    cox[3, h, rows, :] = front * xsuf[s] * (-step_x)
                    for c in range(3):
                        cox[4 + c, h, rows, :] = 0.25 * cox[c, h, rows, :]
                    front = front * xc[3, h, rows, :]
        cox_copy.start()

    def scatter(sq, ids):
        owner = jnp.zeros((8, LANE), jnp.int32)
        for s, o in enumerate(ids):
            owner = jnp.where(sub == s, o, owner)
        return jnp.where(lane == owner, jnp.sum(sq, axis=1, keepdims=True), 0.0)

    def ez_copies():
        return [remote(ez.at[7], ez.at[d - 1], sem_ez.at[d - 1], row[d - 1]) for d in range(1, 8)]

    def ex_copies():
        return [remote(ex.at[3], ex.at[d - 1], sem_ex.at[d - 1], slabs[d - 1]) for d in (1, 2, 3)]

    def ey_copies():
        return [remote(ey.at[3], ey.at[d - 1], sem_ey.at[d - 1], column[d - 1]) for d in (1, 2, 3)]

    def err_start():
        total = jnp.zeros((8, LANE), F32)
        for k in range(2):
            for i in range(2):
                cell = k * HALF + core * 8 + chip * 2 + i
                total = total + scatter(err[k * 2 + i], [ix * 32 + ozb[0, s * SEG + cell] for s in range(NSEG)])
        ez[7] = total
        ex[3] = scatter(err[4], [oxb[0, ix * 8 + s] * 8 + iz for s in range(8)])
        for c in ez_copies() + ex_copies():
            c.start()

    def err_middle():
        for c in ez_copies() + ex_copies():
            c.wait_recv()
        total = ez[7] + ex[3]
        for d in range(7):
            total = total + ez[d]
        for d in range(3):
            total = total + ex[d]
        ey[3] = total
        for c in ey_copies():
            c.start()

    def err_finish():
        for c in ey_copies():
            c.wait_recv()
        total = ey[0] + ey[1] + ey[2] + ey[3]
        mine = jnp.where(lane == ix * 32 + iy * 8 + iz, total, 0.0)
        owned[0, 0] = jnp.sum(mine) * share

    for i in range(3):
        xc[i] = jnp.zeros_like(xc[i])
    xc[3] = jnp.ones_like(xc[3])

    def clear(m, _):
        for f in range(4):
            zc[m, f] = jnp.full((8, 256), float(f == 3), F32)
        return 0

    lax.fori_loop(0, SEG, clear, 0)
    tab_copy.wait()
    load.wait(0)
    for part in range(2):
        upsample_part(ebuf, sbuf, 0, tab, fine0, part)

    def pair_of_steps(i, _):
        for b, (fine, ahead) in enumerate(((fine0, fine1), (fine1, fine0))):
            t = i * 2 + b

            @pl.when(t + 1 < STEPS)
            def _():
                load.wait(t + 1)

            forward_scan(
                fine, zc, xc, t // NZG, t % NZG,
                lambda part: upsample_part(ebuf, sbuf, t + 1, tab, ahead, part),
            )

        @pl.when(i == 3)
        def _():
            pl.semaphore_wait(barrier, 13)
            sib_copy(0).start()

        @pl.when(i == 4)
        def _():
            z_compose(0)

        return 0

    lax.fori_loop(0, STEPS // 2, pair_of_steps, 0)
    sib_copy(1).start()
    x_compose()
    for c in late:
        c.wait()

    def widen(c, _):
        r = jnp.dot(tzb[c], perm[...], preferred_element_type=F32)
        for h in range(2):
            for s in range(NSEG):
                tzf[c, h, pl.ds(s * (SEG + 4), SEG), :] = r[s * SEG : (s + 1) * SEG, half(h)]
        txf[c] = jnp.dot(txb[c], perm[...], preferred_element_type=F32)
        return 0

    lax.fori_loop(0, 3, widen, 0)
    z_merge(0)
    z_compose(1)
    for part in range(2):
        upsample_part(ebuf, sbuf, 0, tab_back, fine0, part)
    zcar[0] = jnp.ones_like(zcar[0])
    xcar[0] = jnp.ones_like(xcar[0])
    x_merge()
    z_split(0)
    z_merge(1)
    err_start()
    x_split()
    xcar[1] = cox[3]
    fin_copy(0).wait_recv()
    coz[0, other] = finr[0]
    zcar[1] = coz[0, :, 3]

    def stores(t):
        return store_copies(eout, sout, ge0_hbm, gs0_hbm, sem_out, t)

    def store(t):
        for c in stores(t):
            c.start()

    def state_copy(i):
        rows = pl.ds(pl.multiple_of(i * 2 * ZG * NSEG, 2 * ZG * NSEG), 2 * ZG * NSEG)
        return pltpu.make_async_copy(xcar.at[:, :, rows, :], xst_hbm.at[:, :, rows, :], sem_xst.at[i])

    def after(i):
        state_copy(i).start()

        @pl.when(i == 1)
        def _():
            z_split(1)
            mine_copy.start()
            err_middle()

    backward_steps(
        lambda t: None, after, store, ebuf, sbuf, tab_back, (fine0, fine1), (coarse0, coarse1),
        eout, sout, zcar, xcar, coz.at[0], cox,
    )
    fin_copy(1).wait_recv()
    other_copy.start()
    err_finish()
    for k in range(2):
        for c in [sib_copy(k)] + chip_copies(k) + rep_copies(k) + [fin_copy(k)]:
            c.wait_send()
    for c in x_copies() + xr_copies() + ez_copies() + ex_copies() + ey_copies():
        c.wait_send()
    for c in (mine_copy, other_copy, cox_copy):
        c.wait()

    def finish(t, _):
        for c in stores(t):
            c.wait()
        return 0

    lax.fori_loop(0, NZG, finish, 0)
    for i in range(NZG // 2):
        state_copy(i).wait()


def project_down(even, odd, third):
    return even + third * odd + pltpu.roll(odd + third * even, LANE - 1, axis=1)


def backward_scan(fine, zcar, xcar, coz, cox, coarse, zg, pair, third):
    planes = [pair * 2 + i for i in range(2)]
    rows = [pl.ds(pl.multiple_of((zg * ZG + z) * NSEG, NSEG), NSEG) for z in planes]
    carry = [[[xcar[i, h, r, :] for i in range(2)] for h in range(2)] for r in rows]
    gx = [[[cox[c, h, r, :] for c in range(3)] for h in range(2)] for r in rows]
    for xm in range(HALF):
        z_carry = [[zcar[i, xm, :, half(h)] for i in range(2)] for h in range(2)]
        gz = [[coz[xm, c, :, half(h)] for c in range(3)] for h in range(2)]
        for n, z in enumerate(planes):
            out = [[None] * 2 for _ in range(4)]
            for h in range(2):
                e0, e1, e2, sg = [fine[f, z, h, pl.ds(xm, NSEG, stride=PITCH), :] for f in range(4)]
                g0, g1, g2 = gz[h]
                t_z, a_z = z_carry[h]
                t_new = t_z * jnp.exp2(sg)
                share_z = t_z - t_new
                inner = g0 * e0 + g1 * e1 + g2 * e2
                a_z = a_z + share_z * inner
                grad = t_new * inner + a_z
                z_carry[h] = [t_new, a_z]
                h0, h1, h2 = gx[n][h]
                t_x, a_x = carry[n][h]
                t_new = t_x * jnp.exp2(sg * 0.25)
                share_x = t_x - t_new
                q0, q1, q2 = [cox[4 + c, h, rows[n], :] for c in range(3)]
                inner = q0 * e0 + q1 * e1 + q2 * e2
                a_x = a_x + share_x * inner
                out[3][h] = (grad + a_x) + t_new * inner
                carry[n][h] = [t_new, a_x]
                out[0][h] = g0 * share_z + h0 * share_x
                out[1][h] = g1 * share_z + h1 * share_x
                out[2][h] = g2 * share_z + h2 * share_x
            for f in range(4):
                coarse[f, z, pl.ds(xm, NSEG, stride=PITCH), :] = project_down(out[f][0], out[f][1], third)
        for h in range(2):
            for i in range(2):
                zcar[i, xm, :, half(h)] = z_carry[h][i]
    for n, r in enumerate(rows):
        for h in range(2):
            for i in range(2):
                xcar[i, h, r, :] = carry[n][h][i]


def narrow_part(coarse, eout, sout, t, part):
    for z in (2 * part, 2 * part + 1):
        for f in range(4):
            for s in range(NSEG):
                v = coarse[f, z, pl.ds(s * PITCH, HALF), :].astype(BF16)
                if f == 3:
                    sout[t, z, s] = v
                else:
                    eout[t, f, z, s] = v


def lane_third():
    return jnp.where(lax.broadcasted_iota(jnp.int32, (NSEG, LANE), 1) == 0, 0.0, 1.0 / 3.0)


def backward_steps(ahead_wait, after, store, ebuf, sbuf, tab, fines, coarses, eout, sout, zcar, xcar, coz, cox):
    third = lane_third()
    fine0, fine1 = fines
    coarse0, coarse1 = coarses

    def pair_of_steps(i, _):
        for b, (fine, ahead, new, old) in enumerate(((fine0, fine1, coarse0, coarse1), (fine1, fine0, coarse1, coarse0))):
            t = i * 2 + b
            ahead_wait(t + 1)
            for part in range(2):
                upsample_part(ebuf, sbuf, t + 1, tab, ahead, part)
                narrow_part(old, eout, sout, lax.rem(t + NZG, NZG + 1), part)
                backward_scan(fine, zcar, xcar, coz, cox, new, t, part, third)

            @pl.when(t > 0)
            def _():
                store(t - 1)

        after(i)
        return 0

    lax.fori_loop(0, NZG // 2, pair_of_steps, 0)
    for part in range(2):
        narrow_part(coarse1, eout, sout, NZG - 1, part)
    store(NZG - 1)


def store_copies(eout, sout, ge, gs, sems, t):
    zr = pl.ds(t * ZG, ZG)
    return (
        pltpu.make_async_copy(eout.at[t], ge.at[:, zr], sems.at[t, 0]),
        pltpu.make_async_copy(sout.at[t], gs.at[zr], sems.at[t, 1]),
    )


def backward_kernel(
    e_hbm, s_hbm, tab_hbm, coz_hbm, cox_hbm, xst_hbm, ge0_hbm, gs0_hbm,
    ge_hbm, gs_hbm,
    ebuf, sbuf, fine0, fine1, tab, coarse0, coarse1,
    eout, sout, zcar, xcar, coz, cox, epass, spass,
    in_sem, out_sem, tab_sem, co_sem, hand_sem, pass_sem, on_sem,
):
    load = Loader(e_hbm, s_hbm, ebuf, sbuf, in_sem, NZG)
    tab_copy = pltpu.make_async_copy(tab_hbm, tab, tab_sem)
    coz_copy = pltpu.make_async_copy(coz_hbm, coz, co_sem)

    def handed(t):
        rows = pl.ds(pl.multiple_of(t * ZG * NSEG, ZG * NSEG), ZG * NSEG)
        return load.copies(t) + (
            pltpu.make_async_copy(cox_hbm.at[:, :, rows, :], cox.at[:, :, rows, :], hand_sem.at[t, 0]),
            pltpu.make_async_copy(xst_hbm.at[:, :, rows, :], xcar.at[:, :, rows, :], hand_sem.at[t, 1]),
        )

    def begin(t, _):
        for c in handed(t):
            c.start()
        return 0

    def fetches(t):
        zr = pl.ds(t * ZG, ZG)
        return (
            pltpu.make_async_copy(ge0_hbm.at[:, zr], epass.at[t], pass_sem.at[t, 0]),
            pltpu.make_async_copy(gs0_hbm.at[zr], spass.at[t], pass_sem.at[t, 1]),
        )

    def passes(t):
        xr = pl.ds(0, HALF)
        return store_copies(epass, spass, ge_hbm.at[:, :, :, xr, :], gs_hbm.at[:, :, xr, :], on_sem, t)

    tab_copy.start()
    begin(0, 0)
    coz_copy.start()
    lax.fori_loop(1, NZG, begin, 0)

    def fetch(t, _):
        for c in fetches(t):
            c.start()
        return 0

    lax.fori_loop(0, NZG, fetch, 0)

    def stores(t):
        xr = pl.ds(HALF, HALF)
        return store_copies(eout, sout, ge_hbm.at[:, :, :, xr, :], gs_hbm.at[:, :, xr, :], out_sem, t)

    def store(t):
        for c in stores(t):
            c.start()
        for c in fetches(t):
            c.wait()
        for c in passes(t):
            c.start()

    def ahead_wait(t):
        @pl.when(t < NZG)
        def _():
            for c in handed(t):
                c.wait()

    zcar[0] = jnp.ones_like(zcar[0])
    tab_copy.wait()
    load.wait(0)
    for part in range(2):
        upsample_part(ebuf, sbuf, 0, tab, fine0, part)
    for c in handed(0)[2:]:
        c.wait()
    coz_copy.wait()
    zcar[1] = coz[:, 3]
    backward_steps(
        ahead_wait, lambda i: None, store, ebuf, sbuf, tab, (fine0, fine1), (coarse0, coarse1),
        eout, sout, zcar, xcar, coz, cox,
    )

    def finish(t, _):
        for c in stores(t) + passes(t):
            c.wait()
        return 0

    lax.fori_loop(0, NZG, finish, 0)


def vmem(*shape, dtype=F32):
    return pltpu.VMEM(shape, dtype)


HBM = pl.BlockSpec(memory_space=pltpu.HBM)


def local(emission, absorption, target_z, target_x, owner_z, owner_x):
    depth_z, width_x, width_y = absorption.shape
    pixels = 2 * width_y
    count_x = lax.axis_size("gx")
    count_y = lax.axis_size("gy")
    count_z = lax.axis_size("gz")
    step_z = OPTICAL / (depth_z * count_z)
    step_x = OPTICAL / (width_x * count_x)
    interp = interp_table(width_y)
    rate = interp.T * (-step_z * math.log2(math.e))
    order = np.concatenate([np.arange(0, pixels, 2), np.roll(np.arange(1, pixels, 2), 1)])
    rate_hi = rate.astype(BF16)
    rate_lo = (rate - rate_hi.astype(np.float64)).astype(BF16)
    tab = np.concatenate([interp.T.astype(BF16), rate_hi, rate_lo], axis=0)[:, order]
    tab_back = np.concatenate([(interp.T * step_z).astype(BF16), rate_hi, rate_lo], axis=0)[:, order]
    perm = np.eye(pixels)[:, order].astype(BF16)
    slots = 2 * width_x // (count_y * count_z) + 2 * depth_z // (count_x * count_y)
    e5 = emission.reshape(3, depth_z, NSEG, SEG, width_y)
    s4 = absorption.reshape(depth_z, NSEG, SEG, width_y)

    def buffers(steps):
        return [
            vmem(steps + 1, 3, ZG, NSEG, HALF, LANE, dtype=BF16), vmem(steps + 1, ZG, NSEG, HALF, LANE, dtype=BF16),
            vmem(4, ZG, 2, NSEG * PITCH, LANE), vmem(4, ZG, 2, NSEG * PITCH, LANE),
        ]

    back_buffers = [
        vmem(3 * LANE, 256, dtype=BF16), vmem(4, ZG, NSEG * PITCH, LANE), vmem(4, ZG, NSEG * PITCH, LANE),
        vmem(NZG + 1, 3, ZG, NSEG, HALF, LANE, dtype=BF16), vmem(NZG + 1, ZG, NSEG, HALF, LANE, dtype=BF16),
        vmem(2, HALF, NSEG, 256), vmem(2, 2, NZ * NSEG, LANE),
    ]
    dma = pltpu.SemaphoreType.DMA
    coz, cox, xst, ge0, gs0, owned = pl.pallas_call(
        functools.partial(forward_kernel, step_z, step_x, 1.0 / (3.0 * pixels * slots)),
        out_shape=[
            jax.ShapeDtypeStruct((HALF, 4, NSEG, 256), F32),
            jax.ShapeDtypeStruct((7, 2, NZ * NSEG, LANE), F32),
            jax.ShapeDtypeStruct((2, 2, NZ * NSEG, LANE), F32),
            jax.ShapeDtypeStruct((3, NZ, NSEG, HALF, LANE), BF16),
            jax.ShapeDtypeStruct((NZ, NSEG, HALF, LANE), BF16),
            jax.ShapeDtypeStruct((1, 1), F32),
        ],
        in_specs=[HBM] * 9,
        out_specs=[HBM] * 5 + [pl.BlockSpec(memory_space=pltpu.SMEM)],
        scratch_shapes=buffers(STEPS) + [
            vmem(SEG, 4, NSEG, 256), vmem(4, 2, NZ * NSEG, LANE), vmem(2, HALF, 4, NSEG, 256), vmem(7, 2, NZ * NSEG, LANE),
        ] + back_buffers + [
            vmem(3, 256, 256, dtype=BF16), vmem(3, NZ, 256, dtype=BF16),
            vmem(3, 2, NSEG * (SEG + 4), LANE), vmem(3, NZ, 256),
            vmem(2, 8, 4, 8, 256), vmem(2, 8, 4, 8, 256), vmem(2, 4, 2, 4, 8, 256), vmem(2, 4, 2, 4, 8, 256),
            vmem(2, 8, 4, 8, 256), vmem(2, 8, 4, 8, 256), vmem(2, 8, 4, 8, 256),
            vmem(4, 4, 8, 256), vmem(4, 4, 8, 256), vmem(4, 4, 8, 256), vmem(4, 4, 8, 256), vmem(NSEG, 8, LANE),
            vmem(3 * LANE, 256, dtype=BF16), vmem(256, 256, dtype=BF16), vmem(5, 8, LANE),
            pltpu.SMEM((1, 256), jnp.int32), pltpu.SMEM((1, NZ), jnp.int32),
            vmem(8, 8, LANE), vmem(4, 8, LANE), vmem(4, 8, LANE),
            dma((STEPS, 2)), dma((7,)), dma((2, 2)), dma((2, 3, 2)), dma((2, 3, 2)), dma((2, 2)), dma((3, 2)), dma((3, 2)),
            dma((7, 2)), dma((3, 2)), dma((3, 2)), dma((3,)), dma((NZG, 2)), dma((NZG // 2,)),
        ],
        compiler_params=pltpu.CompilerParams(
            collective_id=0, has_side_effects=True, vmem_limit_bytes=VMEM_LIMIT
        ),
    )(
        e5, s4, target_z, target_x, owner_z.reshape(count_x, count_y, 1, width_x),
        owner_x.reshape(count_y, count_z, 1, depth_z), tab, perm, tab_back,
    )

    grad_e, grad_s = pl.pallas_call(
        backward_kernel,
        out_shape=[jax.ShapeDtypeStruct(e5.shape, BF16), jax.ShapeDtypeStruct(s4.shape, BF16)],
        in_specs=[HBM] * 8,
        out_specs=[HBM, HBM],
        scratch_shapes=buffers(NZG) + back_buffers + [
            vmem(HALF, 4, NSEG, 256), vmem(7, 2, NZ * NSEG, LANE),
            vmem(NZG, 3, ZG, NSEG, HALF, LANE, dtype=BF16), vmem(NZG, ZG, NSEG, HALF, LANE, dtype=BF16),
            dma((NZG, 2)), dma((NZG, 2)), dma(()), dma(()), dma((NZG, 2)), dma((NZG, 2)), dma((NZG, 2)),
        ],
        compiler_params=pltpu.CompilerParams(vmem_limit_bytes=VMEM_LIMIT),
        cost_estimate=pl.CostEstimate(flops=6 * 10**9, bytes_accessed=20 * 2**20, transcendentals=0),
    )(e5, s4, tab_back, coz, cox, xst, ge0, gs0)
    return (grad_e.reshape(emission.shape), grad_s.reshape(absorption.shape), owned.reshape(1, 1, 1))


def solution(mesh):
    return jax.shard_map(
        local,
        mesh=mesh,
        in_specs=(P(None, "gz", "gx", "gy"), P("gz", "gx", "gy"), P(), P(), P(), P()),
        out_specs=(P(None, "gz", "gx", "gy"), P("gz", "gx", "gy"), P("gx", "gy", "gz")),
        check_vma=False,
    )
```

```python
import functools
import math

import jax
import jax.numpy as jnp
import numpy as np
from jax import lax
from jax.experimental import pallas as pl
from jax.experimental.pallas import tpu as pltpu
from jax.sharding import PartitionSpec as P

F32 = jnp.float32
BF16 = jnp.bfloat16
OPTICAL = 1.5
BACKLIGHT = 1.0

NSEG = 8
SEG = 32
HALF = 16
PITCH = 20
ZG = 4
NZ = 32
NZG = NZ // ZG
STEPS = 2 * NZG
LANE = 128
VMEM_LIMIT = 61 * 2**20 + 2**19


def interp_table(width):
    pixels = np.arange(2 * width)
    nearest = pixels // 2
    second = np.clip(nearest + 2 * (pixels % 2) - 1, 0, width - 1)
    columns = np.arange(width)
    return 0.75 * (columns[None, :] == nearest[:, None]) + 0.25 * (columns[None, :] == second[:, None])


def half(h):
    return slice(h * LANE, (h + 1) * LANE)


def upsample_store(fine, f, z, r):
    for s in range(NSEG):
        for h in range(2):
            fine[f, z, h, s * PITCH : s * PITCH + HALF] = r[s * HALF : (s + 1) * HALF, half(h)]


def upsample_part(ebuf, sbuf, t, tab, fine, part):
    rows = NSEG * HALF
    if part == 0:
        a = ebuf[t, 0:2].reshape(2 * ZG * rows, LANE)
        r = jnp.dot(a, tab[0:LANE], preferred_element_type=F32)
        for f in range(2):
            for z in range(ZG):
                i = f * ZG + z
                upsample_store(fine, f, z, r[i * rows : (i + 1) * rows])
    else:
        r = jnp.dot(ebuf[t, 2].reshape(ZG * rows, LANE), tab[0:LANE], preferred_element_type=F32)
        s = sbuf[t].reshape(ZG * rows, LANE)
        q = jnp.dot(jnp.concatenate([s, s], axis=1), tab[LANE:], preferred_element_type=F32)
        for z in range(ZG):
            upsample_store(fine, 2, z, r[z * rows : (z + 1) * rows])
            upsample_store(fine, 3, z, q[z * rows : (z + 1) * rows])


class Loader:
    def __init__(self, e_hbm, s_hbm, ebuf, sbuf, sems, base):
        self.refs = (e_hbm, s_hbm, ebuf, sbuf, sems)
        self.base = base

    def copies(self, t):
        e_hbm, s_hbm, ebuf, sbuf, sems = self.refs
        k, zg = (self.base + t) // NZG, (self.base + t) % NZG
        zs, xs = pl.ds(zg * ZG, ZG), pl.ds(pl.multiple_of(k * HALF, HALF), HALF)
        return (
            pltpu.make_async_copy(e_hbm.at[:, zs, :, xs, :], ebuf.at[t], sems.at[t, 0]),
            pltpu.make_async_copy(s_hbm.at[zs, :, xs, :], sbuf.at[t], sems.at[t, 1]),
        )

    def start(self, first, end):
        def one(t, _):
            for c in self.copies(t):
                c.start()
            return 0

        lax.fori_loop(first, end, one, 0)

    def wait(self, t):
        for c in self.copies(t):
            c.wait()


def forward_scan(fine, zc, xc, k, zg, extra):
    for h in range(2):
        hs = half(h)
        rows = [pl.ds(pl.multiple_of((zg * ZG + z) * NSEG, NSEG), NSEG) for z in range(ZG)]
        carry = [[xc[i, h, r, :] for i in range(4)] for r in rows]
        extra(h)
        for xm in range(HALF):
            zr = k * HALF + xm
            c0, c1, c2, t_z = [zc[zr, i, :, hs] for i in range(4)]
            for z in range(ZG):
                e0, e1, e2, sg = [fine[f, z, h, pl.ds(xm, NSEG, stride=PITCH), :] for f in range(4)]
                t_new = t_z * jnp.exp2(sg)
                share = t_z - t_new
                t_z = t_new
                c0 = c0 + share * e0
                c1 = c1 + share * e1
                c2 = c2 + share * e2
                d0, d1, d2, t_x = carry[z]
                t_new = t_x * jnp.exp2(sg * 0.25)
                share = t_x - t_new
                carry[z] = [d0 + share * e0, d1 + share * e1, d2 + share * e2, t_new]
            for i, v in enumerate((c0, c1, c2, t_z)):
                zc[zr, i, :, hs] = v
        for z in range(ZG):
            for i in range(4):
                xc[i, h, rows[z], :] = carry[z][i]


def compose(front, back):
    c0, c1, c2, t = front
    d0, d1, d2, u = back
    return (c0 + t * d0, c1 + t * d1, c2 + t * d2, t * u)


def merge(bricks, target, inv_step):
    ahead = (jnp.zeros_like(target[0]),) * 3 + (jnp.ones_like(target[0]),)
    fronts = []
    for brick in bricks:
        fronts.append(ahead[3])
        ahead = compose(ahead, brick)
    resid = [ahead[c] + ahead[3] * BACKLIGHT - target[c] for c in range(3)]
    g = [r * inv_step for r in resid]
    behind = [jnp.full_like(target[0], BACKLIGHT)] * 3
    replies = []
    for front, brick in reversed(list(zip(fronts, bricks))):
        dot = g[0] * behind[0] + g[1] * behind[1] + g[2] * behind[2]
        replies.append([front * g[0], front * g[1], front * g[2], front * dot])
        behind = [brick[c] + brick[3] * behind[c] for c in range(3)]
    replies.reverse()
    return replies, resid[0] * resid[0] + resid[1] * resid[1] + resid[2] * resid[2]


def forward_kernel(
    step_z, step_x, share,
    e_hbm, s_hbm, tz_hbm, tx_hbm, oz_hbm, ox_hbm, tab_hbm, perm_hbm, back_hbm,
    coz_hbm, cox_hbm, xst_hbm, ge0_hbm, gs0_hbm, owned,
    ebuf, sbuf, fine0, fine1, zc, xc, coz, cox,
    tab_back, coarse0, coarse1, eout, sout, zcar, xcar,
    tzb, txb, tzf, txf,
    sib, pc, got, rep, back, fin, finr,
    xloc, xgot, xrep, xback, xsuf,
    tab, perm, err, ozb, oxb, ez, ex, ey,
    in_sem, t_sem, sem_sib, sem_chip, sem_rep, sem_fin, sem_x, sem_xr, sem_ez, sem_ex, sem_ey, sem_co, sem_out, sem_xst,
):
    ix, iy, iz = lax.axis_index("gx"), lax.axis_index("gy"), lax.axis_index("gz")
    chip, core = iz // 2, iz % 2
    load = Loader(e_hbm, s_hbm, ebuf, sbuf, in_sem, 0)
    tab_copy = pltpu.make_async_copy(tab_hbm, tab, t_sem.at[4])
    tab_copy.start()
    load.start(0, STEPS)
    lane = lax.broadcasted_iota(jnp.int32, (8, LANE), 1)
    sub = lax.broadcasted_iota(jnp.int32, (8, LANE), 0)
    weight = jnp.where(lane == 0, 1.0, 0.75)
    px = pl.ds(pl.multiple_of(iy * 256, 256), 256)
    tz_copy = pltpu.make_async_copy(tz_hbm.at[:, pl.ds(pl.multiple_of(ix * 256, 256), 256), px], tzb, t_sem.at[0])
    tx_copy = pltpu.make_async_copy(tx_hbm.at[:, pl.ds(pl.multiple_of(iz * NZ, NZ), NZ), px], txb, t_sem.at[1])
    oz_copy = pltpu.make_async_copy(oz_hbm.at[ix, iy], ozb, t_sem.at[2])
    ox_copy = pltpu.make_async_copy(ox_hbm.at[iy, iz], oxb, t_sem.at[3])
    perm_copy = pltpu.make_async_copy(perm_hbm, perm, t_sem.at[5])
    back_copy = pltpu.make_async_copy(back_hbm, tab_back, t_sem.at[6])
    late = (tz_copy, tx_copy, oz_copy, ox_copy, perm_copy, back_copy)
    for c in late:
        c.start()

    sibling = {"gz": chip * 2 + 1 - core}
    chips = [{"gz": lax.rem(chip + d, 4) * 2 + core} for d in (1, 2, 3)]
    slabs = [{"gx": lax.rem(ix + d, 4)} for d in (1, 2, 3)]
    barrier = pltpu.get_barrier_semaphore()
    row = [{"gz": lax.rem(iz + d, 8)} for d in range(1, 8)]
    column = [{"gy": lax.rem(iy + d, 4)} for d in (1, 2, 3)]
    for peer in row + slabs + column:
        pl.semaphore_signal(barrier, inc=1, device_id=peer, device_id_type=pl.DeviceIdType.MESH)

    def remote(src, dst, sems, peer):
        return pltpu.make_async_remote_copy(
            src_ref=src, dst_ref=dst, send_sem=sems.at[0], recv_sem=sems.at[1],
            device_id=peer, device_id_type=pl.DeviceIdType.MESH,
        )

    def sib_copy(k):
        return remote(zc.at[pl.ds(k * HALF + (1 - core) * 8, 8)], sib.at[k], sem_sib.at[k], sibling)

    def chip_copies(k):
        return [
            remote(pc.at[k, pl.ds(lax.rem(chip + d, 4) * 2, 2)], got.at[k, chip], sem_chip.at[k, d - 1], chips[d - 1])
            for d in (1, 2, 3)
        ]

    def rep_copies(k):
        return [
            remote(rep.at[k, lax.rem(chip + d, 4)], back.at[k, pl.ds(chip * 2, 2)], sem_rep.at[k, d - 1], chips[d - 1])
            for d in (1, 2, 3)
        ]

    def fin_copy(k):
        return remote(fin.at[k], finr.at[k], sem_fin.at[k], sibling)

    def x_copies():
        return [remote(xloc.at[lax.rem(ix + d, 4)], xgot.at[ix], sem_x.at[d - 1], slabs[d - 1]) for d in (1, 2, 3)]

    def xr_copies():
        return [remote(xrep.at[lax.rem(ix + d, 4)], xback.at[ix], sem_xr.at[d - 1], slabs[d - 1]) for d in (1, 2, 3)]

    def pair(k, m, hs):
        mine = [zc[k * HALF + core * 8 + m, i, :, hs] for i in range(4)]
        other = [sib[k, m, i, :, hs] for i in range(4)]
        first = core == 0
        return [jnp.where(first, a, b) for a, b in zip(mine, other)], [jnp.where(first, b, a) for a, b in zip(mine, other)]

    def z_compose(k):
        sib_copy(k).wait_recv()

        def body(m, _):
            for h in range(2):
                front, rear = pair(k, m, half(h))
                for i, v in enumerate(compose(front, rear)):
                    pc[k, m, i, :, half(h)] = v
            return 0

        def four(n, _):
            for u in range(4):
                body(n * 4 + u, 0)
            return 0

        lax.fori_loop(0, 2, four, 0)
        for c in chip_copies(k):
            c.start()

    def z_merge(k):
        for c in chip_copies(k):
            c.wait_recv()
        for i in range(2):
            m = chip * 2 + i
            got[k, chip, i] = pc[k, m]
            sq = jnp.zeros((8, LANE), F32)
            for h in range(2):
                bricks = [[got[k, o, i, f, :, half(h)] for f in range(4)] for o in range(4)]
                row = k * HALF + core * 8 + m
                target = [tzf[c, h, pl.ds(row, NSEG, stride=SEG + 4), :] for c in range(3)]
                replies, s = merge(bricks, target, weight * (1.0 / step_z))
                sq = sq + s
                for o in range(4):
                    for f in range(4):
                        rep[k, o, i, f, :, half(h)] = replies[o][f]
            err[k * 2 + i] = sq
        for c in rep_copies(k):
            c.start()
        back[k, pl.ds(chip * 2, 2)] = rep[k, chip]

    def z_split(k):
        for c in rep_copies(k):
            c.wait_recv()

        def body(m, _):
            for h in range(2):
                hs = half(h)
                a, b = pair(k, m, hs)
                g0, g1, g2, gt = [back[k, m, f, :, hs] for f in range(4)]
                inner_b = g0 * b[0] + g1 * b[1] + g2 * b[2] + gt * b[3]
                k_b = -(a[3] * inner_b)
                k_a = k_b - (g0 * a[0] + g1 * a[1] + g2 * a[2])
                part_a = (g0, g1, g2, k_a * step_z)
                part_b = (a[3] * g0, a[3] * g1, a[3] * g2, k_b * step_z)
                first = core == 0
                for f in range(4):
                    coz[k, core * 8 + m, f, :, hs] = jnp.where(first, part_a[f], part_b[f])
                    fin[k, m, f, :, hs] = jnp.where(first, part_b[f], part_a[f])
            return 0

        def four(n, _):
            for u in range(4):
                body(n * 4 + u, 0)
            return 0

        lax.fori_loop(0, 2, four, 0)
        fin_copy(k).start()

    mine, other = pl.ds(core * 8, 8), pl.ds((1 - core) * 8, 8)
    mine_copy = pltpu.make_async_copy(coz.at[1, mine], coz_hbm.at[mine], sem_co.at[0])
    other_copy = pltpu.make_async_copy(finr.at[1], coz_hbm.at[other], sem_co.at[1])

    def x_compose():
        for g in range(4):
            for h in range(2):
                acc = None
                for s in range(NSEG):
                    rows = pl.ds(g * 64 + s, 8, stride=NSEG)
                    seg = tuple(xc[i, h, rows, :] for i in range(4))
                    acc = seg if acc is None else compose(acc, seg)
                for f in range(4):
                    xloc[g, f, :, half(h)] = acc[f]
        for c in x_copies():
            c.start()

    def x_merge():
        for c in x_copies():
            c.wait_recv()
        xgot[ix] = xloc[ix]
        sq = jnp.zeros((8, LANE), F32)
        for h in range(2):
            bricks = [[xgot[o, f, :, half(h)] for f in range(4)] for o in range(4)]
            target = [txf[c, pl.ds(pl.multiple_of(ix * 8, 8), 8), half(h)] for c in range(3)]
            replies, s = merge(bricks, target, weight * (1.0 / step_x))
            sq = sq + s
            for o in range(4):
                for f in range(4):
                    xrep[o, f, :, half(h)] = replies[o][f]
        err[4] = sq
        for c in xr_copies():
            c.start()
        xback[ix] = xrep[ix]

    cox_copy = pltpu.make_async_copy(cox, cox_hbm, sem_co.at[2])

    def x_split():
        for c in xr_copies():
            c.wait_recv()
        for g in range(4):
            for h in range(2):
                g0, g1, g2, gt = [xback[g, f, :, half(h)] for f in range(4)]
                suffix = None
                for s in reversed(range(NSEG)):
                    rows = pl.ds(g * 64 + s, 8, stride=NSEG)
                    seg = tuple(xc[i, h, rows, :] for i in range(4))
                    suffix = seg if suffix is None else compose(seg, suffix)
                    xsuf[s] = g0 * suffix[0] + g1 * suffix[1] + g2 * suffix[2] + gt * suffix[3]
                front = jnp.ones((8, LANE), F32)
                for s in range(NSEG):
                    rows = pl.ds(g * 64 + s, 8, stride=NSEG)
                    for c, colour in enumerate((g0, g1, g2)):
                        v = front * colour
                        cox[c, h, rows, :] = v
                        cox[4 + c, h, rows, :] = 0.25 * v
                    cox[3, h, rows, :] = front * xsuf[s] * (-step_x)
                    front = front * xc[3, h, rows, :]
        cox_copy.start()

    def scatter(sq, ids):
        owner = jnp.zeros((8, LANE), jnp.int32)
        for s, o in enumerate(ids):
            owner = jnp.where(sub == s, o, owner)
        return jnp.where(lane == owner, jnp.sum(sq, axis=1, keepdims=True), 0.0)

    def ez_copies():
        return [remote(ez.at[7], ez.at[d - 1], sem_ez.at[d - 1], row[d - 1]) for d in range(1, 8)]

    def ex_copies():
        return [remote(ex.at[3], ex.at[d - 1], sem_ex.at[d - 1], slabs[d - 1]) for d in (1, 2, 3)]

    def ey_copies():
        return [remote(ey.at[3], ey.at[d - 1], sem_ey.at[d - 1], column[d - 1]) for d in (1, 2, 3)]

    def err_start():
        total = jnp.zeros((8, LANE), F32)
        for k in range(2):
            for i in range(2):
                cell = k * HALF + core * 8 + chip * 2 + i
                total = total + scatter(err[k * 2 + i], [ix * 32 + ozb[0, s * SEG + cell] for s in range(NSEG)])
        ez[7] = total
        ex[3] = scatter(err[4], [oxb[0, ix * 8 + s] * 8 + iz for s in range(8)])
        for c in ez_copies() + ex_copies():
            c.start()

    def err_middle():
        for c in ez_copies() + ex_copies():
            c.wait_recv()
        total = ez[7] + ex[3]
        for d in range(7):
            total = total + ez[d]
        for d in range(3):
            total = total + ex[d]
        ey[3] = total
        for c in ey_copies():
            c.start()

    def err_finish():
        for c in ey_copies():
            c.wait_recv()
        total = ey[0] + ey[1] + ey[2] + ey[3]
        mine = jnp.where(lane == ix * 32 + iy * 8 + iz, total, 0.0)
        owned[0, 0] = jnp.sum(mine) * share

    for i in range(3):
        xc[i] = jnp.zeros_like(xc[i])
    xc[3] = jnp.ones_like(xc[3])

    def clear(m, _):
        for f in range(4):
            zc[m, f] = jnp.full((8, 256), float(f == 3), F32)
        return 0

    lax.fori_loop(0, SEG, clear, 0)
    tab_copy.wait()
    load.wait(0)
    for part in range(2):
        upsample_part(ebuf, sbuf, 0, tab, fine0, part)

    def pair_of_steps(i, _):
        for b, (fine, ahead) in enumerate(((fine0, fine1), (fine1, fine0))):
            t = i * 2 + b

            @pl.when(t + 1 < STEPS)
            def _():
                load.wait(t + 1)

            forward_scan(
                fine, zc, xc, t // NZG, t % NZG,
                lambda part: upsample_part(ebuf, sbuf, t + 1, tab, ahead, part),
            )

        @pl.when(i == 3)
        def _():
            pl.semaphore_wait(barrier, 13)
            sib_copy(0).start()

        @pl.when(i == 4)
        def _():
            z_compose(0)

        return 0

    lax.fori_loop(0, STEPS // 2, pair_of_steps, 0)
    sib_copy(1).start()
    x_compose()
    for c in late:
        c.wait()

    def widen(c, _):
        r = jnp.dot(tzb[c], perm[...], preferred_element_type=F32)
        for h in range(2):
            for s in range(NSEG):
                tzf[c, h, pl.ds(s * (SEG + 4), SEG), :] = r[s * SEG : (s + 1) * SEG, half(h)]
        txf[c] = jnp.dot(txb[c], perm[...], preferred_element_type=F32)
        return 0

    lax.fori_loop(0, 3, widen, 0)
    z_merge(0)
    z_compose(1)
    for part in range(2):
        upsample_part(ebuf, sbuf, 0, tab_back, fine0, part)
    zcar[0] = jnp.ones_like(zcar[0])
    xcar[0] = jnp.ones_like(xcar[0])
    x_merge()
    z_split(0)
    z_merge(1)
    err_start()
    x_split()
    xcar[1] = cox[3]
    fin_copy(0).wait_recv()
    coz[0, other] = finr[0]
    zcar[1] = coz[0, :, 3]

    def stores(t):
        return store_copies(eout, sout, ge0_hbm, gs0_hbm, sem_out, t)

    def store(t):
        for c in stores(t):
            c.start()

    def state_copy(i):
        rows = pl.ds(pl.multiple_of(i * 2 * ZG * NSEG, 2 * ZG * NSEG), 2 * ZG * NSEG)
        return pltpu.make_async_copy(xcar.at[:, :, rows, :], xst_hbm.at[:, :, rows, :], sem_xst.at[i])

    def after(i):
        state_copy(i).start()

        @pl.when(i == 1)
        def _():
            z_split(1)
            mine_copy.start()
            err_middle()

    backward_steps(
        lambda t: None, after, store, ebuf, sbuf, tab_back, (fine0, fine1), (coarse0, coarse1),
        eout, sout, zcar, xcar, coz.at[0], cox,
    )
    fin_copy(1).wait_recv()
    other_copy.start()
    err_finish()
    for k in range(2):
        for c in [sib_copy(k)] + chip_copies(k) + rep_copies(k) + [fin_copy(k)]:
            c.wait_send()
    for c in x_copies() + xr_copies() + ez_copies() + ex_copies() + ey_copies():
        c.wait_send()
    for c in (mine_copy, other_copy, cox_copy):
        c.wait()

    def finish(t, _):
        for c in stores(t):
            c.wait()
        return 0

    lax.fori_loop(0, NZG, finish, 0)
    for i in range(NZG // 2):
        state_copy(i).wait()


def project_down(even, odd, third):
    return even + third * odd + pltpu.roll(odd + third * even, LANE - 1, axis=1)


def backward_scan(fine, zcar, xcar, coz, cox, coarse, zg, pair, third):
    planes = [pair * 2 + i for i in range(2)]
    rows = [pl.ds(pl.multiple_of((zg * ZG + z) * NSEG, NSEG), NSEG) for z in planes]
    carry = [[[xcar[i, h, r, :] for i in range(2)] for h in range(2)] for r in rows]
    gx = [[[cox[c, h, r, :] for c in range(3)] for h in range(2)] for r in rows]
    for xm in range(HALF):
        z_carry = [[zcar[i, xm, :, half(h)] for i in range(2)] for h in range(2)]
        gz = [[coz[xm, c, :, half(h)] for c in range(3)] for h in range(2)]
        for n, z in enumerate(planes):
            out = [[None] * 2 for _ in range(4)]
            for h in range(2):
                e0, e1, e2, sg = [fine[f, z, h, pl.ds(xm, NSEG, stride=PITCH), :] for f in range(4)]
                g0, g1, g2 = gz[h]
                t_z, a_z = z_carry[h]
                t_new = t_z * jnp.exp2(sg)
                share_z = t_z - t_new
                inner = g0 * e0 + g1 * e1 + g2 * e2
                a_z = a_z + share_z * inner
                grad = t_new * inner + a_z
                z_carry[h] = [t_new, a_z]
                h0, h1, h2 = gx[n][h]
                t_x, a_x = carry[n][h]
                t_new = t_x * jnp.exp2(sg * 0.25)
                share_x = t_x - t_new
                q0, q1, q2 = [cox[4 + c, h, rows[n], :] for c in range(3)]
                inner = q0 * e0 + q1 * e1 + q2 * e2
                a_x = a_x + share_x * inner
                out[3][h] = (grad + a_x) + t_new * inner
                carry[n][h] = [t_new, a_x]
                out[0][h] = g0 * share_z + h0 * share_x
                out[1][h] = g1 * share_z + h1 * share_x
                out[2][h] = g2 * share_z + h2 * share_x
            for f in range(4):
                coarse[f, z, pl.ds(xm, NSEG, stride=PITCH), :] = project_down(out[f][0], out[f][1], third)
        for h in range(2):
            for i in range(2):
                zcar[i, xm, :, half(h)] = z_carry[h][i]
    for n, r in enumerate(rows):
        for h in range(2):
            for i in range(2):
                xcar[i, h, r, :] = carry[n][h][i]


def narrow_part(coarse, eout, sout, t, part):
    for z in (2 * part, 2 * part + 1):
        for f in range(4):
            for s in range(NSEG):
                v = coarse[f, z, pl.ds(s * PITCH, HALF), :].astype(BF16)
                if f == 3:
                    sout[t, z, s] = v
                else:
                    eout[t, f, z, s] = v


def lane_third():
    return jnp.where(lax.broadcasted_iota(jnp.int32, (NSEG, LANE), 1) == 0, 0.0, 1.0 / 3.0)


def backward_steps(ahead_wait, after, store, ebuf, sbuf, tab, fines, coarses, eout, sout, zcar, xcar, coz, cox):
    third = lane_third()
    fine0, fine1 = fines
    coarse0, coarse1 = coarses

    def pair_of_steps(i, _):
        for b, (fine, ahead, new, old) in enumerate(((fine0, fine1, coarse0, coarse1), (fine1, fine0, coarse1, coarse0))):
            t = i * 2 + b
            ahead_wait(t + 1)
            for part in range(2):
                upsample_part(ebuf, sbuf, t + 1, tab, ahead, part)
                narrow_part(old, eout, sout, lax.rem(t + NZG, NZG + 1), part)
                backward_scan(fine, zcar, xcar, coz, cox, new, t, part, third)

            @pl.when(t > 0)
            def _():
                store(t - 1)

        after(i)
        return 0

    lax.fori_loop(0, NZG // 2, pair_of_steps, 0)
    for part in range(2):
        narrow_part(coarse1, eout, sout, NZG - 1, part)
    store(NZG - 1)


def store_copies(eout, sout, ge, gs, sems, t):
    zr = pl.ds(t * ZG, ZG)
    return (
        pltpu.make_async_copy(eout.at[t], ge.at[:, zr], sems.at[t, 0]),
        pltpu.make_async_copy(sout.at[t], gs.at[zr], sems.at[t, 1]),
    )


def backward_kernel(
    e_hbm, s_hbm, tab_hbm, coz_hbm, cox_hbm, xst_hbm, ge0_hbm, gs0_hbm,
    ge_hbm, gs_hbm,
    ebuf, sbuf, fine0, fine1, tab, coarse0, coarse1,
    eout, sout, zcar, xcar, coz, cox, epass, spass,
    in_sem, out_sem, tab_sem, co_sem, hand_sem, pass_sem, on_sem,
):
    load = Loader(e_hbm, s_hbm, ebuf, sbuf, in_sem, NZG)
    tab_copy = pltpu.make_async_copy(tab_hbm, tab, tab_sem)
    coz_copy = pltpu.make_async_copy(coz_hbm, coz, co_sem)

    def handed(t):
        rows = pl.ds(pl.multiple_of(t * ZG * NSEG, ZG * NSEG), ZG * NSEG)
        return load.copies(t) + (
            pltpu.make_async_copy(cox_hbm.at[:, :, rows, :], cox.at[:, :, rows, :], hand_sem.at[t, 0]),
            pltpu.make_async_copy(xst_hbm.at[:, :, rows, :], xcar.at[:, :, rows, :], hand_sem.at[t, 1]),
        )

    def begin(t, _):
        for c in handed(t):
            c.start()
        return 0

    def fetches(t):
        zr = pl.ds(t * ZG, ZG)
        return (
            pltpu.make_async_copy(ge0_hbm.at[:, zr], epass.at[t], pass_sem.at[t, 0]),
            pltpu.make_async_copy(gs0_hbm.at[zr], spass.at[t], pass_sem.at[t, 1]),
        )

    def passes(t):
        xr = pl.ds(0, HALF)
        return store_copies(epass, spass, ge_hbm.at[:, :, :, xr, :], gs_hbm.at[:, :, xr, :], on_sem, t)

    tab_copy.start()
    begin(0, 0)
    coz_copy.start()
    lax.fori_loop(1, NZG, begin, 0)

    def fetch(t, _):
        for c in fetches(t):
            c.start()
        return 0

    lax.fori_loop(0, NZG, fetch, 0)

    def stores(t):
        xr = pl.ds(HALF, HALF)
        return store_copies(eout, sout, ge_hbm.at[:, :, :, xr, :], gs_hbm.at[:, :, xr, :], out_sem, t)

    def store(t):
        for c in stores(t):
            c.start()
        for c in fetches(t):
            c.wait()
        for c in passes(t):
            c.start()

    def ahead_wait(t):
        @pl.when(t < NZG)
        def _():
            for c in handed(t):
                c.wait()

    zcar[0] = jnp.ones_like(zcar[0])
    tab_copy.wait()
    load.wait(0)
    for part in range(2):
        upsample_part(ebuf, sbuf, 0, tab, fine0, part)
    for c in handed(0)[2:]:
        c.wait()
    coz_copy.wait()
    zcar[1] = coz[:, 3]
    backward_steps(
        ahead_wait, lambda i: None, store, ebuf, sbuf, tab, (fine0, fine1), (coarse0, coarse1),
        eout, sout, zcar, xcar, coz, cox,
    )

    def finish(t, _):
        for c in stores(t) + passes(t):
            c.wait()
        return 0

    lax.fori_loop(0, NZG, finish, 0)


def vmem(*shape, dtype=F32):
    return pltpu.VMEM(shape, dtype)


HBM = pl.BlockSpec(memory_space=pltpu.HBM)


def local(emission, absorption, target_z, target_x, owner_z, owner_x):
    depth_z, width_x, width_y = absorption.shape
    pixels = 2 * width_y
    count_x = lax.axis_size("gx")
    count_y = lax.axis_size("gy")
    count_z = lax.axis_size("gz")
    step_z = OPTICAL / (depth_z * count_z)
    step_x = OPTICAL / (width_x * count_x)
    interp = interp_table(width_y)
    rate = interp.T * (-step_z * math.log2(math.e))
    order = np.concatenate([np.arange(0, pixels, 2), np.roll(np.arange(1, pixels, 2), 1)])
    rate_hi = rate.astype(BF16)
    rate_lo = (rate - rate_hi.astype(np.float64)).astype(BF16)
    tab = np.concatenate([interp.T.astype(BF16), rate_hi, rate_lo], axis=0)[:, order]
    tab_back = np.concatenate([(interp.T * step_z).astype(BF16), rate_hi, rate_lo], axis=0)[:, order]
    perm = np.eye(pixels)[:, order].astype(BF16)
    slots = 2 * width_x // (count_y * count_z) + 2 * depth_z // (count_x * count_y)
    e5 = emission.reshape(3, depth_z, NSEG, SEG, width_y)
    s4 = absorption.reshape(depth_z, NSEG, SEG, width_y)

    def buffers(steps):
        return [
            vmem(steps + 1, 3, ZG, NSEG, HALF, LANE, dtype=BF16), vmem(steps + 1, ZG, NSEG, HALF, LANE, dtype=BF16),
            vmem(4, ZG, 2, NSEG * PITCH, LANE), vmem(4, ZG, 2, NSEG * PITCH, LANE),
        ]

    back_buffers = [
        vmem(3 * LANE, 256, dtype=BF16), vmem(4, ZG, NSEG * PITCH, LANE), vmem(4, ZG, NSEG * PITCH, LANE),
        vmem(NZG + 1, 3, ZG, NSEG, HALF, LANE, dtype=BF16), vmem(NZG + 1, ZG, NSEG, HALF, LANE, dtype=BF16),
        vmem(2, HALF, NSEG, 256), vmem(2, 2, NZ * NSEG, LANE),
    ]
    dma = pltpu.SemaphoreType.DMA
    coz, cox, xst, ge0, gs0, owned = pl.pallas_call(
        functools.partial(forward_kernel, step_z, step_x, 1.0 / (3.0 * pixels * slots)),
        out_shape=[
            jax.ShapeDtypeStruct((HALF, 4, NSEG, 256), F32),
            jax.ShapeDtypeStruct((7, 2, NZ * NSEG, LANE), F32),
            jax.ShapeDtypeStruct((2, 2, NZ * NSEG, LANE), F32),
            jax.ShapeDtypeStruct((3, NZ, NSEG, HALF, LANE), BF16),
            jax.ShapeDtypeStruct((NZ, NSEG, HALF, LANE), BF16),
            jax.ShapeDtypeStruct((1, 1), F32),
        ],
        in_specs=[HBM] * 9,
        out_specs=[HBM] * 5 + [pl.BlockSpec(memory_space=pltpu.SMEM)],
        scratch_shapes=buffers(STEPS) + [
            vmem(SEG, 4, NSEG, 256), vmem(4, 2, NZ * NSEG, LANE), vmem(2, HALF, 4, NSEG, 256), vmem(7, 2, NZ * NSEG, LANE),
        ] + back_buffers + [
            vmem(3, 256, 256, dtype=BF16), vmem(3, NZ, 256, dtype=BF16),
            vmem(3, 2, NSEG * (SEG + 4), LANE), vmem(3, NZ, 256),
            vmem(2, 8, 4, 8, 256), vmem(2, 8, 4, 8, 256), vmem(2, 4, 2, 4, 8, 256), vmem(2, 4, 2, 4, 8, 256),
            vmem(2, 8, 4, 8, 256), vmem(2, 8, 4, 8, 256), vmem(2, 8, 4, 8, 256),
            vmem(4, 4, 8, 256), vmem(4, 4, 8, 256), vmem(4, 4, 8, 256), vmem(4, 4, 8, 256), vmem(NSEG, 8, LANE),
            vmem(3 * LANE, 256, dtype=BF16), vmem(256, 256, dtype=BF16), vmem(5, 8, LANE),
            pltpu.SMEM((1, 256), jnp.int32), pltpu.SMEM((1, NZ), jnp.int32),
            vmem(8, 8, LANE), vmem(4, 8, LANE), vmem(4, 8, LANE),
            dma((STEPS, 2)), dma((7,)), dma((2, 2)), dma((2, 3, 2)), dma((2, 3, 2)), dma((2, 2)), dma((3, 2)), dma((3, 2)),
            dma((7, 2)), dma((3, 2)), dma((3, 2)), dma((3,)), dma((NZG, 2)), dma((NZG // 2,)),
        ],
        compiler_params=pltpu.CompilerParams(
            collective_id=0, has_side_effects=True, vmem_limit_bytes=VMEM_LIMIT
        ),
    )(
        e5, s4, target_z, target_x, owner_z.reshape(count_x, count_y, 1, width_x),
        owner_x.reshape(count_y, count_z, 1, depth_z), tab, perm, tab_back,
    )

    grad_e, grad_s = pl.pallas_call(
        backward_kernel,
        out_shape=[jax.ShapeDtypeStruct(e5.shape, BF16), jax.ShapeDtypeStruct(s4.shape, BF16)],
        in_specs=[HBM] * 8,
        out_specs=[HBM, HBM],
        scratch_shapes=buffers(NZG) + back_buffers + [
            vmem(HALF, 4, NSEG, 256), vmem(7, 2, NZ * NSEG, LANE),
            vmem(NZG, 3, ZG, NSEG, HALF, LANE, dtype=BF16), vmem(NZG, ZG, NSEG, HALF, LANE, dtype=BF16),
            dma((NZG, 2)), dma((NZG, 2)), dma(()), dma(()), dma((NZG, 2)), dma((NZG, 2)), dma((NZG, 2)),
        ],
        compiler_params=pltpu.CompilerParams(vmem_limit_bytes=VMEM_LIMIT),
        cost_estimate=pl.CostEstimate(flops=6 * 10**9, bytes_accessed=20 * 2**20, transcendentals=0),
    )(e5, s4, tab_back, coz, cox, xst, ge0, gs0)
    return (grad_e.reshape(emission.shape), grad_s.reshape(absorption.shape), owned.reshape(1, 1, 1))


def solution(mesh):
    return jax.shard_map(
        local,
        mesh=mesh,
        in_specs=(P(None, "gz", "gx", "gy"), P("gz", "gx", "gy"), P(), P(), P(), P()),
        out_specs=(P(None, "gz", "gx", "gy"), P("gz", "gx", "gy"), P("gx", "gy", "gz")),
        check_vma=False,
    )
```
